32 devices in a mesh: wide: 8 (over z, x), narrow: 4 (over y, core).
Axes of the slice: x: 2, y: 2, z: 4, core: 2. Of those that a mesh axis runs over, the one named last changes fastest.
Arguments:
- token_ids: int32 [8, 2, 1024], P('wide'), may hold values from 0 to 50686
- mask_slots: int32 [8, 2, 256], P('wide'), may hold values from 0 to 1023, as said below
- mask_counts: int32 [8, 2], P('wide'), may hold values from 64 to 256, as said below
- embedding: float32 [50688, 768], P('narrow', 'wide'), may hold values from -6 to 6
- out_table: float32 [768, 50688], P('wide', 'narrow')
- qkv_weight: float32 [3, 768, 768], P(None, 'wide', 'narrow'), may hold values from -0.21875 to 0.21875
- proj_weight: float32 [768, 768], P('narrow', 'wide'), may hold values from -1.75 to 1.75
- up_weight: float32 [768, 3072], P('wide', 'narrow'), may hold values from -0.21875 to 0.21875
- down_weight: float32 [3072, 768], P('narrow', 'wide'), may hold values from -0.109375 to 0.109375
- mod_weight: float32 [128, 6144], P(None, 'wide'), may hold values from -0.5 to 0.5
- vectors: float32 [9216], P('wide')
- embedding_first: float32 [50688, 768], P('narrow', 'wide'), may hold values from -3.5762787e-07 to 3.5762787e-07
- out_table_first: float32 [768, 50688], P('wide', 'narrow'), may hold values from -3.5762787e-07 to 3.5762787e-07
- qkv_first: float32 [3, 768, 768], P(None, 'wide', 'narrow'), may hold values from -3.5762787e-07 to 3.5762787e-07
- proj_first: float32 [768, 768], P('narrow', 'wide'), may hold values from -3.5762787e-07 to 3.5762787e-07
- up_first: float32 [768, 3072], P('wide', 'narrow'), may hold values from -3.5762787e-07 to 3.5762787e-07
- down_first: float32 [3072, 768], P('narrow', 'wide'), may hold values from -3.5762787e-07 to 3.5762787e-07
- mod_first: float32 [128, 6144], P(None, 'wide'), may hold values from -3.5762787e-07 to 3.5762787e-07
- vectors_first: float32 [9216], P('wide'), may hold values from -3.8146973e-06 to 3.8146973e-06
- embedding_second: float32 [50688, 768], P('narrow', 'wide'), may hold values from 1.53388e-14 to 6.13552e-14
- out_table_second: float32 [768, 50688], P('wide', 'narrow'), may hold values from 1.53388e-14 to 6.13552e-14
- qkv_second: float32 [3, 768, 768], P(None, 'wide', 'narrow'), may hold values from 1.53388e-14 to 6.13552e-14
- proj_second: float32 [768, 768], P('narrow', 'wide'), may hold values from 1.53388e-14 to 6.13552e-14
- up_second: float32 [768, 3072], P('wide', 'narrow'), may hold values from 1.53388e-14 to 6.13552e-14
- down_second: float32 [3072, 768], P('narrow', 'wide'), may hold values from 1.53388e-14 to 6.13552e-14
- mod_second: float32 [128, 6144], P(None, 'wide'), may hold values from 1.53388e-14 to 6.13552e-14
- vectors_second: float32 [9216], P('wide'), may hold values from 1.53388e-12 to 6.13552e-12
Outputs:
- loss_sum: float32 [], replicated
- grad_norm: float32 [], replicated
- embedding_next: float32 [50688, 768], P('narrow', 'wide')
- embedding_first_next: float32 [50688, 768], P('narrow', 'wide')
- embedding_second_next: float32 [50688, 768], P('narrow', 'wide')
- out_table_next: float32 [768, 50688], P('wide', 'narrow')
- out_table_first_next: float32 [768, 50688], P('wide', 'narrow')
- out_table_second_next: float32 [768, 50688], P('wide', 'narrow')
- qkv_next: float32 [3, 768, 768], P(None, 'wide', 'narrow')
- qkv_first_next: float32 [3, 768, 768], P(None, 'wide', 'narrow')
- qkv_second_next: float32 [3, 768, 768], P(None, 'wide', 'narrow')
- proj_next: float32 [768, 768], P('narrow', 'wide')
- proj_first_next: float32 [768, 768], P('narrow', 'wide')
- proj_second_next: float32 [768, 768], P('narrow', 'wide')
- up_next: float32 [768, 3072], P('wide', 'narrow')
- up_first_next: float32 [768, 3072], P('wide', 'narrow')
- up_second_next: float32 [768, 3072], P('wide', 'narrow')
- down_next: float32 [3072, 768], P('narrow', 'wide')
- down_first_next: float32 [3072, 768], P('narrow', 'wide')
- down_second_next: float32 [3072, 768], P('narrow', 'wide')
- mod_next: float32 [128, 6144], P(None, 'wide')
- mod_first_next: float32 [128, 6144], P(None, 'wide')
- mod_second_next: float32 [128, 6144], P(None, 'wide')
- vectors_next: float32 [9216], P('wide')
- vectors_first_next: float32 [9216], P('wide')
- vectors_second_next: float32 [9216], P('wide')
The draws below stay inside these ranges and needn't reach their ends.
Inputs may be any that keep to these rules, and one draw needn't show every extreme that they name: `mask_counts`: in each micro-batch, the counts of rows w and w + 4 sum to 320; row 4 holds 256 in every micro-batch. `mask_slots`: the 256 positions of one sequence are distinct.
All inputs are finite; a program needn't handle non-finite values.
Results may differ from the reference program's by a relative error of at most 0.012.
The reference program's roundings to bfloat16 on the way count: a program that leaves them out, or rounds other values in their place, can miss the bound.
Values may be sent and summed in bfloat16 or wider, within the bound.
No kernel may reach another device: no remote copies, remote signals or barrier semaphores. Data moves between devices by JAX's collectives and lax.ppermute only.
A program may use at most 448 MiB of HBM per device.

```python
import math
import jax
import jax.numpy as jnp
from jax import lax

D = 768
H = 12
HD = 64
FF = 3072
COND = 128
VOCAB = 50688
ROWS = 1024
MICRO = 2
STEP = 10
CAP = 256
MASK_PAIR = 320
TOKENS = 16384
PARAMS = 85730304
N_WIDE = 8


def draw_mask_counts(key, part):
    half_rows = N_WIDE // 2
    lowest = MASK_PAIR - CAP
    middle = MASK_PAIR // 2
    ranks = jnp.arange(half_rows, dtype=jnp.int32)[:, None]
    jitter = jax.random.randint(key, (half_rows, MICRO), 0, 3)
    lower = jnp.minimum(middle, lowest + (middle - lowest) * ranks // half_rows + jitter)
    lower = jnp.where(ranks == 0, lowest, lower)
    return jnp.concatenate([lower, MASK_PAIR - lower], axis=0).astype(jnp.int32)


def draw_mask_slots(key, part):
    keys = jax.random.split(key, N_WIDE * MICRO)
    orders = jax.vmap(lambda single: jax.random.permutation(single, ROWS))(keys)
    return orders.reshape(N_WIDE, MICRO, ROWS)[:, :, :CAP].astype(jnp.int32)


def draw_out_table(key, part):
    column = jnp.arange(VOCAB, dtype=jnp.float32) / VOCAB
    base = jax.random.normal(key, (D, VOCAB), jnp.float32)
    spread = 1.0 + 2.0 * column
    return base * spread[None, :] * D ** (-0.5)


def draw_vectors(key, part):
    column = jnp.arange(D, dtype=jnp.float32) / D
    first_key, second_key = jax.random.split(key, 2)
    noise = jax.random.normal(second_key, (9, D), jnp.float32)
    wobble = jax.random.uniform(first_key, (3, D), jnp.float32, 0.8, 1.2)
    gains = (0.5 + column)[None, :] * wobble
    blocks = jnp.arange(9)[:, None]
    gated = (blocks == 3) | (blocks == 6)
    others = jnp.where(gated, 1.0 + 0.2 * noise, 0.1 * noise)
    return jnp.concatenate([gains.reshape(-1), others.reshape(-1)]).astype(jnp.float32)


def plant(entries, stream_key, low, largest):
    dims = entries.shape
    place = [jax.random.randint(jax.random.fold_in(stream_key, axis), (), 0, dims[axis]) for axis in range(len(dims))]
    entries = entries.at[tuple(place)].set(low)
    longest = dims.index(max(dims))
    place[longest] = (place[longest] + 1) % dims[longest]
    return entries.at[tuple(place)].set(largest)


def block_scale(own_key, extent, shards, smallest, high):
    loudness = 1.0
    for position, shards_of in shards:
        heights = jax.random.uniform(jax.random.fold_in(jax.random.fold_in(own_key, 6), position), (shards_of,), jnp.float32, smallest / len(shards), high / len(shards))
        loudness = loudness * jnp.repeat(jnp.exp(heights), extent[position] // shards_of).reshape((-1,) + (1,) * (len(extent) - 1 - position))
    return loudness


def centred(rng, dims, scale, limit, cuts=(), kind=jnp.bfloat16):
    drawn = jax.random.normal(rng, dims, jnp.float32) * scale
    if len(cuts) > 0:
        drawn = block_scale(rng, dims, cuts, -0.22, 0.18) * drawn
    return jnp.clip(drawn, min=-limit, max=limit).astype(kind)


def setup_inputs(seed: int = 0) -> dict:
    arg_keys = jax.random.split(jax.random.key(seed), 28)
    return {
        "token_ids": plant(jax.random.randint(arg_keys[0], (N_WIDE, MICRO, ROWS), 0, VOCAB - 1), jax.random.fold_in(arg_keys[0], 1), 0, (VOCAB - 1) - 1).astype(jnp.int32),
        "mask_slots": draw_mask_slots(jax.random.fold_in(arg_keys[27], 71), 0),
        "mask_counts": draw_mask_counts(jax.random.fold_in(arg_keys[27], 71), 0),
        "embedding": centred(arg_keys[3], (VOCAB, D), 1.0, 6.0, ((0, 4), (1, 8)), jnp.float32),
        "out_table": draw_out_table(jax.random.fold_in(arg_keys[27], 71), 0),
        "qkv_weight": centred(arg_keys[5], (3, D, H * HD), D ** -0.5, 0.21875, ((1, 8), (2, 4)), jnp.float32),
        "proj_weight": centred(arg_keys[6], (H * HD, D), (H * HD * 16 // ROWS) ** -0.5, 1.75, ((0, 4), (1, 8)), jnp.float32),
        "up_weight": centred(arg_keys[7], (D, FF), D ** -0.5, 0.21875, ((0, 8), (1, 4)), jnp.float32),
        "down_weight": centred(arg_keys[8], (FF, D), FF ** -0.5, 0.109375, ((0, 4), (1, 8)), jnp.float32),
        "mod_weight": centred(arg_keys[9], (COND, 8 * D), COND ** -0.5, 0.5, ((1, 8),), jnp.float32),
        "vectors": draw_vectors(jax.random.fold_in(arg_keys[27], 71), 0),
        "embedding_first": centred(arg_keys[11], (VOCAB, D), (0.000555 * PARAMS ** -0.5), 3.5762786865234375e-07, ((0, 4), (1, 8)), jnp.float32),
        "out_table_first": centred(arg_keys[12], (D, VOCAB), (0.000555 * PARAMS ** -0.5), 3.5762786865234375e-07, ((0, 8), (1, 4)), jnp.float32),
        "qkv_first": centred(arg_keys[13], (3, D, H * HD), (0.000555 * PARAMS ** -0.5), 3.5762786865234375e-07, ((1, 8), (2, 4)), jnp.float32),
        "proj_first": centred(arg_keys[14], (H * HD, D), (0.000555 * PARAMS ** -0.5), 3.5762786865234375e-07, ((0, 4), (1, 8)), jnp.float32),
        "up_first": centred(arg_keys[15], (D, FF), (0.000555 * PARAMS ** -0.5), 3.5762786865234375e-07, ((0, 8), (1, 4)), jnp.float32),
        "down_first": centred(arg_keys[16], (FF, D), (0.000555 * PARAMS ** -0.5), 3.5762786865234375e-07, ((0, 4), (1, 8)), jnp.float32),
        "mod_first": centred(arg_keys[17], (COND, 8 * D), (0.000555 * PARAMS ** -0.5), 3.5762786865234375e-07, ((1, 8),), jnp.float32),
        "vectors_first": centred(arg_keys[18], (12 * D,), (0.00555 * PARAMS ** -0.5), 3.814697265625e-06, ((0, 8),), jnp.float32),
        "embedding_second": jnp.clip(jnp.exp(math.log(6.135519745259846e-14) - 1.3862944 * jax.random.uniform(arg_keys[19], (VOCAB, D), jnp.float32) ** block_scale(arg_keys[19], (VOCAB, D), ((0, 4), (1, 8)), -0.2, 0.2)), 1.5338799363149615e-14, 6.135519745259846e-14),
        "out_table_second": jnp.clip(jnp.exp(math.log(6.135519745259846e-14) - 1.3862944 * jax.random.uniform(arg_keys[20], (D, VOCAB), jnp.float32) ** block_scale(arg_keys[20], (D, VOCAB), ((0, 8), (1, 4)), -0.2, 0.2)), 1.5338799363149615e-14, 6.135519745259846e-14),
        "qkv_second": jnp.clip(jnp.exp(math.log(6.135519745259846e-14) - 1.3862944 * jax.random.uniform(arg_keys[21], (3, D, H * HD), jnp.float32) ** block_scale(arg_keys[21], (3, D, H * HD), ((1, 8), (2, 4)), -0.2, 0.2)), 1.5338799363149615e-14, 6.135519745259846e-14),
        "proj_second": jnp.clip(jnp.exp(math.log(6.135519745259846e-14) - 1.3862944 * jax.random.uniform(arg_keys[22], (H * HD, D), jnp.float32) ** block_scale(arg_keys[22], (H * HD, D), ((0, 4), (1, 8)), -0.2, 0.2)), 1.5338799363149615e-14, 6.135519745259846e-14),
        "up_second": jnp.clip(jnp.exp(math.log(6.135519745259846e-14) - 1.3862944 * jax.random.uniform(arg_keys[23], (D, FF), jnp.float32) ** block_scale(arg_keys[23], (D, FF), ((0, 8), (1, 4)), -0.2, 0.2)), 1.5338799363149615e-14, 6.135519745259846e-14),
        "down_second": jnp.clip(jnp.exp(math.log(6.135519745259846e-14) - 1.3862944 * jax.random.uniform(arg_keys[24], (FF, D), jnp.float32) ** block_scale(arg_keys[24], (FF, D), ((0, 4), (1, 8)), -0.2, 0.2)), 1.5338799363149615e-14, 6.135519745259846e-14),
        "mod_second": jnp.clip(jnp.exp(math.log(6.135519745259846e-14) - 1.3862944 * jax.random.uniform(arg_keys[25], (COND, 8 * D), jnp.float32) ** block_scale(arg_keys[25], (COND, 8 * D), ((1, 8),), -0.2, 0.2)), 1.5338799363149615e-14, 6.135519745259846e-14),
        "vectors_second": jnp.clip(jnp.exp(math.log(6.135520043415443e-12) - 1.3862944 * jax.random.uniform(arg_keys[26], (12 * D,), jnp.float32) ** block_scale(arg_keys[26], (12 * D,), ((0, 8),), -0.2, 0.2)), 1.5338800108538608e-12, 6.135520043415443e-12),
    }


@jax.custom_vjp
def low(v):
    return lax.optimization_barrier(v.astype(jnp.bfloat16)).astype(jnp.float32)

@jax.custom_vjp
def low_back(v):
    return v

def low_keep(v):
    return (low(v), None)

def low_pass(kept, grad):
    return (grad,)

def back_keep(v):
    return (v, None)

def back_low(kept, grad):
    return (low(grad),)
low.defvjp(low_keep, low_pass)
low_back.defvjp(back_keep, back_low)
HIGHEST = lax.Precision.HIGHEST
NORM_EPS = 1e-06
CLIP_NORM = 0.005
BETA_ONE = 0.9
BETA_TWO = 0.95
ADAM_EPS = 1e-08
WEIGHT_DECAY = 0.1
LEARN_RATES = (1.0, 0.1, 0.07, 0.5, 0.07, 0.04, 0.2, 0.5)

def layer_norm(values):
    centered = values - lax.optimization_barrier(jnp.mean(values, axis=-1, keepdims=True))
    inverse = lax.rsqrt(lax.optimization_barrier(jnp.mean(centered * centered, axis=-1, keepdims=True)) + NORM_EPS)
    return centered * inverse

def gelu_tanh(values):
    inner = 0.7978845608 * (values + 0.044715 * values * values * values)
    return 0.5 * values * (1.0 + jnp.tanh(inner))

def rotary_tables(length, width):
    freqs = jnp.exp(jnp.arange(width // 2, dtype=jnp.float32) * (-2.0 * math.log(10000.0) / width))
    angle = jnp.arange(length, dtype=jnp.float32)[:, None] * freqs[None, :]
    return (jnp.cos(angle), jnp.sin(angle))

def rotate(values, cosine, sine):
    middle = values.shape[-1] // 2
    first = values[..., :middle]
    second = values[..., middle:]
    return jnp.concatenate([first * cosine - second * sine, second * cosine + first * sine], axis=-1)

def time_features(moment, width):
    freqs = jnp.exp(jnp.arange(width // 2, dtype=jnp.float32) * (-math.log(10000.0) / (width // 2)))
    angle = 1000.0 * moment * freqs
    return jnp.concatenate([jnp.cos(angle), jnp.sin(angle)])

def sequence_loss(params, token_row, slot_row, mask_count):
    embedding, out_table, qkv_weight, proj_weight, up_weight, down_weight, mod_weight, vectors = params
    length = token_row.shape[0]
    width = embedding.shape[1]
    capacity = slot_row.shape[0]
    vocab = embedding.shape[0]
    valid = jnp.arange(capacity) < mask_count
    masked = jnp.zeros((length,), jnp.int32).at[slot_row].set(valid.astype(jnp.int32))
    inputs = jnp.where(masked > 0, vocab - 1, token_row)
    moment = mask_count.astype(jnp.float32) / MASK_PAIR
    condition = jax.nn.silu(time_features(moment, mod_weight.shape[0]))
    modulation = jnp.dot(condition, mod_weight, precision=HIGHEST) + vectors[4 * width:]
    shift_one, scale_one, gate_one, shift_two, scale_two, gate_two, shift_last, scale_last = jnp.split(modulation, 8)
    gain_one, gain_two, gain_last, bias_down = jnp.split(vectors[:4 * width], 4)
    start = embedding[inputs]
    hidden = low(layer_norm(start) * gain_one * (1.0 + scale_one) + shift_one)
    projected = low_back(jnp.einsum('rd,kde->kre', hidden, qkv_weight, precision=HIGHEST))
    heads = projected.reshape(3, length, H, HD).transpose(0, 2, 1, 3)
    cosine, sine = rotary_tables(length, HD)
    query = low(rotate(heads[0], cosine, sine))
    keys = low(rotate(heads[1], cosine, sine))
    values = low(heads[2])
    scores = low_back(jnp.einsum('hqe,hke->hqk', query, keys, precision=HIGHEST) * HD ** (-0.5))
    shifted = jnp.exp(scores - lax.optimization_barrier(jnp.max(scores, axis=-1, keepdims=True)))
    weights = low(shifted / lax.optimization_barrier(jnp.sum(shifted, axis=-1, keepdims=True)))
    mixed = jnp.einsum('hqk,hke->hqe', weights, values, precision=HIGHEST)
    mixed = low(low_back(mixed)).transpose(1, 0, 2).reshape(length, H * HD)
    attended = low_back(jnp.dot(mixed, proj_weight, precision=HIGHEST))
    middle = start + gate_one * attended
    hidden = low(layer_norm(middle) * gain_two * (1.0 + scale_two) + shift_two)
    inner = low_back(jnp.dot(hidden, up_weight, precision=HIGHEST))
    active = low(gelu_tanh(inner))
    output = low_back(jnp.dot(active, down_weight, precision=HIGHEST))
    final = middle + gate_two * (output + bias_down)
    hidden = low(layer_norm(final) * gain_last * (1.0 + scale_last) + shift_last)
    logits = low_back(jnp.dot(hidden[slot_row], out_table, precision=HIGHEST))
    top = lax.optimization_barrier(jnp.max(logits, axis=-1, keepdims=True))
    log_total = top[:, 0] + jnp.log(lax.optimization_barrier(jnp.sum(jnp.exp(logits - top), axis=-1)))
    target = jnp.take_along_axis(logits, token_row[slot_row][:, None], axis=-1)[:, 0]
    return jnp.sum(jnp.where(valid, log_total - target, 0.0))

def reference(token_ids, mask_slots, mask_counts, embedding, out_table, qkv_weight, proj_weight, up_weight, down_weight, mod_weight, vectors, embedding_first, out_table_first, qkv_first, proj_first, up_first, down_first, mod_first, vectors_first, embedding_second, out_table_second, qkv_second, proj_second, up_second, down_second, mod_second, vectors_second):
    masters = (embedding, out_table, qkv_weight, proj_weight, up_weight, down_weight, mod_weight, vectors)
    firsts = (embedding_first, out_table_first, qkv_first, proj_first, up_first, down_first, mod_first, vectors_first)
    seconds = (embedding_second, out_table_second, qkv_second, proj_second, up_second, down_second, mod_second, vectors_second)
    lowered = tuple((weight.astype(jnp.bfloat16).astype(jnp.float32) for weight in masters))
    token_rows = token_ids.reshape(-1, ROWS)
    slot_rows = mask_slots.reshape(-1, CAP)
    count_rows = mask_counts.reshape(-1)

    def objective(params):

        def advance(total, item):
            return (total + jax.checkpoint(sequence_loss)(params, item[0], item[1], item[2]), None)
        total, _ = lax.scan(advance, jnp.zeros((), jnp.float32), (token_rows, slot_rows, count_rows))
        return total
    loss_sum, pullback = jax.vjp(objective, lowered)
    grads = pullback(jnp.ones((), jnp.float32) / TOKENS)[0]
    square = jnp.zeros((), jnp.float32)
    for grad in grads:
        square = square + jnp.sum(grad * grad)
    norm = jnp.sqrt(square)
    factor = CLIP_NORM / jnp.maximum(norm, CLIP_NORM)
    results = []
    for member in range(8):
        grad = grads[member] * factor
        first = BETA_ONE * firsts[member] + (1.0 - BETA_ONE) * grad
        second = BETA_TWO * seconds[member] + (1.0 - BETA_TWO) * grad * grad
        stepped = first / (1.0 - BETA_ONE ** STEP) / (jnp.sqrt(second / (1.0 - BETA_TWO ** STEP)) + ADAM_EPS)
        decay = WEIGHT_DECAY if member < 7 else 0.0
        fresh = masters[member] - LEARN_RATES[member] * (stepped + decay * masters[member])
        results.extend([fresh, first, second])
    return (loss_sum, norm, results[0], results[1], results[2], results[3], results[4], results[5], results[6], results[7], results[8], results[9], results[10], results[11], results[12], results[13], results[14], results[15], results[16], results[17], results[18], results[19], results[20], results[21], results[22], results[23])
```

```python
import functools
import math

import jax
import jax.numpy as jnp
from jax import lax
from jax.experimental import pallas as pl
from jax.experimental.pallas import tpu as pltpu
from jax.sharding import PartitionSpec as P

HD = 64
STEP = 10

HIGHEST = lax.Precision.HIGHEST
NORM_EPS = 1e-06
CLIP_NORM = 0.005
BETA_ONE = 0.9
BETA_TWO = 0.95
ADAM_EPS = 1e-08
WEIGHT_DECAY = 0.1
LEARN_RATES = (1.0, 0.1, 0.07, 0.5, 0.07, 0.04, 0.2, 0.5)
BF = jnp.bfloat16
F32 = jnp.float32
VMEM_LIMIT = 56 * 1024 * 1024


def xor_narrow(value, bits):
    return lax.ppermute(value, "narrow", [(i, i ^ bits) for i in range(lax.axis_size("narrow"))])


def xor_wide(value, bits):
    return lax.ppermute(value, "wide", [(i, i ^ bits) for i in range(lax.axis_size("wide"))])


def swap_wide(value):
    return lax.all_to_all(value, "wide", 0, 0, tiled=True)


def spread_wide(value):
    if lax.axis_size("wide") > 8:
        return lax.all_gather(value, "wide")
    return swap_wide(jnp.broadcast_to(value[None], (lax.axis_size("wide"),) + value.shape))


def swap_wide_async(value):
    count = lax.axis_size("wide")
    if count > 8:
        return swap_wide(value)
    me = lax.axis_index("wide")
    out = value
    pieces = [
        xor_wide(lax.dynamic_index_in_dim(value, me ^ k, 0, keepdims=False), k)
        for k in range(1, count)
    ]
    for k in range(1, count):
        out = lax.dynamic_update_index_in_dim(out, pieces[k - 1], me ^ k, 0)
    return out


def gather_wide(value):
    count = lax.axis_size("wide")
    if count != 8:
        return lax.all_gather(value, "wide", axis=0, tiled=True)
    me = lax.axis_index("wide")
    near = jnp.stack([value] + [xor_wide(value, k) for k in (2, 4, 6)])
    far = xor_wide(near, 1)
    out = jnp.zeros((count,) + value.shape, value.dtype)
    for k in range(4):
        out = lax.dynamic_update_index_in_dim(out, near[k], me ^ (2 * k), 0)
        out = lax.dynamic_update_index_in_dim(out, far[k], me ^ (2 * k + 1), 0)
    return out.reshape((count * value.shape[0],) + value.shape[1:])


def scatter_wide(value):
    count = lax.axis_size("wide")
    if count != 8:
        return lax.psum_scatter(value, "wide", scatter_dimension=0)
    me = lax.axis_index("wide")
    side = me & 1
    pairs = value.reshape((4, 2) + value.shape[1:])
    kept = lax.dynamic_index_in_dim(pairs, side, 1, keepdims=False)
    sent = lax.dynamic_index_in_dim(pairs, 1 - side, 1, keepdims=False).astype(BF)
    half = kept.astype(F32) + xor_wide(sent, 1).astype(F32)
    depth = me >> 1
    total = lax.dynamic_index_in_dim(half, depth, 0, keepdims=False)
    low = half.astype(BF)
    for k in (1, 2, 3):
        piece = lax.dynamic_index_in_dim(low, depth ^ k, 0, keepdims=False)
        total = total + xor_wide(piece, 2 * k).astype(F32)
    return total


def scatter_narrow(parts):
    from_core = xor_narrow(jnp.stack([parts[1], parts[3]]).astype(BF), 1)
    near = parts[0] + from_core[0].astype(F32)
    far = parts[2] + from_core[1].astype(F32)
    return near + xor_narrow(far.astype(BF), 2).astype(F32)


def gather_narrow(value):
    across = xor_narrow(value, 2)
    beside = xor_narrow(value, 1)
    corner = xor_narrow(across, 1)
    return value, beside, across, corner


def rounded(value):
    return lax.reduce_precision(value, exponent_bits=8, mantissa_bits=7)


def layer_norm(values):
    centered = values - jnp.mean(values, axis=-1, keepdims=True)
    inverse = lax.rsqrt(jnp.mean(centered * centered, axis=-1, keepdims=True) + NORM_EPS)
    return (centered * inverse, inverse)


def norm_back(grad, normed, inverse):
    return inverse * (
        grad
        - jnp.mean(grad, axis=-1, keepdims=True)
        - normed * jnp.mean(grad * normed, axis=-1, keepdims=True)
    )


def gelu_tanh(values):
    inner = 0.7978845608 * (values + 0.044715 * values * values * values)
    return 0.5 * values * (1.0 + jnp.tanh(inner))


def gelu_slope(values):
    tangent = jnp.tanh(0.7978845608 * (values + 0.044715 * values * values * values))
    return 0.5 * (1.0 + tangent) + 0.5 * values * (1.0 - tangent * tangent) * 0.7978845608 * (
        1.0 + 0.134145 * values * values
    )


def rotary_tables(positions, width):
    freqs = jnp.exp(jnp.arange(width // 2, dtype=F32) * (-2.0 * math.log(10000.0) / width))
    angle = positions.astype(F32)[:, None] * freqs[None, :]
    cosine, sine = jnp.cos(angle), jnp.sin(angle)
    return (
        jnp.concatenate([cosine] * 4, axis=1),
        jnp.concatenate([-sine, sine, -sine, sine], axis=1),
    )


def time_features(moment, width):
    freqs = jnp.exp(jnp.arange(width // 2, dtype=F32) * (-math.log(10000.0) / (width // 2)))
    angle = 1000.0 * moment[..., None] * freqs
    return jnp.concatenate([jnp.cos(angle), jnp.sin(angle)], axis=-1)


def turned(values, cosine, sine):
    lanes = lax.broadcasted_iota(jnp.int32, values.shape, 1)
    ahead = pltpu.roll(values, values.shape[1] - HD // 2, 1)
    behind = pltpu.roll(values, HD // 2, 1)
    other = jnp.where((lanes & (HD - 1)) < HD // 2, ahead, behind)
    return values * cosine + other * sine


def qkv_kernel(hidden_ref, weight_ref, cos_ref, sin_ref, out_ref):
    step = pl.program_id(0)
    block = weight_ref.shape[1]
    value = jnp.dot(hidden_ref[...], weight_ref[...], preferred_element_type=F32)

    @pl.when(step * block < 2 * hidden_ref.shape[1])
    def _():
        for part in range(block // (2 * HD)):
            lanes = slice(part * 2 * HD, (part + 1) * 2 * HD)
            out_ref[:, lanes] = turned(value[:, lanes], cos_ref[...], sin_ref[...]).astype(BF)

    @pl.when(step * block >= 2 * hidden_ref.shape[1])
    def _():
        out_ref[...] = value.astype(BF)


def project_qkv(hidden, weight, cosine, sine):
    rows, width = hidden.shape
    block = 256
    return pl.pallas_call(
        qkv_kernel,
        grid=(weight.shape[1] // block,),
        in_specs=[
            pl.BlockSpec((rows, width), lambda i: (0, 0)),
            pl.BlockSpec((width, block), lambda i: (0, i)),
            pl.BlockSpec(cosine.shape, lambda i: (0, 0)),
            pl.BlockSpec(sine.shape, lambda i: (0, 0)),
        ],
        out_specs=pl.BlockSpec((rows, block), lambda i: (0, i)),
        out_shape=jax.ShapeDtypeStruct((rows, weight.shape[1]), BF),
        compiler_params=pltpu.CompilerParams(vmem_limit_bytes=VMEM_LIMIT),
        cost_estimate=pl.CostEstimate(
            flops=2 * rows * width * weight.shape[1], bytes_accessed=8_000_000, transcendentals=0
        ),
        name="qkv",
    )(hidden, weight, cosine, sine)


NT = (((1,), (1,)), ((), ()))
NN = (((1,), (0,)), ((), ()))
TN = (((0,), (0,)), ((), ()))


def mm(a, b, dims):
    return lax.dot_general(a, b, dims, preferred_element_type=F32)


def head_mask(values, head):
    lanes = lax.broadcasted_iota(jnp.int32, values.shape, 1)
    return jnp.where((lanes >= HD) == (head == 1), values, jnp.zeros_like(values))


def attend_kernel(q_ref, k_ref, v_ref, out_ref, log_ref):
    keys, values, query = k_ref[...], v_ref[...], q_ref[...] * BF(HD**-0.5)
    halves = []
    for head in range(2):
        scores = mm(keys, head_mask(query, head), NT)
        top = jnp.max(scores, axis=0, keepdims=True)
        shifted = jnp.exp(scores - top)
        total = jnp.sum(shifted, axis=0, keepdims=True)
        weights = (shifted * (1.0 / total)).astype(BF)
        halves.append(mm(values, weights, TN)[head * HD : (head + 1) * HD])
        log_ref[0, head : head + 1, :] = top + jnp.log(total)
    out_ref[...] = jnp.concatenate(halves, axis=0).T.astype(BF)


def attend(query, keys, values):
    rows, width = query.shape
    length = keys.shape[0]
    pairs = width // (2 * HD)
    lane = pl.BlockSpec((rows, 2 * HD), lambda i: (0, i))
    wide = pl.BlockSpec((length, 2 * HD), lambda i: (0, i))
    return pl.pallas_call(
        attend_kernel,
        grid=(pairs,),
        in_specs=[lane, wide, wide],
        out_specs=[lane, pl.BlockSpec((1, 2, rows), lambda i: (i, 0, 0))],
        out_shape=[
            jax.ShapeDtypeStruct((rows, width), BF),
            jax.ShapeDtypeStruct((pairs, 2, rows), F32),
        ],
        compiler_params=pltpu.CompilerParams(vmem_limit_bytes=VMEM_LIMIT),
        cost_estimate=pl.CostEstimate(
            flops=4 * rows * length * width * 4,
            bytes_accessed=5_000_000,
            transcendentals=rows * length * width // HD,
        ),
        name="attend",
    )(query, keys, values)


def attend_back_kernel(
    q_ref, k_ref, v_ref, do_ref, log_ref, cos_ref, sin_ref, kcos_ref, ksin_ref,
    dq_ref, dk_ref, dv_ref, dk_far_ref, dv_far_ref,
):
    keys, values, query, grad = k_ref[...], v_ref[...], q_ref[...], do_ref[...]
    scale = HD**-0.5
    rows = query.shape[0]
    dq = jnp.zeros((2 * HD, rows), F32)
    dk = jnp.zeros(keys.shape, F32)
    dv = jnp.zeros(keys.shape, F32)
    for head in range(2):
        query_one = head_mask(query * BF(scale), head)
        grad_one = head_mask(grad, head)
        scores = mm(keys, query_one, NT)
        weights = jnp.exp(scores - log_ref[0, head : head + 1, :])
        d_weights = mm(values, grad_one, NT)
        delta = jnp.sum(weights * d_weights, axis=0, keepdims=True)
        d_scores = (weights * (d_weights - delta)).astype(BF)
        dq = dq + mm(head_mask(keys, head), d_scores, TN)
        dk = dk + mm(d_scores, query_one, NN)
        dv = dv + mm(weights.astype(BF), grad_one, NN)
    dq_ref[...] = turned(dq.T * scale, cos_ref[...], -sin_ref[...]).astype(BF)
    dk = turned(dk, kcos_ref[...], -ksin_ref[...])
    dk_ref[...] = dk[:rows]
    dv_ref[...] = dv[:rows]
    dk_far_ref[...] = dk[rows:].astype(BF)
    dv_far_ref[...] = dv[rows:].astype(BF)


def attend_back(query, keys, values, grad, logs, cosine, sine, key_cosine, key_sine):
    rows, width = query.shape
    length = keys.shape[0]
    pairs = width // (2 * HD)
    lane = pl.BlockSpec((rows, 2 * HD), lambda i: (0, i))
    wide = pl.BlockSpec((length, 2 * HD), lambda i: (0, i))
    whole = lambda table: pl.BlockSpec(table.shape, lambda i: (0, 0))
    return pl.pallas_call(
        attend_back_kernel,
        grid=(pairs,),
        in_specs=[
            lane, wide, wide, lane, pl.BlockSpec((1, 2, rows), lambda i: (i, 0, 0)),
            whole(cosine), whole(sine), whole(key_cosine), whole(key_sine),
        ],
        out_specs=[lane] * 5,
        out_shape=[
            jax.ShapeDtypeStruct((rows, width), BF),
            jax.ShapeDtypeStruct((rows, width), F32),
            jax.ShapeDtypeStruct((rows, width), F32),
            jax.ShapeDtypeStruct((length - rows, width), BF),
            jax.ShapeDtypeStruct((length - rows, width), BF),
        ],
        compiler_params=pltpu.CompilerParams(vmem_limit_bytes=VMEM_LIMIT),
        cost_estimate=pl.CostEstimate(
            flops=10 * rows * length * width * 4,
            bytes_accessed=10_000_000,
            transcendentals=rows * length * width // HD,
        ),
        name="attend_back",
    )(query, keys, values, grad, logs, cosine, sine, key_cosine, key_sine)


def lookup_kernel(id_ref, table_ref, out_ref, scratch):
    block = scratch.shape[0]
    unroll = 16

    def body(step, _):
        for k in range(unroll):
            place = step * unroll + k
            scratch[pl.ds(place, 1), :] = table_ref[pl.ds(id_ref[0, 0, place], 1), :]
        return 0

    lax.fori_loop(0, block // unroll, body, 0)
    out_ref[...] = scratch[...].astype(BF)


def lookup(table, ids):
    count = ids.shape[0]
    block = min(2048, count)
    width = table.shape[1]
    return pl.pallas_call(
        lookup_kernel,
        grid=(count // block,),
        in_specs=[
            pl.BlockSpec((1, 1, block), lambda i: (i, 0, 0), memory_space=pltpu.SMEM),
            pl.BlockSpec(table.shape, lambda i: (0, 0), pipeline_mode=pl.Buffered(1)),
        ],
        out_specs=pl.BlockSpec((block, width), lambda i: (i, 0)),
        out_shape=jax.ShapeDtypeStruct((count, width), BF),
        scratch_shapes=[pltpu.VMEM((block, width), F32)],
        compiler_params=pltpu.CompilerParams(vmem_limit_bytes=VMEM_LIMIT),
        cost_estimate=pl.CostEstimate(flops=0, bytes_accessed=60_000_000, transcendentals=0),
        name="lookup",
    )(ids.reshape(count // block, 1, block), table)


def collect_kernel(shift, key_ref, count_ref, grad_ref, out_ref, rows_ref):
    step = pl.program_id(0)

    @pl.when(step == 0)
    def _():
        out_ref[...] = jnp.zeros_like(out_ref)

    rows_ref[...] = grad_ref[0].astype(F32)
    mask = (1 << shift) - 1

    def body(item, _):
        key = key_ref[0, 0, item]
        target = pl.ds(lax.shift_right_logical(key, shift), 1)
        out_ref[target, :] = out_ref[target, :] + rows_ref[pl.ds(key & mask, 1), :]
        return 0

    lax.fori_loop(0, count_ref[0, 0, 0], body, 0)


def collect(keys, counts, grads, shift, entries):
    parts, tokens, width = grads.shape
    return pl.pallas_call(
        functools.partial(collect_kernel, shift),
        grid=(parts,),
        in_specs=[
            pl.BlockSpec((1, 1, tokens), lambda i: (i, 0, 0), memory_space=pltpu.SMEM),
            pl.BlockSpec((1, 1, 1), lambda i: (i, 0, 0), memory_space=pltpu.SMEM),
            pl.BlockSpec((1, tokens, width), lambda i: (i, 0, 0)),
        ],
        out_specs=pl.BlockSpec((entries, width), lambda i: (0, 0)),
        out_shape=jax.ShapeDtypeStruct((entries, width), F32),
        scratch_shapes=[pltpu.VMEM((tokens, width), F32)],
        compiler_params=pltpu.CompilerParams(vmem_limit_bytes=VMEM_LIMIT),
        cost_estimate=pl.CostEstimate(flops=0, bytes_accessed=60_000_000, transcendentals=0),
        name="collect",
    )(keys.reshape(parts, 1, tokens), counts.reshape(parts, 1, 1), grads)


def local(
    token_ids, mask_slots, mask_counts,
    embedding, out_table, qkv_weight, proj_weight, up_weight, down_weight, mod_weight, vectors,
    embedding_first, out_table_first, qkv_first, proj_first, up_first, down_first, mod_first,
    vectors_first,
    embedding_second, out_table_second, qkv_second, proj_second, up_second, down_second,
    mod_second, vectors_second,
):
    masters = (
        embedding, out_table, qkv_weight, proj_weight, up_weight, down_weight, mod_weight, vectors,
    )
    firsts = (
        embedding_first, out_table_first, qkv_first, proj_first, up_first, down_first, mod_first,
        vectors_first,
    )
    seconds = (
        embedding_second, out_table_second, qkv_second, proj_second, up_second, down_second,
        mod_second, vectors_second,
    )
    wide = lax.axis_size("wide")
    narrow = lax.axis_size("narrow")
    me = lax.axis_index("wide")
    group = lax.axis_index("narrow")
    part = group & 1
    micro = group >> 1
    entries, share = embedding.shape
    width = share * wide
    vocab = entries * narrow
    micro_count, length = token_ids.shape[1:]
    capacity = mask_slots.shape[2]
    rows = length // 2
    pair_total = 5 * length // 16
    quarter = pair_total // 4
    loss_scale = 1.0 / (length * micro_count * wide)
    positions = jnp.arange(length, dtype=jnp.int32)

    tokens, slots, counts = token_ids[0], mask_slots[0], mask_counts[0]
    at_slot = slots[:, :, None] == positions[None, None, :]
    valid = jnp.arange(capacity)[None, :] < counts[:, None]
    masked = jnp.any(at_slot & valid[:, :, None], axis=1)
    targets = jnp.sum(jnp.where(at_slot, tokens[:, None, :], 0), axis=2)
    inputs = jnp.where(masked, vocab - 1, tokens)
    packed = jnp.concatenate(
        [inputs, targets, jnp.broadcast_to(counts[:, None], (micro_count, 128))], axis=1
    )
    packed_all = spread_wide(packed)
    inputs_all = packed_all[:, :, :length]
    targets_all = packed_all[:, :, length : length + capacity]
    counts_all = packed_all[:, :, length + capacity]

    shard_a = jnp.concatenate(
        [qkv_weight[0], qkv_weight[1], qkv_weight[2], proj_weight.T], axis=1
    ).astype(BF)
    full_a = gather_narrow(gather_wide(shard_a))
    full_b = gather_narrow(gather_wide(up_weight.astype(BF)))
    full_c = gather_narrow(gather_wide(down_weight.T.astype(BF)))
    heads_width = width // narrow
    column = lambda k: [full[:, k * heads_width : (k + 1) * heads_width] for full in full_a]
    weight_qkv = jnp.concatenate(column(0) + column(1) + column(2), axis=1)
    weight_proj = jnp.concatenate(column(3), axis=1)

    chunk = entries // wide
    table_own = out_table.astype(BF).reshape(share, wide, chunk).transpose(1, 0, 2)
    tables = gather_narrow(swap_wide_async(table_own).reshape(width, chunk))

    moments = counts_all.astype(F32) / pair_total
    condition = jax.nn.silu(time_features(moments, mod_weight.shape[0]))
    condition_mine = lax.dynamic_index_in_dim(condition, micro, 1, keepdims=False)
    mod_part = jnp.dot(condition_mine, rounded(mod_weight), precision=HIGHEST)
    vector_part = jnp.broadcast_to(rounded(vectors), (wide, vectors.shape[0]))
    mod_recv = swap_wide(jnp.concatenate([mod_part, vector_part], axis=1))
    mod_share = mod_part.shape[1]
    vector_full = mod_recv[:, mod_share:].reshape(-1)
    modulation = mod_recv[:, :mod_share].reshape(-1) + vector_full[4 * width :]
    (
        shift_one, scale_one, gate_one, shift_two, scale_two, gate_two, shift_last, scale_last,
    ) = jnp.split(modulation, 8)
    gain_one, gain_two, gain_last, bias_down = jnp.split(vector_full[: 4 * width], 4)

    own_table = embedding.T.astype(BF)
    table_rows = (
        jnp.concatenate(
            [own_table, xor_narrow(own_table, 1), jnp.zeros((share, 128), BF)], axis=1
        )
        .astype(F32)
        .T
    )
    half_ids = lax.dynamic_slice_in_dim(inputs_all, part * rows, rows, axis=2)
    half_ids = jnp.stack(
        [
            lax.dynamic_index_in_dim(half_ids, micro, 1, keepdims=False),
            lax.dynamic_index_in_dim(half_ids, 1 - micro, 1, keepdims=False),
        ]
    )
    owner = half_ids // entries
    inside = half_ids - owner * entries
    places = jnp.where(
        owner == group, inside, jnp.where(owner == (group ^ 1), entries + inside, 2 * entries)
    )
    looked = lookup(table_rows, places.reshape(-1)).reshape(2, wide, rows, share)
    start_part = looked[0] + xor_narrow(looked[1], 2)
    start = swap_wide(start_part).astype(F32).transpose(1, 0, 2).reshape(rows, width)

    my_positions = part * rows + jnp.arange(rows, dtype=jnp.int32)
    far_positions = (1 - part) * rows + jnp.arange(rows, dtype=jnp.int32)
    key_cosine, key_sine = rotary_tables(jnp.concatenate([my_positions, far_positions]), HD)
    cosine, sine = key_cosine[:rows], key_sine[:rows]
    normed_one, inverse_one = layer_norm(start)
    hidden_one = (normed_one * gain_one * (1.0 + scale_one) + shift_one).astype(BF)
    projected = project_qkv(hidden_one, weight_qkv, cosine, sine)
    query = projected[:, :width]
    far = xor_narrow(projected[:, width:], 1)
    swapped = [
        far[:, kind * width + (s ^ 1) * heads_width : kind * width + ((s ^ 1) + 1) * heads_width]
        for kind in range(2)
        for s in range(narrow)
    ]
    keys = jnp.concatenate(
        [projected[:, width : 2 * width], jnp.concatenate(swapped[:narrow], axis=1)]
    )
    values = jnp.concatenate(
        [projected[:, 2 * width :], jnp.concatenate(swapped[narrow:], axis=1)]
    )
    mixed, logs = attend(query, keys, values)
    attended = mm(mixed, weight_proj, NT)
    middle = start + gate_one * attended
    normed_two, inverse_two = layer_norm(middle)
    hidden_two = (normed_two * gain_two * (1.0 + scale_two) + shift_two).astype(BF)
    inner = [mm(hidden_two, full_b[s], NN) for s in range(narrow)]
    active = [gelu_tanh(value).astype(BF) for value in inner]
    output = sum(mm(active[s], full_c[s], NT) for s in range(narrow))
    final = middle + gate_two * (output + bias_down)
    normed, inverse = layer_norm(final)
    lifted = gain_last * (1.0 + scale_last)
    hidden = (normed * lifted + shift_last).astype(BF)

    side = me // (wide // 2)
    low = me % (wide // 2)
    count_low = lax.dynamic_index_in_dim(
        lax.dynamic_index_in_dim(counts_all, low, 0, keepdims=False), micro, 0, keepdims=False
    )
    slot_row = lax.dynamic_index_in_dim(slots, micro, 0, keepdims=False)
    offset = jnp.arange(quarter, dtype=jnp.int32)
    order = jnp.concatenate(
        [
            s * (2 * quarter) + p * quarter + offset
            for p in (part, 1 - part)
            for s in (side, 1 - side)
        ]
    )
    from_low = order < count_low
    index = jnp.where(from_low, order, order - count_low)
    mine = from_low == (side == 0)
    wanted = jnp.sum(
        jnp.where(index[:, None] == jnp.arange(capacity)[None, :], slot_row[None, :], 0), axis=1
    )
    select = ((wanted[:, None] == my_positions[None, :]) & mine[:, None]).astype(BF)
    picked = mm(select, hidden, NN).astype(BF)
    picked = picked[: 2 * quarter] + xor_narrow(picked[2 * quarter :], 1)
    row_part = picked[:quarter] + xor_wide(picked[quarter:], wide // 2)
    head_rows = spread_wide(row_part).reshape(wide * quarter, width)

    targets_mine = lax.dynamic_index_in_dim(targets_all, micro, 1, keepdims=False)
    counts_mine = lax.dynamic_index_in_dim(counts_all, micro, 1, keepdims=False)
    pairs = wide // 2
    both = jnp.concatenate([targets_mine[:pairs], targets_mine[pairs:]], axis=1)
    spot = jnp.stack([s * 2 * quarter + part * quarter + offset for s in (0, 1)])
    low_counts = counts_mine[:pairs, None, None]
    spot = jnp.where(spot[None] < low_counts, spot[None], capacity + spot[None] - low_counts)
    row_targets = jnp.sum(
        jnp.where(
            spot[..., None] == jnp.arange(2 * capacity)[None, None, None, :],
            both[:, None, None, :],
            0,
        ),
        axis=-1,
    )
    row_targets = row_targets.transpose(1, 0, 2).reshape(-1)
    target_owner = row_targets // entries
    target_rest = row_targets - target_owner * entries
    target_wide = target_rest // chunk
    target_column = jnp.where(
        target_wide == me, (target_owner ^ group) * chunk + target_rest - target_wide * chunk, -1
    )

    logits = [mm(head_rows, table, NN) for table in tables]
    hitting = [
        jnp.arange(chunk)[None, :] + s * chunk == target_column[:, None] for s in range(narrow)
    ]
    top = functools.reduce(jnp.maximum, [jnp.max(value, axis=-1) for value in logits])
    total = sum(jnp.sum(jnp.exp(value - top[:, None]), axis=-1) for value in logits)
    target_logit = sum(
        jnp.sum(jnp.where(hit, value, 0.0), axis=-1) for hit, value in zip(hitting, logits)
    )
    stats = spread_wide(jnp.stack([top, total, target_logit]))
    top_all = jnp.max(stats[:, 0], axis=0)
    total_all = jnp.sum(stats[:, 1] * jnp.exp(stats[:, 0] - top_all[None]), axis=0)
    log_total = top_all + jnp.log(total_all)
    loss_part = jnp.sum(log_total - jnp.sum(stats[:, 2], axis=0))
    d_logits = [
        ((jnp.exp(value - log_total[:, None]) - hit.astype(F32)) * loss_scale).astype(BF)
        for hit, value in zip(hitting, logits)
    ]
    d_rows = sum(mm(grad, table, NT) for grad, table in zip(d_logits, tables))
    d_table_parts = [mm(head_rows, grad, TN) for grad in d_logits]
    d_table = scatter_narrow(d_table_parts).astype(BF).reshape(wide, share, chunk)
    d_table = swap_wide_async(d_table).astype(F32).transpose(1, 0, 2).reshape(share, entries)

    d_recv = swap_wide(d_rows.astype(BF).reshape(wide, quarter, width))
    d_mine = jnp.sum(d_recv.astype(F32), axis=0).astype(BF)
    d_sides = jnp.concatenate([d_mine, xor_wide(d_mine, wide // 2)])
    d_all = jnp.concatenate([d_sides, xor_narrow(d_sides, 1)])
    d_hidden = mm(select, d_all, TN)

    d_shift_last = jnp.sum(d_hidden, axis=0)
    d_hidden_normed = jnp.sum(d_hidden * normed, axis=0)
    d_scale_last = d_hidden_normed * gain_last
    d_gain_last = d_hidden_normed * (1.0 + scale_last)
    d_final = norm_back(d_hidden * lifted, normed, inverse)
    d_bias = jnp.sum(d_final, axis=0) * gate_two
    d_gate_two = jnp.sum(d_final * (output + bias_down), axis=0)
    d_output = (d_final * gate_two).astype(BF)
    d_inner = [
        (mm(d_output, full_c[s], NN) * gelu_slope(inner[s])).astype(BF) for s in range(narrow)
    ]
    d_c = [mm(d_output, active[s], TN) for s in range(narrow)]
    d_b = [mm(hidden_two, d_inner[s], TN) for s in range(narrow)]
    d_c = scatter_wide(scatter_narrow(d_c).reshape(wide, share, width))
    d_b = scatter_wide(scatter_narrow(d_b).reshape(wide, share, width))
    d_hidden_two = sum(mm(d_inner[s], full_b[s], NT) for s in range(narrow))
    d_shift_two = jnp.sum(d_hidden_two, axis=0)
    d_two_normed = jnp.sum(d_hidden_two * normed_two, axis=0)
    d_scale_two = d_two_normed * gain_two
    d_gain_two = d_two_normed * (1.0 + scale_two)
    d_middle = d_final + norm_back(
        d_hidden_two * gain_two * (1.0 + scale_two), normed_two, inverse_two
    )
    d_gate_one = jnp.sum(d_middle * attended, axis=0)
    d_attended = (d_middle * gate_one).astype(BF)
    d_proj = mm(d_attended, mixed, TN)
    d_mixed = mm(d_attended, weight_proj, NN).astype(BF)
    d_query, d_keys, d_values, d_keys_far, d_values_far = attend_back(
        query, keys, values, d_mixed, logs, cosine, sine, key_cosine, key_sine
    )
    d_far = xor_narrow(jnp.concatenate([d_keys_far, d_values_far], axis=1), 1)
    d_far = jnp.concatenate(
        [
            d_far[:, kind * width + (s ^ 1) * heads_width : kind * width + ((s ^ 1) + 1) * heads_width]
            for kind in range(2)
            for s in range(narrow)
        ],
        axis=1,
    ).astype(F32)
    d_projected = jnp.concatenate(
        [
            d_query,
            (d_keys + d_far[:, :width]).astype(BF),
            (d_values + d_far[:, width:]).astype(BF),
        ],
        axis=1,
    )
    d_qkv = mm(hidden_one, d_projected, TN)
    d_a = [
        jnp.concatenate(
            [
                d_qkv[:, kind * width + s * heads_width : kind * width + (s + 1) * heads_width]
                for kind in range(3)
            ]
            + [d_proj[:, s * heads_width : (s + 1) * heads_width]],
            axis=1,
        )
        for s in range(narrow)
    ]
    d_a = scatter_wide(scatter_narrow(d_a).reshape(wide, share, width))
    d_hidden_one = mm(d_projected, weight_qkv, NT)
    d_shift_one = jnp.sum(d_hidden_one, axis=0)
    d_one_normed = jnp.sum(d_hidden_one * normed_one, axis=0)
    d_scale_one = d_one_normed * gain_one
    d_gain_one = d_one_normed * (1.0 + scale_one)
    d_start = d_middle + norm_back(
        d_hidden_one * gain_one * (1.0 + scale_one), normed_one, inverse_one
    )

    padded = rows + 16
    mask_entry = vocab - 1
    my_inputs = lax.dynamic_slice_in_dim(
        lax.dynamic_index_in_dim(inputs, micro, 0, keepdims=False), part * rows, rows, axis=0
    )
    mask_sum = jnp.sum(jnp.where((my_inputs == mask_entry)[:, None], d_start, 0.0), axis=0)
    d_start_rows = jnp.concatenate(
        [d_start, mask_sum[None], jnp.zeros((padded - rows - 1, width), F32)]
    ).astype(BF)
    d_start_recv = swap_wide(d_start_rows.reshape(padded, wide, share).transpose(1, 0, 2))
    d_start_all = jnp.stack(gather_narrow(d_start_recv.reshape(wide * padded, share)))
    ids = jnp.stack(
        [
            lax.dynamic_slice_in_dim(
                lax.dynamic_index_in_dim(inputs_all, (group ^ s) >> 1, 1, keepdims=False),
                ((group ^ s) & 1) * rows,
                rows,
                axis=1,
            )
            for s in range(narrow)
        ]
    )
    ids = jnp.concatenate(
        [
            jnp.where(ids == mask_entry, -1, ids),
            jnp.full((narrow, wide, 1), mask_entry, jnp.int32),
            jnp.full((narrow, wide, padded - rows - 1), -1, jnp.int32),
        ],
        axis=2,
    ).reshape(narrow, wide * padded)
    local_ids = ids - group * entries
    here = (local_ids >= 0) & (local_ids < entries)
    shift = (wide * padded - 1).bit_length()
    sort_keys = jnp.where(
        here,
        local_ids * (1 << shift) + jnp.arange(wide * padded, dtype=jnp.int32)[None, :],
        jnp.iinfo(jnp.int32).max,
    )
    sort_keys = lax.sort(sort_keys, dimension=1)
    hits = jnp.sum(here.astype(jnp.int32), axis=1)
    d_embed = collect(sort_keys, hits, d_start_all, shift, entries)

    d_modulation = jnp.concatenate(
        (
            d_shift_one, d_scale_one, d_gate_one, d_shift_two, d_scale_two, d_gate_two,
            d_shift_last, d_scale_last,
        )
    )
    d_vector = jnp.concatenate((d_gain_one, d_gain_two, d_gain_last, d_bias, d_modulation))
    small = jnp.concatenate(
        [d_modulation.reshape(wide, -1), d_vector.reshape(wide, -1)], axis=1
    )
    small = swap_wide(small)
    small = small + xor_narrow(small, 1)
    small_far = xor_narrow(small, 2)
    d_vectors = jnp.sum(small[:, mod_share:] + small_far[:, mod_share:], axis=0)
    condition_far = lax.dynamic_index_in_dim(condition, 1 - micro, 1, keepdims=False)
    d_mod_weight = lax.dot_general(
        condition_mine, small[:, :mod_share], TN, precision=HIGHEST
    ) + lax.dot_general(condition_far, small_far[:, :mod_share], TN, precision=HIGHEST)

    shards = (
        d_embed,
        d_table,
        jnp.stack([d_a[:, k * heads_width : (k + 1) * heads_width] for k in range(3)]),
        d_a[:, 3 * heads_width :].T,
        d_b,
        d_c.T,
        d_mod_weight,
        d_vectors,
    )

    square = jnp.zeros((), F32)
    for grad in shards[:6]:
        square = square + jnp.sum(grad * grad)
    shared_square = jnp.sum(shards[6] * shards[6]) + jnp.sum(shards[7] * shards[7])
    square = square + shared_square / narrow
    sums = lax.all_to_all(
        jnp.broadcast_to(jnp.stack([loss_part / wide, square])[None, None], (wide * narrow, 1, 2)),
        ("wide", "narrow"),
        0,
        0,
        tiled=True,
    )
    sums = jnp.sum(sums, axis=(0, 1))
    loss_sum = sums[0]
    grad_norm = jnp.sqrt(sums[1])
    factor = CLIP_NORM / jnp.maximum(grad_norm, CLIP_NORM)
    results = []
    for member in range(8):
        grad = shards[member] * factor
        first = BETA_ONE * firsts[member] + (1.0 - BETA_ONE) * grad
        second = BETA_TWO * seconds[member] + (1.0 - BETA_TWO) * grad * grad
        stepped = (
            first / (1.0 - BETA_ONE**STEP) / (jnp.sqrt(second / (1.0 - BETA_TWO**STEP)) + ADAM_EPS)
        )
        decay = WEIGHT_DECAY if member < 7 else 0.0
        fresh = masters[member] - LEARN_RATES[member] * (stepped + decay * masters[member])
        results.extend([fresh, first, second])
    return (loss_sum, grad_norm, *results)


def solution(mesh):
    weights = (
        P("narrow", "wide"),
        P("wide", "narrow"),
        P(None, "wide", "narrow"),
        P("narrow", "wide"),
        P("wide", "narrow"),
        P("narrow", "wide"),
        P(None, "wide"),
        P("wide"),
    )
    data = (P("wide", None, None), P("wide", None, None), P("wide", None))
    outs = [P(), P()]
    for spec in weights:
        outs.extend([spec] * 3)
    return jax.shard_map(
        local,
        mesh=mesh,
        in_specs=data + weights * 3,
        out_specs=tuple(outs),
        check_vma=False,
    )
```

```python
import functools
import math

import jax
import jax.numpy as jnp
from jax import lax
from jax.experimental import pallas as pl
from jax.experimental.pallas import tpu as pltpu
from jax.sharding import PartitionSpec as P

HD = 64
STEP = 10

HIGHEST = lax.Precision.HIGHEST
NORM_EPS = 1e-06
CLIP_NORM = 0.005
BETA_ONE = 0.9
BETA_TWO = 0.95
ADAM_EPS = 1e-08
WEIGHT_DECAY = 0.1
LEARN_RATES = (1.0, 0.1, 0.07, 0.5, 0.07, 0.04, 0.2, 0.5)
NARROW = ("line", "core")
BF = jnp.bfloat16
F32 = jnp.float32
VMEM_LIMIT = 56 * 1024 * 1024
FREE = pl.CostEstimate(flops=0, bytes_accessed=0, transcendentals=0)


def together(*values):
    return lax.optimization_barrier(values)


def xor_narrow(value, bits):
    return lax.ppermute(
        value, NARROW, [(i, i ^ bits) for i in range(lax.axis_size(NARROW))]
    )


def xor_wide(value, bits):
    return lax.ppermute(value, "wide", [(i, i ^ bits) for i in range(lax.axis_size("wide"))])


def swap_wide(value):
    return lax.all_to_all(value, "wide", 0, 0, tiled=True)


def spread_wide(value):
    if lax.axis_size("wide") > 8:
        return lax.all_gather(value, "wide")
    return swap_wide(jnp.broadcast_to(value[None], (lax.axis_size("wide"),) + value.shape))


def gather_wide(value, axis):
    return lax.all_gather(value, "wide", axis=axis, tiled=True)


def scatter_wide(value):
    count = lax.axis_size("wide")
    if count != 8:
        return lax.psum_scatter(value, "wide", scatter_dimension=0)
    me = lax.axis_index("wide")
    side = me & 1
    pairs = value.reshape((4, 2) + value.shape[1:])
    kept = lax.dynamic_index_in_dim(pairs, side, 1, keepdims=False)
    sent = lax.dynamic_index_in_dim(pairs, 1 - side, 1, keepdims=False).astype(BF)
    half = kept.astype(F32) + xor_wide(sent, 1).astype(F32)
    depth = me >> 1
    total = lax.dynamic_index_in_dim(half, depth, 0, keepdims=False)
    low = half.astype(BF)
    for k in (1, 2, 3):
        piece = lax.dynamic_index_in_dim(low, depth ^ k, 0, keepdims=False)
        total = total + xor_wide(piece, 2 * k).astype(F32)
    return total


def scatter_core(sent, own):
    from_core = xor_narrow(sent, 1).astype(F32)
    near = own[0].astype(F32) + from_core[0]
    far = own[1].astype(F32) + from_core[1]
    return near, far.astype(BF)


def gather_narrow(value):
    across = xor_narrow(value, 2)
    beside = xor_narrow(value, 1)
    corner = xor_narrow(across, 1)
    return value, beside, across, corner


def rounded(value):
    return lax.reduce_precision(value, exponent_bits=8, mantissa_bits=7)


def layer_norm(values):
    centered = values - jnp.mean(values, axis=-1, keepdims=True)
    inverse = lax.rsqrt(jnp.mean(centered * centered, axis=-1, keepdims=True) + NORM_EPS)
    return (centered * inverse, inverse)


def norm_back(grad, normed, inverse):
    return inverse * (
        grad
        - jnp.mean(grad, axis=-1, keepdims=True)
        - normed * jnp.mean(grad * normed, axis=-1, keepdims=True)
    )


def gelu_tanh(values):
    inner = 0.7978845608 * (values + 0.044715 * values * values * values)
    return 0.5 * values * (1.0 + jnp.tanh(inner))


def gelu_slope(values):
    tangent = jnp.tanh(0.7978845608 * (values + 0.044715 * values * values * values))
    return 0.5 * (1.0 + tangent) + 0.5 * values * (1.0 - tangent * tangent) * 0.7978845608 * (
        1.0 + 0.134145 * values * values
    )


def rotary_tables(positions, width):
    freqs = jnp.exp(jnp.arange(width // 2, dtype=F32) * (-2.0 * math.log(10000.0) / width))
    angle = positions.astype(F32)[:, None] * freqs[None, :]
    cosine, sine = jnp.cos(angle), jnp.sin(angle)
    return (
        jnp.concatenate([cosine] * 4, axis=1),
        jnp.concatenate([-sine, sine, -sine, sine], axis=1),
    )


def time_features(moment, width):
    freqs = jnp.exp(jnp.arange(width // 2, dtype=F32) * (-math.log(10000.0) / (width // 2)))
    angle = 1000.0 * moment[..., None] * freqs
    return jnp.concatenate([jnp.cos(angle), jnp.sin(angle)], axis=-1)


def turned(values, cosine, sine):
    blocks = []
    for place in range(0, values.shape[1], 2 * HD):
        block = values[:, place : place + 2 * HD]
        lanes = lax.broadcasted_iota(jnp.int32, block.shape, 1)
        ahead = pltpu.roll(block, 2 * HD - HD // 2, 1)
        behind = pltpu.roll(block, HD // 2, 1)
        other = jnp.where((lanes & (HD - 1)) < HD // 2, ahead, behind)
        blocks.append(block * cosine + other * sine)
    return jnp.concatenate(blocks, axis=1) if len(blocks) > 1 else blocks[0]


def turned_back(values, cosine, sine):
    spare = -values.shape[1] % (2 * HD)
    filled = jnp.concatenate([values, jnp.zeros((values.shape[0], spare), F32)], axis=1)
    return turned(filled, cosine, -sine)[:, : values.shape[1]]


NT = (((1,), (1,)), ((), ()))
NN = (((1,), (0,)), ((), ()))
TN = (((0,), (0,)), ((), ()))


def mm(a, b, dims):
    return lax.dot_general(a, b, dims, preferred_element_type=F32)


SHIFT_ONE, SCALE_ONE, GATE_ONE, SHIFT_TWO, SCALE_TWO, GATE_TWO, SHIFT_LAST, SCALE_LAST = range(8)
GAIN_ONE, GAIN_TWO, GAIN_LAST, BIAS_DOWN = range(8, 12)
LOCAL = dict(
    compiler_params=pltpu.CompilerParams(vmem_limit_bytes=60 * 1024 * 1024), cost_estimate=FREE
)
BUSY = dict(LOCAL, cost_estimate=pl.CostEstimate(10**10, 0, 4 * 10**7))


def column_sum(values):
    return jnp.sum(values, axis=0, keepdims=True)


def qkv_kernel(
    recv_ref, par_ref, a0, a1, a2, a3, cos_ref, sin_ref, q_ref, kv_ref, hidden_ref, start_ref
):
    par = lambda k: par_ref[k : k + 1, :]
    rows = start_ref.shape[0]
    start = jnp.concatenate(
        [recv_ref[piece, :rows, :].astype(F32) for piece in range(recv_ref.shape[0])], axis=1
    )
    start_ref[...] = start
    normed, _ = layer_norm(start)
    hidden = normed * par(GAIN_ONE) * (1.0 + par(SCALE_ONE)) + par(SHIFT_ONE)
    hidden = hidden.astype(BF)
    hidden_ref[...] = hidden
    share = q_ref.shape[2]
    for s, weight in enumerate((a0, a1, a2, a3)):
        value = mm(hidden, weight[...], NN)
        pair = turned(value[:, : 2 * share], cos_ref[...], sin_ref[...])
        q_ref[s] = pair[:, :share].astype(BF)
        kv_ref[s] = jnp.concatenate(
            [pair[:, share:], value[:, 2 * share : 3 * share]], axis=1
        ).astype(BF)


def project_qkv(recv, params, weights, cosine, sine):
    rows, width = cosine.shape[0], params.shape[1]
    share = width // 4
    return pl.pallas_call(
        qkv_kernel,
        out_shape=[
            jax.ShapeDtypeStruct((4, rows, share), BF),
            jax.ShapeDtypeStruct((4, rows, 2 * share), BF),
            jax.ShapeDtypeStruct((rows, width), BF),
            jax.ShapeDtypeStruct((rows, width), F32),
        ],
        name="qkv",
        **LOCAL,
    )(recv, params, *weights, cosine, sine)


def head_mask(values, head):
    lanes = lax.broadcasted_iota(jnp.int32, values.shape, 1)
    inside = (lanes >= head * HD) & (lanes < (head + 1) * HD)
    return jnp.where(inside, values, jnp.zeros_like(values))


def attend_kernel(q_ref, own_ref, far_ref, out_ref, log_ref):
    query = q_ref[0] * BF(HD**-0.5)
    share = query.shape[1]
    both = jnp.concatenate([own_ref[0], far_ref[0]], axis=0)
    keys, values = both[:, :share], both[:, share:].T
    parts = []
    for head in range(query.shape[1] // HD):
        scores = mm(keys, head_mask(query, head), NT)
        top = jnp.max(scores, axis=0, keepdims=True)
        shifted = jnp.exp(scores - top)
        total = jnp.sum(shifted, axis=0, keepdims=True)
        weights = (shifted * (1.0 / total)).astype(BF)
        parts.append(mm(values[head * HD : (head + 1) * HD], weights, NN))
        log_ref[0, head : head + 1, :] = top + jnp.log(total)
    out_ref[0] = jnp.concatenate(parts, axis=0).T.astype(BF)


def attend_specs(rows, share):
    return [
        pl.BlockSpec((1, rows, share), lambda s: (s, 0, 0)),
        pl.BlockSpec((1, rows, 2 * share), lambda s: (s, 0, 0)),
        pl.BlockSpec((1, rows, 2 * share), lambda s: (s ^ 1, 0, 0)),
    ]


def attend(query, own, far):
    slots, rows, share = query.shape
    heads = share // HD
    return pl.pallas_call(
        attend_kernel,
        grid=(slots,),
        in_specs=attend_specs(rows, share),
        out_specs=[
            pl.BlockSpec((1, rows, share), lambda s: (s, 0, 0)),
            pl.BlockSpec((1, heads, rows), lambda s: (s, 0, 0)),
        ],
        out_shape=[
            jax.ShapeDtypeStruct((slots, rows, share), BF),
            jax.ShapeDtypeStruct((slots, heads, rows), F32),
        ],
        name="attend",
        **LOCAL,
    )(query, own, far)


def feed_kernel(
    mixed_ref, start_ref, par_ref, a0, a1, a2, a3, bc0, bc1, bc2, bc3, select_ref,
    attended_ref, middle_ref, output_ref, hidden_ref, inner_ref, picked_ref,
):
    par = lambda k: par_ref[k : k + 1, :]
    share = mixed_ref.shape[2]
    attended = sum(
        mm(mixed_ref[s], weight[:, 3 * share :], NT) for s, weight in enumerate((a0, a1, a2, a3))
    )
    attended_ref[...] = attended
    middle = start_ref[...] + par(GATE_ONE) * attended
    middle_ref[...] = middle
    normed, _ = layer_norm(middle)
    hidden = normed * par(GAIN_TWO) * (1.0 + par(SCALE_TWO)) + par(SHIFT_TWO)
    hidden = hidden.astype(BF)
    hidden_ref[...] = hidden
    output = jnp.zeros(middle.shape, F32)
    for s, weight in enumerate((bc0, bc1, bc2, bc3)):
        inner = mm(hidden, weight[0], NN)
        inner_ref[s] = inner
        output = output + mm(gelu_tanh(inner).astype(BF), weight[1], NT)
    output_ref[...] = output
    final = middle + par(GATE_TWO) * (output + par(BIAS_DOWN))
    normed, _ = layer_norm(final)
    last = normed * (par(GAIN_LAST) * (1.0 + par(SCALE_LAST))) + par(SHIFT_LAST)
    picked_ref[...] = mm(select_ref[...], last.astype(BF), NN).astype(BF)


def feed(mixed, start, params, weights_a, weights_bc, select):
    rows, width = start.shape
    plain = jax.ShapeDtypeStruct((rows, width), F32)
    return pl.pallas_call(
        feed_kernel,
        out_shape=[
            plain,
            plain,
            plain,
            jax.ShapeDtypeStruct((rows, width), BF),
            jax.ShapeDtypeStruct((4, rows, width), F32),
            jax.ShapeDtypeStruct((select.shape[0], width), BF),
        ],
        name="feed",
        **LOCAL,
    )(mixed, start, params, *weights_a, *weights_bc, select)


SLOT_PLACES = ((1, 0, 0), (3, 0, 1), (0, 1, 0), (2, 1, 1))


def feed_back_kernel(
    rows_ref, select_ref, par_ref, middle_ref, output_ref, attended_ref, hidden_ref, inner_ref,
    a0, a1, a2, a3, bc0, bc1, bc2, bc3,
    d_middle_ref, d_attended_ref, d_mixed_ref, sent_ref, own_ref, vec_ref,
):
    par = lambda k: par_ref[k : k + 1, :]
    share = d_mixed_ref.shape[2]
    middle, output = middle_ref[...], output_ref[...]
    d_hidden = mm(select_ref[...], rows_ref[...], TN)
    final = middle + par(GATE_TWO) * (output + par(BIAS_DOWN))
    normed, inverse = layer_norm(final)
    d_normed = column_sum(d_hidden * normed)
    vec_ref[SHIFT_LAST : SHIFT_LAST + 1, :] = column_sum(d_hidden)
    vec_ref[SCALE_LAST : SCALE_LAST + 1, :] = d_normed * par(GAIN_LAST)
    vec_ref[GAIN_LAST : GAIN_LAST + 1, :] = d_normed * (1.0 + par(SCALE_LAST))
    d_final = norm_back(d_hidden * (par(GAIN_LAST) * (1.0 + par(SCALE_LAST))), normed, inverse)
    vec_ref[BIAS_DOWN : BIAS_DOWN + 1, :] = column_sum(d_final) * par(GATE_TWO)
    vec_ref[GATE_TWO : GATE_TWO + 1, :] = column_sum(d_final * (output + par(BIAS_DOWN)))
    d_output = (d_final * par(GATE_TWO)).astype(BF)
    hidden = hidden_ref[...]
    d_hidden = jnp.zeros(middle.shape, F32)
    weights = (bc0, bc1, bc2, bc3)
    for s, kept, place in SLOT_PLACES:
        out_ref = own_ref if kept else sent_ref
        inner = inner_ref[s]
        tangent = jnp.tanh(0.7978845608 * (inner + 0.044715 * inner * inner * inner))
        active = (0.5 * inner * (1.0 + tangent)).astype(BF)
        slope = 0.5 * (1.0 + tangent) + 0.5 * inner * (
            1.0 - tangent * tangent
        ) * 0.7978845608 * (1.0 + 0.134145 * inner * inner)
        d_inner = (mm(d_output, weights[s][1], NN) * slope).astype(BF)
        out_ref[place, 0] = mm(hidden, d_inner, TN).astype(BF)
        out_ref[place, 1] = mm(d_output, active, TN).astype(BF)
        d_hidden = d_hidden + mm(d_inner, weights[s][0], NT)
    normed, inverse = layer_norm(middle)
    d_normed = column_sum(d_hidden * normed)
    vec_ref[SHIFT_TWO : SHIFT_TWO + 1, :] = column_sum(d_hidden)
    vec_ref[SCALE_TWO : SCALE_TWO + 1, :] = d_normed * par(GAIN_TWO)
    vec_ref[GAIN_TWO : GAIN_TWO + 1, :] = d_normed * (1.0 + par(SCALE_TWO))
    d_middle = d_final + norm_back(
        d_hidden * par(GAIN_TWO) * (1.0 + par(SCALE_TWO)), normed, inverse
    )
    d_middle_ref[...] = d_middle
    vec_ref[GATE_ONE : GATE_ONE + 1, :] = column_sum(d_middle * attended_ref[...])
    d_attended = (d_middle * par(GATE_ONE)).astype(BF)
    d_attended_ref[...] = d_attended
    for s, weight in enumerate((a0, a1, a2, a3)):
        d_mixed_ref[s] = mm(d_attended, weight[:, 3 * share :], NN).astype(BF)
    for unused in (SHIFT_ONE, SCALE_ONE, GAIN_ONE):
        vec_ref[unused : unused + 1, :] = jnp.zeros_like(par(0))


def feed_back(
    d_rows, select, params, middle, output, attended, hidden, inner, weights_a, weights_bc
):
    rows, width = middle.shape
    half = jax.ShapeDtypeStruct((2, 2, width, width), BF)
    return pl.pallas_call(
        feed_back_kernel,
        out_shape=[
            jax.ShapeDtypeStruct((rows, width), F32),
            jax.ShapeDtypeStruct((rows, width), BF),
            jax.ShapeDtypeStruct((4, rows, width // 4), BF),
            half,
            half,
            jax.ShapeDtypeStruct(params.shape, F32),
        ],
        name="feed_back",
        **LOCAL,
    )(
        d_rows, select, params, middle, output, attended, hidden, inner, *weights_a, *weights_bc
    )


def attend_back_kernel(
    q_ref, own_ref, far_ref, grad_ref, log_ref, cos_ref, sin_ref, kcos_ref, ksin_ref,
    dq_ref, d_own_ref, d_far_ref,
):
    query, grad = q_ref[0], grad_ref[0]
    share = query.shape[1]
    both = jnp.concatenate([own_ref[0], far_ref[0]], axis=0)
    keys, values = both[:, :share], both[:, share:]
    turned_keys = keys.T
    scale = HD**-0.5
    rows = query.shape[0]
    dq = []
    dk = jnp.zeros(keys.shape, F32)
    dv = jnp.zeros(keys.shape, F32)
    for head in range(query.shape[1] // HD):
        query_one = head_mask(query * BF(scale), head)
        grad_one = head_mask(grad, head)
        scores = mm(keys, query_one, NT)
        weights = jnp.exp(scores - log_ref[0, head : head + 1, :])
        d_weights = mm(values, grad_one, NT)
        delta = jnp.sum(weights * d_weights, axis=0, keepdims=True)
        d_scores = (weights * (d_weights - delta)).astype(BF)
        dq.append(mm(turned_keys[head * HD : (head + 1) * HD], d_scores, NN))
        dk = dk + mm(d_scores, query_one, NN)
        dv = dv + mm(weights.astype(BF), grad_one, NN)
    dq = jnp.concatenate(dq, axis=0).T * scale
    dq_ref[0] = turned_back(dq, cos_ref[...], sin_ref[...]).astype(BF)
    dk = turned_back(dk, kcos_ref[...], ksin_ref[...])
    both = jnp.concatenate([dk, dv], axis=1)
    d_own_ref[0] = both[:rows]
    d_far_ref[0] = both[rows:].astype(BF)


def attend_back(query, own, far, grad, logs, cosine, sine, key_cosine, key_sine):
    slots, rows, share = query.shape
    heads = share // HD
    whole = lambda table: pl.BlockSpec(table.shape, lambda s: (0, 0))
    one, two, other = attend_specs(rows, share)
    return pl.pallas_call(
        attend_back_kernel,
        grid=(slots,),
        in_specs=[
            one, two, other, one, pl.BlockSpec((1, heads, rows), lambda s: (s, 0, 0)),
            whole(cosine), whole(sine), whole(key_cosine), whole(key_sine),
        ],
        out_specs=[one, two, two],
        out_shape=[
            jax.ShapeDtypeStruct((slots, rows, share), BF),
            jax.ShapeDtypeStruct((slots, rows, 2 * share), F32),
            jax.ShapeDtypeStruct((slots, rows, 2 * share), BF),
        ],
        name="attend_back",
        **LOCAL,
    )(query, own, far, grad, logs, cosine, sine, key_cosine, key_sine)


def slot_grads(dq_ref, d_own_ref, d_far_ref, s):
    return jnp.concatenate(
        [
            dq_ref[s],
            (d_own_ref[s] + d_far_ref[s ^ 1].astype(F32)).astype(BF),
        ],
        axis=1,
    )


def qkv_back_kernel(
    dq_ref, d_own_ref, d_far_ref, a0, a1, a2, a3, d_middle_ref, start_ref, par_ref, mask_ref,
    out_ref, grads_ref, vec_ref,
):
    par = lambda k: par_ref[k : k + 1, :]
    share = dq_ref.shape[2]
    rows = start_ref.shape[0]
    d_hidden = jnp.zeros(start_ref.shape, F32)
    for s, weight in enumerate((a0, a1, a2, a3)):
        grads = slot_grads(dq_ref, d_own_ref, d_far_ref, s)
        grads_ref[s] = grads
        d_hidden = d_hidden + mm(grads, weight[:, : 3 * share], NT)
    normed, inverse = layer_norm(start_ref[...])
    d_normed = column_sum(d_hidden * normed)
    vec_ref[0:1, :] = column_sum(d_hidden)
    vec_ref[1:2, :] = d_normed * par(GAIN_ONE)
    vec_ref[2:3, :] = d_normed * (1.0 + par(SCALE_ONE))
    d_start = d_middle_ref[...] + norm_back(
        d_hidden * par(GAIN_ONE) * (1.0 + par(SCALE_ONE)), normed, inverse
    )
    masked = column_sum(d_start * mask_ref[...])
    extra = out_ref.shape[1] - rows
    first = lax.broadcasted_iota(jnp.int32, (extra, 1), 0) == 0
    whole = jnp.concatenate([d_start, jnp.where(first, masked, 0.0)], axis=0).astype(BF)
    columns = out_ref.shape[2]
    for piece in range(out_ref.shape[0]):
        out_ref[piece] = whole[:, piece * columns : (piece + 1) * columns]


def qkv_back(dq, d_own, d_far, weights, d_middle, start, params, is_mask, padded, wide):
    rows, width = start.shape
    return pl.pallas_call(
        qkv_back_kernel,
        out_shape=[
            jax.ShapeDtypeStruct((wide, padded, width // wide), BF),
            jax.ShapeDtypeStruct((4, rows, 3 * width // 4), BF),
            jax.ShapeDtypeStruct((3, width), F32),
        ],
        name="qkv_back",
        **LOCAL,
    )(dq, d_own, d_far, *weights, d_middle, start, params, is_mask)


def qkv_grads_kernel(grads_ref, hidden_ref, d_attended_ref, mixed_ref, sent_ref, own_ref):
    for s, kept, place in SLOT_PLACES:
        out_ref = own_ref if kept else sent_ref
        out_ref[place] = jnp.concatenate(
            [
                mm(hidden_ref[...], grads_ref[s], TN),
                mm(d_attended_ref[...], mixed_ref[s], TN),
            ],
            axis=1,
        ).astype(BF)


def qkv_grads(grads, hidden, d_attended, mixed):
    width = hidden.shape[1]
    half = jax.ShapeDtypeStruct((2, width, width), BF)
    return pl.pallas_call(
        qkv_grads_kernel, out_shape=[half, half], name="qkv_grads", **BUSY
    )(grads, hidden, d_attended, mixed)


def rows_kernel(own_ref, other_ref, out_ref):
    step = pl.program_id(0)
    half = pl.num_programs(0) // 2

    @pl.when(step < half)
    def _():
        out_ref[...] = own_ref[...].astype(BF).astype(F32).T

    @pl.when((step >= half) & (step < 2 * half))
    def _():
        out_ref[...] = other_ref[...].astype(F32).T

    @pl.when(step == 2 * half)
    def _():
        out_ref[...] = jnp.zeros_like(out_ref)


def table_rows_of(own, other):
    width, entries = own.shape
    block = next(b for b in (1408, 1152, 384, 128) if entries % b == 0)
    half = entries // block
    return pl.pallas_call(
        rows_kernel,
        grid=(2 * half + 1,),
        in_specs=[
            pl.BlockSpec((width, block), lambda i: (0, jnp.minimum(i, half - 1))),
            pl.BlockSpec((width, block), lambda i: (0, jnp.clip(i - half, 0, half - 1))),
        ],
        out_specs=pl.BlockSpec((block, width), lambda i: (i, 0)),
        out_shape=jax.ShapeDtypeStruct((2 * entries + block, width), F32),
        name="table_rows",
        **BUSY,
    )(own, other)


def lookup_kernel(id_ref, table_ref, out_ref, scratch):
    block = scratch.shape[0]
    unroll = 16

    def body(step, _):
        for k in range(unroll):
            place = step * unroll + k
            scratch[pl.ds(place, 1), :] = table_ref[pl.ds(id_ref[0, 0, place], 1), :]
        return 0

    lax.fori_loop(0, block // unroll, body, 0)
    out_ref[...] = scratch[...].astype(BF)


def lookup(table, ids):
    count = ids.shape[0]
    block = min(2048, count)
    width = table.shape[1]
    return pl.pallas_call(
        lookup_kernel,
        grid=(count // block,),
        in_specs=[
            pl.BlockSpec((1, 1, block), lambda i: (i, 0, 0), memory_space=pltpu.SMEM),
            pl.BlockSpec(table.shape, lambda i: (0, 0), pipeline_mode=pl.Buffered(1)),
        ],
        out_specs=pl.BlockSpec((block, width), lambda i: (i, 0)),
        out_shape=jax.ShapeDtypeStruct((count, width), BF),
        scratch_shapes=[pltpu.VMEM((block, width), F32)],
        name="lookup",
        **LOCAL,
    )(ids.reshape(count // block, 1, block), table)


def collect_kernel(shift, first, key_ref, count_ref, grad_ref, *refs):
    step = pl.program_id(0)
    if first:
        out_ref, rows_ref = refs
        sum_ref = out_ref
    else:
        old_ref, out_ref, rows_ref, sum_ref = refs

    @pl.when(step == 0)
    def _():
        sum_ref[...] = jnp.zeros_like(sum_ref) if first else old_ref[...]

    rows_ref[...] = grad_ref[0].astype(F32)
    mask = (1 << shift) - 1
    count = count_ref[0, 0, 0]
    unroll = 8

    def group(item, _):
        keys = [key_ref[0, 0, item * unroll + k] for k in range(unroll)]
        targets = [lax.shift_right_logical(key, shift) for key in keys]
        olds = [sum_ref[pl.ds(target, 1), :] for target in targets]
        news = [rows_ref[pl.ds(key & mask, 1), :] for key in keys]
        sums = []
        for k in range(unroll):
            old = olds[k]
            if k:
                old = jnp.where(targets[k] == targets[k - 1], sums[k - 1], old)
            sums.append(old + news[k])
        for k in range(unroll):
            sum_ref[pl.ds(targets[k], 1), :] = sums[k]
        return 0

    def single(item, _):
        key = key_ref[0, 0, item]
        target = pl.ds(lax.shift_right_logical(key, shift), 1)
        sum_ref[target, :] = sum_ref[target, :] + rows_ref[pl.ds(key & mask, 1), :]
        return 0

    groups = lax.shift_right_logical(count, 3)
    lax.fori_loop(0, groups, group, 0)
    lax.fori_loop(groups * unroll, count, single, 0)

    if not first:

        @pl.when(step == pl.num_programs(0) - 1)
        def _():
            def turn(block, _):
                place = pl.ds(pl.multiple_of(block * 128, 128), 128)
                out_ref[:, place] = sum_ref[place, :].T
                return 0

            lax.fori_loop(0, sum_ref.shape[0] // 128, turn, 0)


def collect(keys, counts, grads, shift, before, entries):
    parts, tokens, width = grads.shape
    first = before is None
    out_dims = (entries, width) if first else (width, entries)
    scratch = [pltpu.VMEM((tokens, width), F32)]
    if not first:
        scratch.append(pltpu.VMEM((entries, width), F32))
    return pl.pallas_call(
        functools.partial(collect_kernel, shift, first),
        grid=(parts,),
        in_specs=[
            pl.BlockSpec((1, 1, tokens), lambda i: (i, 0, 0), memory_space=pltpu.SMEM),
            pl.BlockSpec((1, 1, 1), lambda i: (i, 0, 0), memory_space=pltpu.SMEM),
            pl.BlockSpec((1, tokens, width), lambda i: (i, 0, 0)),
        ]
        + ([] if first else [pl.BlockSpec((entries, width), lambda i: (0, 0), pipeline_mode=pl.Buffered(1))]),
        out_specs=pl.BlockSpec(out_dims, lambda i: (0, 0)),
        out_shape=jax.ShapeDtypeStruct(out_dims, F32),
        scratch_shapes=scratch,
        compiler_params=pltpu.CompilerParams(vmem_limit_bytes=VMEM_LIMIT),
        cost_estimate=FREE,
        name="collect",
    )(*[keys.reshape(parts, 1, tokens), counts.reshape(parts, 1, 1), grads] + ([] if first else [before]))


def local(
    token_ids, mask_slots, mask_counts,
    embedding, out_table, qkv_weight, proj_weight, up_weight, down_weight, mod_weight, vectors,
    embedding_first, out_table_first, qkv_first, proj_first, up_first, down_first, mod_first,
    vectors_first,
    embedding_second, out_table_second, qkv_second, proj_second, up_second, down_second,
    mod_second, vectors_second,
):
    masters = (
        embedding, out_table, qkv_weight, proj_weight, up_weight, down_weight, mod_weight, vectors,
    )
    firsts = (
        embedding_first, out_table_first, qkv_first, proj_first, up_first, down_first, mod_first,
        vectors_first,
    )
    seconds = (
        embedding_second, out_table_second, qkv_second, proj_second, up_second, down_second,
        mod_second, vectors_second,
    )
    wide = lax.axis_size("wide")
    narrow = lax.axis_size(NARROW)
    me = lax.axis_index("wide")
    group = lax.axis_index(NARROW)
    part = group & 1
    micro = group >> 1
    entries, share = embedding.shape
    width = share * wide
    vocab = entries * narrow
    micro_count, length = token_ids.shape[1:]
    capacity = mask_slots.shape[2]
    rows = length // 2
    pair_total = 5 * length // 16
    quarter = pair_total // 4
    loss_scale = 1.0 / (length * micro_count * wide)
    positions = jnp.arange(length, dtype=jnp.int32)

    tokens, slots, counts = token_ids[0], mask_slots[0], mask_counts[0]
    at_slot = slots[:, :, None] == positions[None, None, :]
    valid = jnp.arange(capacity)[None, :] < counts[:, None]
    masked = jnp.any(at_slot & valid[:, :, None], axis=1)
    targets = jnp.sum(jnp.where(at_slot, tokens[:, None, :], 0), axis=2)
    inputs = jnp.where(masked, vocab - 1, tokens)
    packed = jnp.concatenate(
        [inputs, targets, jnp.broadcast_to(counts[:, None], (micro_count, 128))], axis=1
    )
    packed_all = spread_wide(packed)
    inputs_all = packed_all[:, :, :length]
    targets_all = packed_all[:, :, length : length + capacity]
    counts_all = packed_all[:, :, length + capacity]

    shard_a = jnp.concatenate(
        [qkv_weight[0], qkv_weight[1], qkv_weight[2], proj_weight.T], axis=1
    ).astype(BF)
    wide_a = gather_wide(shard_a, 0)
    wide_bc = gather_wide(jnp.stack([up_weight.astype(BF), down_weight.T.astype(BF)]), 1)
    heads_width = width // narrow

    chunk = -(-entries // (128 * wide)) * 128
    spare = chunk * wide - entries
    table_own = jnp.pad(out_table.astype(BF), ((0, 0), (0, spare)))
    table_own = table_own.reshape(share, wide, chunk).transpose(1, 0, 2)
    real = me * chunk + jnp.arange(chunk) < entries

    moments = counts_all.astype(F32) / pair_total
    condition = jax.nn.silu(time_features(moments, mod_weight.shape[0]))
    condition_mine = lax.dynamic_index_in_dim(condition, micro, 1, keepdims=False)
    mod_part = jnp.dot(condition_mine, rounded(mod_weight), precision=HIGHEST)
    mod_share = mod_part.shape[1]
    exact = []
    rest = mod_part
    for _ in range(3):
        exact.append(rounded(rest))
        rest = rest - exact[-1]
    extra = jnp.concatenate(
        exact + [jnp.broadcast_to(rounded(vectors), (wide, vectors.shape[0]))], axis=1
    ).astype(BF)
    extra_rows = extra.shape[1] // share
    extra = extra.reshape(wide, extra_rows, share)
    extra = jnp.pad(extra, ((0, 0), (0, -extra_rows % 16), (0, 0)))

    table_rows = table_rows_of(embedding.T, xor_narrow(embedding.T.astype(BF), 1))
    inputs_all, table_rows = together(inputs_all, table_rows)
    half_ids = lax.dynamic_slice_in_dim(inputs_all, part * rows, rows, axis=2)
    half_ids = jnp.stack(
        [
            lax.dynamic_index_in_dim(half_ids, micro, 1, keepdims=False),
            lax.dynamic_index_in_dim(half_ids, 1 - micro, 1, keepdims=False),
        ]
    )
    inside, beside = half_ids - group * entries, half_ids - (group ^ 1) * entries
    inside_here = (inside >= 0) & (inside < entries)
    beside_here = (beside >= 0) & (beside < entries)
    places = jnp.where(
        inside_here, inside, jnp.where(beside_here, beside + entries, 2 * entries)
    )
    looked = lookup(table_rows, places.reshape(-1))
    looked = looked.reshape(2, wide, rows, share)
    start_part = looked[0] + xor_narrow(looked[1], 2)
    start_recv_in = jnp.concatenate([start_part, extra], axis=1)
    start_recv_in, wide_a = together(start_recv_in, wide_a)
    full_a = gather_narrow(wide_a)
    start_recv = swap_wide(start_recv_in)

    my_inputs = lax.dynamic_slice_in_dim(
        lax.dynamic_index_in_dim(inputs, micro, 0, keepdims=False), part * rows, rows, axis=0
    )
    small_rows = (9 * width + 3 * width + 8 * width) // wide // share
    padded = rows + 16 + -(-small_rows // 16) * 16
    padded = rows + 16 + 32
    mask_entry = vocab - 1
    ids = jnp.stack(
        [
            lax.dynamic_slice_in_dim(
                lax.dynamic_index_in_dim(inputs_all, (group ^ s) >> 1, 1, keepdims=False),
                ((group ^ s) & 1) * rows,
                rows,
                axis=1,
            )
            for s in range(narrow)
        ]
    )
    ids = jnp.concatenate(
        [
            jnp.where(ids == mask_entry, -1, ids),
            jnp.full((narrow, wide, 1), mask_entry, jnp.int32),
            jnp.full((narrow, wide, padded - rows - 1), -1, jnp.int32),
        ],
        axis=2,
    ).reshape(narrow, wide * padded)
    local_ids = ids - group * entries
    taken = (local_ids >= 0) & (local_ids < entries)
    shift = (wide * padded - 1).bit_length()
    sort_keys = jnp.where(
        taken,
        local_ids * (1 << shift) + jnp.arange(wide * padded, dtype=jnp.int32)[None, :],
        jnp.iinfo(jnp.int32).max,
    )
    hits = jnp.sum(taken.astype(jnp.int32), axis=1)
    start_recv, table_own, wide_bc, *full_a = together(start_recv, table_own, wide_bc, *full_a)
    across_bc = xor_narrow(wide_bc, 2)
    table_mine = swap_wide(table_own).reshape(width, chunk)
    extra = start_recv[:, rows : rows + extra_rows].astype(F32).reshape(wide, -1)
    vector_full = extra[:, 3 * mod_share :].reshape(-1)
    modulation = extra[:, :mod_share] + extra[:, mod_share : 2 * mod_share]
    modulation = (modulation + extra[:, 2 * mod_share : 3 * mod_share]).reshape(-1)
    modulation = modulation + vector_full[4 * width :]
    params = jnp.concatenate(
        [modulation.reshape(8, width), vector_full[: 4 * width].reshape(4, width)]
    )

    my_positions = part * rows + jnp.arange(rows, dtype=jnp.int32)
    far_positions = (1 - part) * rows + jnp.arange(rows, dtype=jnp.int32)
    key_cosine, key_sine = rotary_tables(jnp.concatenate([my_positions, far_positions]), HD)
    cosine, sine = key_cosine[:rows], key_sine[:rows]
    query, own_kv, hidden_one, start = project_qkv(start_recv, params, full_a, cosine, sine)
    query, sort_keys = together(query, sort_keys)
    sort_keys = lax.sort(sort_keys, dimension=1)
    far_kv = xor_narrow(own_kv, 1)
    mixed, logs = attend(query, own_kv, far_kv)
    mixed, sort_keys, hits, across_bc = together(mixed, sort_keys, hits, across_bc)
    full_bc = (wide_bc, xor_narrow(wide_bc, 1), across_bc, xor_narrow(across_bc, 1))
    tables = gather_narrow(table_mine)

    side = me // (wide // 2)
    low = me % (wide // 2)
    count_low = lax.dynamic_index_in_dim(
        lax.dynamic_index_in_dim(counts_all, low, 0, keepdims=False), micro, 0, keepdims=False
    )
    slot_row = lax.dynamic_index_in_dim(slots, micro, 0, keepdims=False)
    offset = jnp.arange(quarter, dtype=jnp.int32)
    order = jnp.concatenate(
        [
            s * (2 * quarter) + p * quarter + offset
            for p in (part, 1 - part)
            for s in (side, 1 - side)
        ]
    )
    from_low = order < count_low
    index = jnp.where(from_low, order, order - count_low)
    mine = from_low == (side == 0)
    wanted = jnp.sum(
        jnp.where(index[:, None] == jnp.arange(capacity)[None, :], slot_row[None, :], 0), axis=1
    )
    select = ((wanted[:, None] == my_positions[None, :]) & mine[:, None]).astype(BF)
    attended, middle, output, hidden_two, inner, picked = feed(
        mixed, start, params, full_a, full_bc, select
    )
    picked = picked[: 2 * quarter] + xor_narrow(picked[2 * quarter :], 1)
    row_part = picked[:quarter] + xor_wide(picked[quarter:], wide // 2)
    head_rows = spread_wide(row_part).reshape(wide * quarter, width)

    targets_mine = lax.dynamic_index_in_dim(targets_all, micro, 1, keepdims=False)
    counts_mine = lax.dynamic_index_in_dim(counts_all, micro, 1, keepdims=False)
    pairs = wide // 2
    both = jnp.concatenate([targets_mine[:pairs], targets_mine[pairs:]], axis=1)
    spot = jnp.stack([s * 2 * quarter + part * quarter + offset for s in (0, 1)])
    low_counts = counts_mine[:pairs, None, None]
    spot = jnp.where(spot[None] < low_counts, spot[None], capacity + spot[None] - low_counts)
    row_targets = jnp.sum(
        jnp.where(
            spot[..., None] == jnp.arange(2 * capacity)[None, None, None, :],
            both[:, None, None, :],
            0,
        ),
        axis=-1,
    )
    row_targets = row_targets.transpose(1, 0, 2).reshape(-1)
    target_owner = sum((row_targets >= k * entries).astype(jnp.int32) for k in range(1, narrow))
    target_rest = row_targets - target_owner * entries - me * chunk
    target_column = jnp.where(
        (target_rest >= 0) & (target_rest < chunk), (target_owner ^ group) * chunk + target_rest, -1
    )

    logits = [jnp.where(real[None, :], mm(head_rows, table, NN), -1e30) for table in tables]
    hitting = [
        jnp.arange(chunk)[None, :] + s * chunk == target_column[:, None] for s in range(narrow)
    ]
    top = functools.reduce(jnp.maximum, [jnp.max(value, axis=-1) for value in logits])
    total = sum(jnp.sum(jnp.exp(value - top[:, None]), axis=-1) for value in logits)
    target_logit = sum(
        jnp.sum(jnp.where(hit, value, 0.0), axis=-1) for hit, value in zip(hitting, logits)
    )
    stats = spread_wide(jnp.stack([top, total, target_logit]))
    top_all = jnp.max(stats[:, 0], axis=0)
    total_all = jnp.sum(stats[:, 1] * jnp.exp(stats[:, 0] - top_all[None]), axis=0)
    log_total = top_all + jnp.log(total_all)
    loss_part = jnp.sum(log_total - jnp.sum(stats[:, 2], axis=0))
    d_logits = [
        ((jnp.exp(value - log_total[:, None]) - hit.astype(F32)) * loss_scale).astype(BF)
        for hit, value in zip(hitting, logits)
    ]
    d_rows = sum(mm(grad, table, NT) for grad, table in zip(d_logits, tables))
    d_table_parts = [mm(head_rows, grad, TN) for grad in d_logits]
    d_recv = swap_wide(d_rows.astype(BF).reshape(wide, quarter, width))
    d_recv, *d_table_parts = together(d_recv, *d_table_parts)
    table_sent = [xor_narrow(d_table_parts[s].astype(BF), 1) for s in (1, 3)]
    d_mine = jnp.sum(d_recv.astype(F32), axis=0).astype(BF)
    d_sides = jnp.concatenate([d_mine, xor_wide(d_mine, wide // 2)])
    d_all = jnp.concatenate([d_sides, xor_narrow(d_sides, 1)])
    table_far = (d_table_parts[2] + table_sent[1].astype(F32)).astype(BF)
    d_all, table_far = together(d_all, table_far)
    half = width // 2
    table_from = [xor_narrow(table_far[:half], 2), xor_narrow(table_far[half:], 2)]

    d_middle, d_attended, d_mixed, bc_sent, bc_own, d_params = feed_back(
        d_all, select, params, middle, output, attended, hidden_two, inner, full_a, full_bc
    )
    d_mixed, table_from[0] = together(d_mixed, table_from[0])
    bc_near, bc_far = scatter_core(bc_sent, bc_own)
    d_query, d_own, d_far = attend_back(
        query, own_kv, far_kv, d_mixed, logs, cosine, sine, key_cosine, key_sine
    )
    d_query, d_own, d_far, table_from[1], bc_far = together(
        d_query, d_own, d_far, table_from[1], bc_far
    )
    b_from, c_from = xor_narrow(bc_far[0], 2), xor_narrow(bc_far[1], 2)
    d_far = xor_narrow(d_far, 1)
    is_mask = (my_inputs == mask_entry).astype(F32)[:, None]
    d_start_rows, d_projected, d_first = qkv_back(
        d_query, d_own, d_far, full_a, d_middle, start, params, is_mask, rows + 16, wide
    )

    d_start_rows, d_first, b_from = together(d_start_rows, d_first, b_from)
    d_params = jnp.concatenate([d_first[:2], d_params[2:8], d_first[2:3], d_params[9:]])
    d_modulation = d_params[:8].reshape(-1)
    d_vector = jnp.concatenate([d_params[8:].reshape(-1), d_modulation])
    small = jnp.concatenate(
        [d_modulation.reshape(wide, -1, share), d_vector.reshape(wide, -1, share)], axis=1
    ).astype(BF)
    small = jnp.pad(small, ((0, 0), (0, padded - rows - 16 - small_rows), (0, 0)))
    d_start_rows = jnp.concatenate([d_start_rows, small], axis=1)
    d_start_recv = swap_wide(d_start_rows)
    a_sent, a_own = qkv_grads(d_projected, hidden_one, d_attended, mixed)
    a_near, a_far = scatter_core(a_sent, a_own)
    a_far, c_from, d_start_recv = together(a_far, c_from, d_start_recv)
    d_b = scatter_wide((bc_near[0] + b_from.astype(F32)).reshape(wide, share, width))
    d_c = scatter_wide((bc_near[1] + c_from.astype(F32)).reshape(wide, share, width))
    d_table = d_table_parts[0] + table_sent[0].astype(F32)
    d_table = (d_table + jnp.concatenate(table_from).astype(F32)).astype(BF)
    d_table = swap_wide(d_table.reshape(wide, share, chunk)).astype(F32).transpose(1, 0, 2)
    d_table = d_table.reshape(share, chunk * wide)[:, :entries]
    a_from = xor_narrow(a_far, 2)
    d_a = scatter_wide((a_near + a_from.astype(F32)).reshape(wide, share, width))
    d_start_recv = d_start_recv.reshape(wide * padded, share)
    d_start_across = xor_narrow(d_start_recv, 2)
    d_near = jnp.stack([d_start_recv, xor_narrow(d_start_recv, 1)])
    d_embed = collect(sort_keys[:2], hits[:2], d_near, shift, None, entries)
    d_far = jnp.stack([d_start_across, xor_narrow(d_start_across, 1)])
    d_embed = collect(sort_keys[2:], hits[2:], d_far, shift, d_embed, entries)

    small = jnp.stack([d_near, d_far]).reshape(2, 2, wide, padded, share)
    small = small[:, :, :, rows + 16 : rows + 16 + small_rows].astype(F32)
    small = small.sum(axis=1).reshape(2, wide, -1)
    small, small_far = small[0], small[1]
    d_vectors = jnp.sum(small[:, mod_share:] + small_far[:, mod_share:], axis=0)
    condition_far = lax.dynamic_index_in_dim(condition, 1 - micro, 1, keepdims=False)
    d_mod_weight = lax.dot_general(
        condition_mine, small[:, :mod_share], TN, precision=HIGHEST
    ) + lax.dot_general(condition_far, small_far[:, :mod_share], TN, precision=HIGHEST)

    shards = (
        d_embed,
        d_table,
        jnp.stack([d_a[:, k * heads_width : (k + 1) * heads_width] for k in range(3)]),
        together(d_a[:, 3 * heads_width :].T)[0],
        d_b,
        d_c,
        d_mod_weight,
        d_vectors,
    )

    square = jnp.zeros((), F32)
    for grad in shards[:6]:
        square = square + jnp.sum(grad * grad)
    shared_square = jnp.sum(shards[6] * shards[6]) + jnp.sum(shards[7] * shards[7])
    square = square + shared_square / narrow
    sums = lax.all_to_all(
        jnp.broadcast_to(jnp.stack([loss_part / wide, square])[None, None], (wide * narrow, 1, 2)),
        ("wide",) + NARROW,
        0,
        0,
        tiled=True,
    )
    sums = jnp.sum(sums, axis=(0, 1))
    loss_sum = sums[0]
    grad_norm = jnp.sqrt(sums[1])
    factor = CLIP_NORM / jnp.maximum(grad_norm, CLIP_NORM)
    results = []
    for member in range(8):
        turn = (lambda value: value.T) if member in (0, 5) else (lambda value: value)
        master = turn(masters[member])
        grad = shards[member] * factor
        first = BETA_ONE * turn(firsts[member]) + (1.0 - BETA_ONE) * grad
        second = BETA_TWO * turn(seconds[member]) + (1.0 - BETA_TWO) * grad * grad
        stepped = (
            first / (1.0 - BETA_ONE**STEP) / (jnp.sqrt(second / (1.0 - BETA_TWO**STEP)) + ADAM_EPS)
        )
        decay = WEIGHT_DECAY if member < 7 else 0.0
        fresh = master - LEARN_RATES[member] * (stepped + decay * master)
        results.extend([turn(fresh), turn(first), turn(second)])
    return (loss_sum, grad_norm, *results)


def solution(mesh):
    shape = (mesh.shape["wide"], mesh.shape["narrow"] // 2, 2)
    mesh = jax.sharding.Mesh(mesh.devices.reshape(shape), ("wide",) + NARROW)
    weights = (
        P(NARROW, "wide"),
        P("wide", NARROW),
        P(None, "wide", NARROW),
        P(NARROW, "wide"),
        P("wide", NARROW),
        P(NARROW, "wide"),
        P(None, "wide"),
        P("wide"),
    )
    data = (P("wide", None, None), P("wide", None, None), P("wide", None))
    outs = [P(), P()]
    for spec in weights:
        outs.extend([spec] * 3)
    return jax.shard_map(
        local,
        mesh=mesh,
        in_specs=data + weights * 3,
        out_specs=tuple(outs),
        check_vma=False,
    )
```

```python
import functools
import math

import jax
import jax.numpy as jnp
from jax import lax
from jax.experimental import pallas as pl
from jax.experimental.pallas import tpu as pltpu
from jax.sharding import PartitionSpec as P

HD = 64
STEP = 10

HIGHEST = lax.Precision.HIGHEST
NORM_EPS = 1e-06
CLIP_NORM = 0.005
BETA_ONE = 0.9
BETA_TWO = 0.95
ADAM_EPS = 1e-08
WEIGHT_DECAY = 0.1
LEARN_RATES = (1.0, 0.1, 0.07, 0.5, 0.07, 0.04, 0.2, 0.5)
NARROW = ("line", "core")
BF = jnp.bfloat16
F32 = jnp.float32
VMEM_LIMIT = 56 * 1024 * 1024
FREE = pl.CostEstimate(flops=0, bytes_accessed=0, transcendentals=0)


def together(*values):
    return lax.optimization_barrier(values)


def xor_narrow(value, bits):
    return lax.ppermute(
        value, NARROW, [(i, i ^ bits) for i in range(lax.axis_size(NARROW))]
    )


def xor_wide(value, bits):
    return lax.ppermute(value, "wide", [(i, i ^ bits) for i in range(lax.axis_size("wide"))])


def swap_wide(value):
    return lax.all_to_all(value, "wide", 0, 0, tiled=True)


def spread_wide(value):
    if lax.axis_size("wide") > 8:
        return lax.all_gather(value, "wide")
    return swap_wide(jnp.broadcast_to(value[None], (lax.axis_size("wide"),) + value.shape))


def gather_wide(value, axis):
    return lax.all_gather(value, "wide", axis=axis, tiled=True)


def scatter_pair(value):
    count = lax.axis_size("wide")
    if count != 8:
        return value
    side = lax.axis_index("wide") & 1
    pairs = value.reshape((4, 2) + value.shape[1:])
    kept = lax.dynamic_index_in_dim(pairs, side, 1, keepdims=False)
    sent = lax.dynamic_index_in_dim(pairs, 1 - side, 1, keepdims=False).astype(BF)
    return kept + xor_wide(sent, 1).astype(F32)


def scatter_line(half):
    if lax.axis_size("wide") != 8:
        return lax.psum_scatter(half, "wide", scatter_dimension=0)
    depth = lax.axis_index("wide") >> 1
    total = lax.dynamic_index_in_dim(half, depth, 0, keepdims=False)
    low = half.astype(BF)
    for k in (1, 2, 3):
        piece = lax.dynamic_index_in_dim(low, depth ^ k, 0, keepdims=False)
        total = total + xor_wide(piece, 2 * k).astype(F32)
    return total


def scatter_core(sent, own):
    from_core = xor_narrow(sent, 1).astype(F32)
    near = own[0].astype(F32) + from_core[0]
    far = own[1].astype(F32) + from_core[1]
    return near, far.astype(BF)


def gather_narrow(value):
    across = xor_narrow(value, 2)
    beside = xor_narrow(value, 1)
    corner = xor_narrow(across, 1)
    return value, beside, across, corner


def rounded(value):
    return lax.reduce_precision(value, exponent_bits=8, mantissa_bits=7)


def layer_norm(values):
    centered = values - jnp.mean(values, axis=-1, keepdims=True)
    inverse = lax.rsqrt(jnp.mean(centered * centered, axis=-1, keepdims=True) + NORM_EPS)
    return (centered * inverse, inverse)


def norm_back(grad, normed, inverse):
    return inverse * (
        grad
        - jnp.mean(grad, axis=-1, keepdims=True)
        - normed * jnp.mean(grad * normed, axis=-1, keepdims=True)
    )


def gelu_tanh(values):
    inner = 0.7978845608 * (values + 0.044715 * values * values * values)
    return 0.5 * values * (1.0 + jnp.tanh(inner))


def gelu_slope(values):
    tangent = jnp.tanh(0.7978845608 * (values + 0.044715 * values * values * values))
    return 0.5 * (1.0 + tangent) + 0.5 * values * (1.0 - tangent * tangent) * 0.7978845608 * (
        1.0 + 0.134145 * values * values
    )


def rotary_tables(positions, width):
    freqs = jnp.exp(jnp.arange(width // 2, dtype=F32) * (-2.0 * math.log(10000.0) / width))
    angle = positions.astype(F32)[:, None] * freqs[None, :]
    cosine, sine = jnp.cos(angle), jnp.sin(angle)
    return (
        jnp.concatenate([cosine] * 4, axis=1),
        jnp.concatenate([-sine, sine, -sine, sine], axis=1),
    )


def time_features(moment, width):
    freqs = jnp.exp(jnp.arange(width // 2, dtype=F32) * (-math.log(10000.0) / (width // 2)))
    angle = 1000.0 * moment[..., None] * freqs
    return jnp.concatenate([jnp.cos(angle), jnp.sin(angle)], axis=-1)


def turned(values, cosine, sine):
    blocks = []
    for place in range(0, values.shape[1], 2 * HD):
        block = values[:, place : place + 2 * HD]
        lanes = lax.broadcasted_iota(jnp.int32, block.shape, 1)
        ahead = pltpu.roll(block, 2 * HD - HD // 2, 1)
        behind = pltpu.roll(block, HD // 2, 1)
        other = jnp.where((lanes & (HD - 1)) < HD // 2, ahead, behind)
        blocks.append(block * cosine + other * sine)
    return jnp.concatenate(blocks, axis=1) if len(blocks) > 1 else blocks[0]


def turned_back(values, cosine, sine):
    spare = -values.shape[1] % (2 * HD)
    filled = jnp.concatenate([values, jnp.zeros((values.shape[0], spare), F32)], axis=1)
    return turned(filled, cosine, -sine)[:, : values.shape[1]]


NT = (((1,), (1,)), ((), ()))
NN = (((1,), (0,)), ((), ()))
TN = (((0,), (0,)), ((), ()))


def mm(a, b, dims):
    return lax.dot_general(a, b, dims, preferred_element_type=F32)


SHIFT_ONE, SCALE_ONE, GATE_ONE, SHIFT_TWO, SCALE_TWO, GATE_TWO, SHIFT_LAST, SCALE_LAST = range(8)
GAIN_ONE, GAIN_TWO, GAIN_LAST, BIAS_DOWN = range(8, 12)
LOCAL = dict(
    compiler_params=pltpu.CompilerParams(vmem_limit_bytes=60 * 1024 * 1024), cost_estimate=FREE
)
BUSY = dict(LOCAL, cost_estimate=pl.CostEstimate(10**10, 0, 4 * 10**7))


def column_sum(values):
    return jnp.sum(values, axis=0, keepdims=True)


def qkv_kernel(
    recv_ref, par_ref, a0, a1, a2, a3, cos_ref, sin_ref, q_ref, kv_ref, hidden_ref, start_ref
):
    par = lambda k: par_ref[k : k + 1, :]
    rows = start_ref.shape[0]
    start = jnp.concatenate(
        [recv_ref[piece, :rows, :].astype(F32) for piece in range(recv_ref.shape[0])], axis=1
    )
    start_ref[...] = start
    normed, _ = layer_norm(start)
    hidden = normed * par(GAIN_ONE) * (1.0 + par(SCALE_ONE)) + par(SHIFT_ONE)
    hidden = hidden.astype(BF)
    hidden_ref[...] = hidden
    share = q_ref.shape[2]
    for s, weight in enumerate((a0, a1, a2, a3)):
        value = mm(hidden, weight[...], NN)
        pair = turned(value[:, : 2 * share], cos_ref[...], sin_ref[...])
        q_ref[s] = pair[:, :share].astype(BF)
        kv_ref[s] = jnp.concatenate(
            [pair[:, share:], value[:, 2 * share : 3 * share]], axis=1
        ).astype(BF)


def project_qkv(recv, params, weights, cosine, sine):
    rows, width = cosine.shape[0], params.shape[1]
    share = width // 4
    return pl.pallas_call(
        qkv_kernel,
        out_shape=[
            jax.ShapeDtypeStruct((4, rows, share), BF),
            jax.ShapeDtypeStruct((4, rows, 2 * share), BF),
            jax.ShapeDtypeStruct((rows, width), BF),
            jax.ShapeDtypeStruct((rows, width), F32),
        ],
        name="qkv",
        **LOCAL,
    )(recv, params, *weights, cosine, sine)


def head_mask(values, head):
    lanes = lax.broadcasted_iota(jnp.int32, values.shape, 1)
    inside = (lanes >= head * HD) & (lanes < (head + 1) * HD)
    return jnp.where(inside, values, jnp.zeros_like(values))


def attend_kernel(q_ref, own_ref, far_ref, out_ref, log_ref):
    query = q_ref[0] * BF(HD**-0.5)
    share = query.shape[1]
    both = jnp.concatenate([own_ref[0], far_ref[0]], axis=0)
    keys, values = both[:, :share], both[:, share:].T
    parts = []
    for head in range(query.shape[1] // HD):
        scores = mm(keys, head_mask(query, head), NT)
        top = jnp.max(scores, axis=0, keepdims=True)
        shifted = jnp.exp(scores - top)
        total = jnp.sum(shifted, axis=0, keepdims=True)
        weights = (shifted * (1.0 / total)).astype(BF)
        parts.append(mm(values[head * HD : (head + 1) * HD], weights, NN))
        log_ref[0, head : head + 1, :] = top + jnp.log(total)
    out_ref[0] = jnp.concatenate(parts, axis=0).T.astype(BF)


def attend_specs(rows, share):
    return [
        pl.BlockSpec((1, rows, share), lambda s: (s, 0, 0)),
        pl.BlockSpec((1, rows, 2 * share), lambda s: (s, 0, 0)),
        pl.BlockSpec((1, rows, 2 * share), lambda s: (s ^ 1, 0, 0)),
    ]


def attend(query, own, far):
    slots, rows, share = query.shape
    heads = share // HD
    return pl.pallas_call(
        attend_kernel,
        grid=(slots,),
        in_specs=attend_specs(rows, share),
        out_specs=[
            pl.BlockSpec((1, rows, share), lambda s: (s, 0, 0)),
            pl.BlockSpec((1, heads, rows), lambda s: (s, 0, 0)),
        ],
        out_shape=[
            jax.ShapeDtypeStruct((slots, rows, share), BF),
            jax.ShapeDtypeStruct((slots, heads, rows), F32),
        ],
        name="attend",
        **LOCAL,
    )(query, own, far)


def feed_kernel(
    mixed_ref, start_ref, par_ref, a0, a1, a2, a3, bc0, bc1, bc2, bc3, select_ref,
    attended_ref, middle_ref, output_ref, hidden_ref, inner_ref, picked_ref,
):
    par = lambda k: par_ref[k : k + 1, :]
    share = mixed_ref.shape[2]
    attended = sum(
        mm(mixed_ref[s], weight[:, 3 * share :], NT) for s, weight in enumerate((a0, a1, a2, a3))
    )
    attended_ref[...] = attended
    middle = start_ref[...] + par(GATE_ONE) * attended
    middle_ref[...] = middle
    normed, _ = layer_norm(middle)
    hidden = normed * par(GAIN_TWO) * (1.0 + par(SCALE_TWO)) + par(SHIFT_TWO)
    hidden = hidden.astype(BF)
    hidden_ref[...] = hidden
    output = jnp.zeros(middle.shape, F32)
    for s, weight in enumerate((bc0, bc1, bc2, bc3)):
        inner = mm(hidden, weight[0], NN)
        inner_ref[s] = inner
        output = output + mm(gelu_tanh(inner).astype(BF), weight[1], NT)
    output_ref[...] = output
    final = middle + par(GATE_TWO) * (output + par(BIAS_DOWN))
    normed, _ = layer_norm(final)
    last = normed * (par(GAIN_LAST) * (1.0 + par(SCALE_LAST))) + par(SHIFT_LAST)
    picked_ref[...] = mm(select_ref[...], last.astype(BF), NN).astype(BF)


def feed(mixed, start, params, weights_a, weights_bc, select):
    rows, width = start.shape
    plain = jax.ShapeDtypeStruct((rows, width), F32)
    return pl.pallas_call(
        feed_kernel,
        out_shape=[
            plain,
            plain,
            plain,
            jax.ShapeDtypeStruct((rows, width), BF),
            jax.ShapeDtypeStruct((4, rows, width), F32),
            jax.ShapeDtypeStruct((select.shape[0], width), BF),
        ],
        name="feed",
        **LOCAL,
    )(mixed, start, params, *weights_a, *weights_bc, select)


SLOT_PLACES = ((1, 0, 0), (3, 0, 1), (0, 1, 0), (2, 1, 1))


def feed_back_kernel(
    rows_ref, select_ref, par_ref, middle_ref, output_ref, attended_ref, hidden_ref, inner_ref,
    a0, a1, a2, a3, bc0, bc1, bc2, bc3,
    d_middle_ref, d_attended_ref, d_mixed_ref, b_sent_ref, c_sent_ref, b_own_ref, c_own_ref,
    vec_ref,
):
    par = lambda k: par_ref[k : k + 1, :]
    share = d_mixed_ref.shape[2]
    middle, output = middle_ref[...], output_ref[...]
    d_hidden = mm(select_ref[...], rows_ref[...], TN)
    final = middle + par(GATE_TWO) * (output + par(BIAS_DOWN))
    normed, inverse = layer_norm(final)
    d_normed = column_sum(d_hidden * normed)
    vec_ref[SHIFT_LAST : SHIFT_LAST + 1, :] = column_sum(d_hidden)
    vec_ref[SCALE_LAST : SCALE_LAST + 1, :] = d_normed * par(GAIN_LAST)
    vec_ref[GAIN_LAST : GAIN_LAST + 1, :] = d_normed * (1.0 + par(SCALE_LAST))
    d_final = norm_back(d_hidden * (par(GAIN_LAST) * (1.0 + par(SCALE_LAST))), normed, inverse)
    vec_ref[BIAS_DOWN : BIAS_DOWN + 1, :] = column_sum(d_final) * par(GATE_TWO)
    vec_ref[GATE_TWO : GATE_TWO + 1, :] = column_sum(d_final * (output + par(BIAS_DOWN)))
    d_output = (d_final * par(GATE_TWO)).astype(BF)
    hidden = hidden_ref[...]
    d_hidden = jnp.zeros(middle.shape, F32)
    weights = (bc0, bc1, bc2, bc3)
    for s, kept, place in SLOT_PLACES:
        b_ref, c_ref = (b_own_ref, c_own_ref) if kept else (b_sent_ref, c_sent_ref)
        inner = inner_ref[s]
        tangent = jnp.tanh(0.7978845608 * (inner + 0.044715 * inner * inner * inner))
        active = (0.5 * inner * (1.0 + tangent)).astype(BF)
        slope = 0.5 * (1.0 + tangent) + 0.5 * inner * (
            1.0 - tangent * tangent
        ) * 0.7978845608 * (1.0 + 0.134145 * inner * inner)
        d_inner = (mm(d_output, weights[s][1], NN) * slope).astype(BF)
        b_ref[place] = mm(hidden, d_inner, TN).astype(BF)
        c_ref[place] = mm(d_output, active, TN).astype(BF)
        d_hidden = d_hidden + mm(d_inner, weights[s][0], NT)
    normed, inverse = layer_norm(middle)
    d_normed = column_sum(d_hidden * normed)
    vec_ref[SHIFT_TWO : SHIFT_TWO + 1, :] = column_sum(d_hidden)
    vec_ref[SCALE_TWO : SCALE_TWO + 1, :] = d_normed * par(GAIN_TWO)
    vec_ref[GAIN_TWO : GAIN_TWO + 1, :] = d_normed * (1.0 + par(SCALE_TWO))
    d_middle = d_final + norm_back(
        d_hidden * par(GAIN_TWO) * (1.0 + par(SCALE_TWO)), normed, inverse
    )
    d_middle_ref[...] = d_middle
    vec_ref[GATE_ONE : GATE_ONE + 1, :] = column_sum(d_middle * attended_ref[...])
    d_attended = (d_middle * par(GATE_ONE)).astype(BF)
    d_attended_ref[...] = d_attended
    for s, weight in enumerate((a0, a1, a2, a3)):
        d_mixed_ref[s] = mm(d_attended, weight[:, 3 * share :], NN).astype(BF)
    for unused in (SHIFT_ONE, SCALE_ONE, GAIN_ONE):
        vec_ref[unused : unused + 1, :] = jnp.zeros_like(par(0))


def feed_back(
    d_rows, select, params, middle, output, attended, hidden, inner, weights_a, weights_bc
):
    rows, width = middle.shape
    half = jax.ShapeDtypeStruct((2, width, width), BF)
    return pl.pallas_call(
        feed_back_kernel,
        out_shape=[
            jax.ShapeDtypeStruct((rows, width), F32),
            jax.ShapeDtypeStruct((rows, width), BF),
            jax.ShapeDtypeStruct((4, rows, width // 4), BF),
            half,
            half,
            half,
            half,
            jax.ShapeDtypeStruct(params.shape, F32),
        ],
        name="feed_back",
        **BUSY,
    )(
        d_rows, select, params, middle, output, attended, hidden, inner, *weights_a, *weights_bc
    )


def attend_back_kernel(
    q_ref, own_ref, far_ref, grad_ref, log_ref, cos_ref, sin_ref, kcos_ref, ksin_ref,
    dq_ref, d_own_ref, d_far_ref,
):
    query, grad = q_ref[0], grad_ref[0]
    share = query.shape[1]
    both = jnp.concatenate([own_ref[0], far_ref[0]], axis=0)
    keys, values = both[:, :share], both[:, share:]
    turned_keys = keys.T
    scale = HD**-0.5
    rows = query.shape[0]
    dq = []
    dk = jnp.zeros(keys.shape, F32)
    dv = jnp.zeros(keys.shape, F32)
    for head in range(query.shape[1] // HD):
        query_one = head_mask(query * BF(scale), head)
        grad_one = head_mask(grad, head)
        scores = mm(keys, query_one, NT)
        weights = jnp.exp(scores - log_ref[0, head : head + 1, :])
        d_weights = mm(values, grad_one, NT)
        delta = jnp.sum(weights * d_weights, axis=0, keepdims=True)
        d_scores = (weights * (d_weights - delta)).astype(BF)
        dq.append(mm(turned_keys[head * HD : (head + 1) * HD], d_scores, NN))
        dk = dk + mm(d_scores, query_one, NN)
        dv = dv + mm(weights.astype(BF), grad_one, NN)
    dq = jnp.concatenate(dq, axis=0).T * scale
    dq_ref[0] = turned_back(dq, cos_ref[...], sin_ref[...]).astype(BF)
    dk = turned_back(dk, kcos_ref[...], ksin_ref[...])
    both = jnp.concatenate([dk, dv], axis=1)
    d_own_ref[0] = both[:rows]
    d_far_ref[0] = both[rows:].astype(BF)


def attend_back(query, own, far, grad, logs, cosine, sine, key_cosine, key_sine):
    slots, rows, share = query.shape
    heads = share // HD
    whole = lambda table: pl.BlockSpec(table.shape, lambda s: (0, 0))
    one, two, other = attend_specs(rows, share)
    return pl.pallas_call(
        attend_back_kernel,
        grid=(slots,),
        in_specs=[
            one, two, other, one, pl.BlockSpec((1, heads, rows), lambda s: (s, 0, 0)),
            whole(cosine), whole(sine), whole(key_cosine), whole(key_sine),
        ],
        out_specs=[one, two, two],
        out_shape=[
            jax.ShapeDtypeStruct((slots, rows, share), BF),
            jax.ShapeDtypeStruct((slots, rows, 2 * share), F32),
            jax.ShapeDtypeStruct((slots, rows, 2 * share), BF),
        ],
        name="attend_back",
        **LOCAL,
    )(query, own, far, grad, logs, cosine, sine, key_cosine, key_sine)


def slot_grads(dq_ref, d_own_ref, d_far_ref, s):
    return jnp.concatenate(
        [
            dq_ref[s],
            (d_own_ref[s] + d_far_ref[s ^ 1].astype(F32)).astype(BF),
        ],
        axis=1,
    )


def qkv_back_kernel(
    dq_ref, d_own_ref, d_far_ref, a0, a1, a2, a3, d_middle_ref, start_ref, par_ref, mask_ref,
    out_ref, grads_ref, vec_ref,
):
    par = lambda k: par_ref[k : k + 1, :]
    share = dq_ref.shape[2]
    rows = start_ref.shape[0]
    d_hidden = jnp.zeros(start_ref.shape, F32)
    for s, weight in enumerate((a0, a1, a2, a3)):
        grads = slot_grads(dq_ref, d_own_ref, d_far_ref, s)
        grads_ref[s] = grads
        d_hidden = d_hidden + mm(grads, weight[:, : 3 * share], NT)
    normed, inverse = layer_norm(start_ref[...])
    d_normed = column_sum(d_hidden * normed)
    vec_ref[0:1, :] = column_sum(d_hidden)
    vec_ref[1:2, :] = d_normed * par(GAIN_ONE)
    vec_ref[2:3, :] = d_normed * (1.0 + par(SCALE_ONE))
    d_start = d_middle_ref[...] + norm_back(
        d_hidden * par(GAIN_ONE) * (1.0 + par(SCALE_ONE)), normed, inverse
    )
    masked = column_sum(d_start * mask_ref[...])
    extra = out_ref.shape[1] - rows
    first = lax.broadcasted_iota(jnp.int32, (extra, 1), 0) == 0
    whole = jnp.concatenate([d_start, jnp.where(first, masked, 0.0)], axis=0).astype(BF)
    columns = out_ref.shape[2]
    for piece in range(out_ref.shape[0]):
        out_ref[piece] = whole[:, piece * columns : (piece + 1) * columns]


def qkv_back(dq, d_own, d_far, weights, d_middle, start, params, is_mask, padded, wide):
    rows, width = start.shape
    return pl.pallas_call(
        qkv_back_kernel,
        out_shape=[
            jax.ShapeDtypeStruct((wide, padded, width // wide), BF),
            jax.ShapeDtypeStruct((4, rows, 3 * width // 4), BF),
            jax.ShapeDtypeStruct((3, width), F32),
        ],
        name="qkv_back",
        **LOCAL,
    )(dq, d_own, d_far, *weights, d_middle, start, params, is_mask)


def flip(value):
    def kernel(value_ref, out_ref):
        out_ref[...] = value_ref[...].T

    return pl.pallas_call(
        kernel, out_shape=jax.ShapeDtypeStruct(value.shape[::-1], value.dtype), name="flip", **LOCAL
    )(value)


def qkv_grads_kernel(grads_ref, hidden_ref, d_attended_ref, mixed_ref, sent_ref, own_ref):
    for s, kept, place in SLOT_PLACES:
        out_ref = own_ref if kept else sent_ref
        out_ref[place] = jnp.concatenate(
            [
                mm(hidden_ref[...], grads_ref[s], TN),
                mm(d_attended_ref[...], mixed_ref[s], TN),
            ],
            axis=1,
        ).astype(BF)


def qkv_grads(grads, hidden, d_attended, mixed):
    width = hidden.shape[1]
    half = jax.ShapeDtypeStruct((2, width, width), BF)
    return pl.pallas_call(
        qkv_grads_kernel, out_shape=[half, half], name="qkv_grads", **BUSY
    )(grads, hidden, d_attended, mixed)


def rows_kernel(own_ref, other_ref, out_ref):
    step = pl.program_id(0)
    half = pl.num_programs(0) // 2

    @pl.when(step < half)
    def _():
        out_ref[...] = own_ref[...].astype(BF).T.astype(F32)

    @pl.when((step >= half) & (step < 2 * half))
    def _():
        out_ref[...] = other_ref[...].T.astype(F32)

    @pl.when(step == 2 * half)
    def _():
        out_ref[...] = jnp.zeros_like(out_ref)


def table_rows_of(own, other):
    width, entries = own.shape
    block = next(b for b in (1408, 1152, 384, 128) if entries % b == 0)
    half = entries // block
    return pl.pallas_call(
        rows_kernel,
        grid=(2 * half + 1,),
        in_specs=[
            pl.BlockSpec((width, block), lambda i: (0, jnp.minimum(i, half - 1))),
            pl.BlockSpec((width, block), lambda i: (0, jnp.clip(i - half, 0, half - 1))),
        ],
        out_specs=pl.BlockSpec((block, width), lambda i: (i, 0)),
        out_shape=jax.ShapeDtypeStruct((2 * entries + block, width), F32),
        name="table_rows",
        **BUSY,
    )(own, other)


def lookup_kernel(id_ref, table_ref, out_ref, scratch):
    block = scratch.shape[0]
    unroll = 16

    def body(step, _):
        for k in range(unroll):
            place = step * unroll + k
            scratch[pl.ds(place, 1), :] = table_ref[pl.ds(id_ref[0, 0, place], 1), :]
        return 0

    lax.fori_loop(0, block // unroll, body, 0)
    out_ref[...] = scratch[...].astype(BF)


def lookup(table, ids):
    count = ids.shape[0]
    block = min(2048, count)
    width = table.shape[1]
    return pl.pallas_call(
        lookup_kernel,
        grid=(count // block,),
        in_specs=[
            pl.BlockSpec((1, 1, block), lambda i: (i, 0, 0), memory_space=pltpu.SMEM),
            pl.BlockSpec(table.shape, lambda i: (0, 0), pipeline_mode=pl.Buffered(1)),
        ],
        out_specs=pl.BlockSpec((block, width), lambda i: (i, 0)),
        out_shape=jax.ShapeDtypeStruct((count, width), BF),
        scratch_shapes=[pltpu.VMEM((block, width), F32)],
        name="lookup",
        **LOCAL,
    )(ids.reshape(count // block, 1, block), table)


def collect_kernel(shift, first, key_ref, count_ref, one_ref, two_ref, *refs):
    if first:
        out_ref, rows_ref = refs
        sum_ref = out_ref
        sum_ref[...] = jnp.zeros_like(sum_ref)
    else:
        old_ref, out_ref, rows_ref, sum_ref = refs
        sum_ref[...] = old_ref[...]
    mask = (1 << shift) - 1
    unroll = 8
    for part, grad_ref in enumerate((one_ref, two_ref)):
        rows_ref[...] = grad_ref[...].astype(F32)
        count = count_ref[part]

        def group(item, _, part=part):
            keys = [key_ref[part, item * unroll + k] for k in range(unroll)]
            targets = [lax.shift_right_logical(key, shift) for key in keys]
            olds = [sum_ref[pl.ds(target, 1), :] for target in targets]
            news = [rows_ref[pl.ds(key & mask, 1), :] for key in keys]
            sums = []
            for k in range(unroll):
                old = olds[k]
                if k:
                    old = jnp.where(targets[k] == targets[k - 1], sums[k - 1], old)
                sums.append(old + news[k])
            for k in range(unroll):
                sum_ref[pl.ds(targets[k], 1), :] = sums[k]
            return 0

        def single(item, _, part=part):
            key = key_ref[part, item]
            target = pl.ds(lax.shift_right_logical(key, shift), 1)
            sum_ref[target, :] = sum_ref[target, :] + rows_ref[pl.ds(key & mask, 1), :]
            return 0

        groups = lax.shift_right_logical(count, 3)
        lax.fori_loop(0, groups, group, 0)
        lax.fori_loop(groups * unroll, count, single, 0)

    if not first:

        def turn(block, _):
            place = pl.ds(pl.multiple_of(block * 128, 128), 128)
            out_ref[:, place] = sum_ref[place, :].T
            return 0

        lax.fori_loop(0, sum_ref.shape[0] // 128, turn, 0)


def collect(keys, counts, grads, shift, before, entries):
    tokens, width = grads[0].shape
    first = before is None
    out_dims = (entries, width) if first else (width, entries)
    scratch = [pltpu.VMEM((tokens, width), F32)]
    if not first:
        scratch.append(pltpu.VMEM((entries, width), F32))
    smem = pl.BlockSpec(memory_space=pltpu.SMEM)
    vmem = pl.BlockSpec(memory_space=pltpu.VMEM)
    return pl.pallas_call(
        functools.partial(collect_kernel, shift, first),
        in_specs=[smem, smem] + [vmem] * (2 if first else 3),
        out_specs=vmem,
        out_shape=jax.ShapeDtypeStruct(out_dims, F32),
        scratch_shapes=scratch,
        name="collect",
        **LOCAL,
    )(keys, counts, *grads, *([] if first else [before]))


def local(
    token_ids, mask_slots, mask_counts,
    embedding, out_table, qkv_weight, proj_weight, up_weight, down_weight, mod_weight, vectors,
    embedding_first, out_table_first, qkv_first, proj_first, up_first, down_first, mod_first,
    vectors_first,
    embedding_second, out_table_second, qkv_second, proj_second, up_second, down_second,
    mod_second, vectors_second,
):
    masters = (
        embedding, out_table, qkv_weight, proj_weight, up_weight, down_weight, mod_weight, vectors,
    )
    firsts = (
        embedding_first, out_table_first, qkv_first, proj_first, up_first, down_first, mod_first,
        vectors_first,
    )
    seconds = (
        embedding_second, out_table_second, qkv_second, proj_second, up_second, down_second,
        mod_second, vectors_second,
    )
    wide = lax.axis_size("wide")
    narrow = lax.axis_size(NARROW)
    me = lax.axis_index("wide")
    group = lax.axis_index(NARROW)
    part = group & 1
    micro = group >> 1
    entries, share = embedding.shape
    width = share * wide
    vocab = entries * narrow
    micro_count, length = token_ids.shape[1:]
    capacity = mask_slots.shape[2]
    rows = length // 2
    pair_total = 5 * length // 16
    quarter = pair_total // 4
    loss_scale = 1.0 / (length * micro_count * wide)
    positions = jnp.arange(length, dtype=jnp.int32)

    tokens, slots, counts = token_ids[0], mask_slots[0], mask_counts[0]
    at_slot = slots[:, :, None] == positions[None, None, :]
    valid = jnp.arange(capacity)[None, :] < counts[:, None]
    masked = jnp.any(at_slot & valid[:, :, None], axis=1)
    targets = jnp.sum(jnp.where(at_slot, tokens[:, None, :], 0), axis=2)
    inputs = jnp.where(masked, vocab - 1, tokens)
    packed = jnp.concatenate(
        [inputs, targets, jnp.broadcast_to(counts[:, None], (micro_count, 128))], axis=1
    )
    packed_all = spread_wide(packed)
    inputs_all = packed_all[:, :, :length]
    targets_all = packed_all[:, :, length : length + capacity]
    counts_all = packed_all[:, :, length + capacity]

    shard_a = jnp.concatenate(
        [qkv_weight[0], qkv_weight[1], qkv_weight[2], proj_weight.T], axis=1
    ).astype(BF)
    wide_all = gather_wide(
        jnp.stack([shard_a, up_weight.astype(BF), down_weight.T.astype(BF)]), 1
    )
    wide_a, wide_bc = wide_all[0], wide_all[1:]
    heads_width = width // narrow

    chunk = -(-entries // (128 * wide)) * 128
    spare = chunk * wide - entries
    table_own = jnp.pad(out_table.astype(BF), ((0, 0), (0, spare)))
    table_own = table_own.reshape(share, wide, chunk).transpose(1, 0, 2)
    cuts = [(0, chunk)]
    table_own = [table_own[:, :, low:high] for low, high in cuts]

    moments = counts_all.astype(F32) / pair_total
    condition = jax.nn.silu(time_features(moments, mod_weight.shape[0]))
    condition_mine = lax.dynamic_index_in_dim(condition, micro, 1, keepdims=False)
    mod_part = jnp.dot(condition_mine, rounded(mod_weight), precision=HIGHEST)
    mod_share = mod_part.shape[1]
    exact = []
    rest = mod_part
    for _ in range(3):
        exact.append(rounded(rest))
        rest = rest - exact[-1]
    extra = jnp.concatenate(
        exact + [jnp.broadcast_to(rounded(vectors), (wide, vectors.shape[0]))], axis=1
    ).astype(BF)
    extra_rows = extra.shape[1] // share
    extra = extra.reshape(wide, extra_rows, share)
    extra = jnp.pad(extra, ((0, 0), (0, -extra_rows % 16), (0, 0)))

    table_rows = table_rows_of(embedding.T, xor_narrow(embedding.T.astype(BF), 1))
    half_ids = lax.dynamic_slice_in_dim(inputs_all, part * rows, rows, axis=2)
    half_ids = jnp.stack(
        [
            lax.dynamic_index_in_dim(half_ids, micro, 1, keepdims=False),
            lax.dynamic_index_in_dim(half_ids, 1 - micro, 1, keepdims=False),
        ]
    )
    inside, beside = half_ids - group * entries, half_ids - (group ^ 1) * entries
    inside_here = (inside >= 0) & (inside < entries)
    beside_here = (beside >= 0) & (beside < entries)
    places = jnp.where(
        inside_here, inside, jnp.where(beside_here, beside + entries, 2 * entries)
    )
    looked = lookup(table_rows, places.reshape(-1))
    looked = looked.reshape(2, wide, rows, share)
    start_part = looked[0] + xor_narrow(looked[1], 2)
    start_recv_in = jnp.concatenate([start_part, extra], axis=1)
    start_recv_in, wide_a = together(start_recv_in, wide_a)
    full_a = gather_narrow(wide_a)
    start_recv = swap_wide(start_recv_in)

    my_inputs = lax.dynamic_slice_in_dim(
        lax.dynamic_index_in_dim(inputs, micro, 0, keepdims=False), part * rows, rows, axis=0
    )
    small_rows = (9 * width + 3 * width + 8 * width) // wide // share
    padded = rows + 16 + -(-small_rows // 16) * 16
    padded = rows + 16 + 32
    mask_entry = vocab - 1
    ids = jnp.stack(
        [
            lax.dynamic_slice_in_dim(
                lax.dynamic_index_in_dim(inputs_all, (group ^ s) >> 1, 1, keepdims=False),
                ((group ^ s) & 1) * rows,
                rows,
                axis=1,
            )
            for s in range(narrow)
        ]
    )
    ids = jnp.concatenate(
        [
            jnp.where(ids == mask_entry, -1, ids),
            jnp.full((narrow, wide, 1), mask_entry, jnp.int32),
            jnp.full((narrow, wide, padded - rows - 1), -1, jnp.int32),
        ],
        axis=2,
    ).reshape(narrow, wide * padded)
    local_ids = ids - group * entries
    taken = (local_ids >= 0) & (local_ids < entries)
    shift = (wide * padded - 1).bit_length()
    sort_keys = jnp.where(
        taken,
        local_ids * (1 << shift) + jnp.arange(wide * padded, dtype=jnp.int32)[None, :],
        jnp.iinfo(jnp.int32).max,
    )
    hits = jnp.sum(taken.astype(jnp.int32), axis=1)
    wide_bc, *full_a = together(wide_bc, *full_a)
    start_recv, *table_own = together(start_recv, *table_own)
    table_mine = [
        swap_wide(piece).reshape(width, high - low) for piece, (low, high) in zip(table_own, cuts)
    ]
    across_bc = xor_narrow(wide_bc, 2)
    extra = start_recv[:, rows : rows + extra_rows].astype(F32).reshape(wide, -1)
    vector_full = extra[:, 3 * mod_share :].reshape(-1)
    modulation = extra[:, :mod_share] + extra[:, mod_share : 2 * mod_share]
    modulation = (modulation + extra[:, 2 * mod_share : 3 * mod_share]).reshape(-1)
    modulation = modulation + vector_full[4 * width :]
    params = jnp.concatenate(
        [modulation.reshape(8, width), vector_full[: 4 * width].reshape(4, width)]
    )

    my_positions = part * rows + jnp.arange(rows, dtype=jnp.int32)
    far_positions = (1 - part) * rows + jnp.arange(rows, dtype=jnp.int32)
    key_cosine, key_sine = rotary_tables(jnp.concatenate([my_positions, far_positions]), HD)
    cosine, sine = key_cosine[:rows], key_sine[:rows]
    query, own_kv, hidden_one, start = project_qkv(start_recv, params, full_a, cosine, sine)
    query, sort_keys = together(query, sort_keys)
    sort_keys = lax.sort(sort_keys, dimension=1)
    far_kv = xor_narrow(own_kv, 1)
    mixed, logs = attend(query, own_kv, far_kv)
    mixed, sort_keys, hits, across_bc, *table_mine = together(
        mixed, sort_keys, hits, across_bc, *table_mine
    )
    full_bc = (wide_bc, xor_narrow(wide_bc, 1), across_bc, xor_narrow(across_bc, 1))
    tables = [gather_narrow(piece) for piece in table_mine]

    side = me // (wide // 2)
    low = me % (wide // 2)
    count_low = lax.dynamic_index_in_dim(
        lax.dynamic_index_in_dim(counts_all, low, 0, keepdims=False), micro, 0, keepdims=False
    )
    slot_row = lax.dynamic_index_in_dim(slots, micro, 0, keepdims=False)
    offset = jnp.arange(quarter, dtype=jnp.int32)
    order = jnp.concatenate(
        [
            s * (2 * quarter) + p * quarter + offset
            for p in (part, 1 - part)
            for s in (side, 1 - side)
        ]
    )
    from_low = order < count_low
    index = jnp.where(from_low, order, order - count_low)
    mine = from_low == (side == 0)
    wanted = jnp.sum(
        jnp.where(index[:, None] == jnp.arange(capacity)[None, :], slot_row[None, :], 0), axis=1
    )
    select = ((wanted[:, None] == my_positions[None, :]) & mine[:, None]).astype(BF)
    attended, middle, output, hidden_two, inner, picked = feed(
        mixed, start, params, full_a, full_bc, select
    )
    picked = picked[: 2 * quarter] + xor_narrow(picked[2 * quarter :], 1)
    row_part = picked[:quarter] + xor_wide(picked[quarter:], wide // 2)
    head_rows = spread_wide(row_part).reshape(wide * quarter, width)

    targets_mine = lax.dynamic_index_in_dim(targets_all, micro, 1, keepdims=False)
    counts_mine = lax.dynamic_index_in_dim(counts_all, micro, 1, keepdims=False)
    pairs = wide // 2
    both = jnp.concatenate([targets_mine[:pairs], targets_mine[pairs:]], axis=1)
    spot = jnp.stack([s * 2 * quarter + part * quarter + offset for s in (0, 1)])
    low_counts = counts_mine[:pairs, None, None]
    spot = jnp.where(spot[None] < low_counts, spot[None], capacity + spot[None] - low_counts)
    row_targets = jnp.sum(
        jnp.where(
            spot[..., None] == jnp.arange(2 * capacity)[None, None, None, :],
            both[:, None, None, :],
            0,
        ),
        axis=-1,
    )
    row_targets = row_targets.transpose(1, 0, 2).reshape(-1)
    target_owner = sum((row_targets >= k * entries).astype(jnp.int32) for k in range(1, narrow))
    target_rest = row_targets - target_owner * entries - me * chunk
    target_column = jnp.where(
        (target_rest >= 0) & (target_rest < chunk), (target_owner ^ group) * chunk + target_rest, -1
    )

    columns = [
        (slot, piece, slot * chunk + low + jnp.arange(high - low))
        for piece, (low, high) in enumerate(cuts)
        for slot in range(narrow)
    ]
    tables = [tables[piece][slot] for slot, piece, _ in columns]
    logits = [
        jnp.where(
            (me * chunk + at - slot * chunk < entries)[None, :], mm(head_rows, table, NN), -1e30
        )
        for table, (slot, _, at) in zip(tables, columns)
    ]
    hitting = [at[None, :] == target_column[:, None] for _, _, at in columns]
    top = functools.reduce(jnp.maximum, [jnp.max(value, axis=-1) for value in logits])
    total = sum(jnp.sum(jnp.exp(value - top[:, None]), axis=-1) for value in logits)
    target_logit = sum(
        jnp.sum(jnp.where(hit, value, 0.0), axis=-1) for hit, value in zip(hitting, logits)
    )
    stats = spread_wide(jnp.stack([top, total, target_logit]))
    top_all = jnp.max(stats[:, 0], axis=0)
    total_all = jnp.sum(stats[:, 1] * jnp.exp(stats[:, 0] - top_all[None]), axis=0)
    log_total = top_all + jnp.log(total_all)
    loss_part = jnp.sum(log_total - jnp.sum(stats[:, 2], axis=0))
    d_logits = [
        ((jnp.exp(value - log_total[:, None]) - hit.astype(F32)) * loss_scale).astype(BF)
        for hit, value in zip(hitting, logits)
    ]
    d_rows = sum(mm(grad, table, NT) for grad, table in zip(d_logits, tables))
    d_table_parts = [mm(head_rows, grad, TN) for grad in d_logits]
    d_recv = swap_wide(d_rows.astype(BF).reshape(wide, quarter, width))
    d_recv, *d_table_parts = together(d_recv, *d_table_parts)
    d_table_parts = [
        d_table_parts[piece * narrow : (piece + 1) * narrow] for piece in range(len(cuts))
    ]
    table_sent = [[xor_narrow(parts[s].astype(BF), 1) for s in (1, 3)] for parts in d_table_parts]
    d_mine = jnp.sum(d_recv.astype(F32), axis=0).astype(BF)
    d_sides = jnp.concatenate([d_mine, xor_wide(d_mine, wide // 2)])
    d_all = jnp.concatenate([d_sides, xor_narrow(d_sides, 1)])
    table_far = [
        (parts[2] + sent[1].astype(F32)).astype(BF)
        for parts, sent in zip(d_table_parts, table_sent)
    ]
    d_all, *table_far = together(d_all, *table_far)
    table_from = [xor_narrow(far, 2) for far in table_far]

    d_middle, d_attended, d_mixed, b_sent, c_sent, b_own, c_own, d_params = feed_back(
        d_all, select, params, middle, output, attended, hidden_two, inner, full_a, full_bc
    )
    def table_sum(piece):
        value = d_table_parts[piece][0] + table_sent[piece][0].astype(F32)
        value = (value + table_from[piece].astype(F32)).astype(BF)
        return value.reshape(wide, share, value.shape[1])

    d_query, d_own, d_far = attend_back(
        query, own_kv, far_kv, d_mixed, logs, cosine, sine, key_cosine, key_sine
    )
    d_query, d_own, d_far, b_sent, c_sent = together(d_query, d_own, d_far, b_sent, c_sent)
    b_near, b_far = scatter_core(b_sent, b_own)
    c_near, c_far = scatter_core(c_sent, c_own)
    d_query, d_own, d_far, *table_from = together(d_query, d_own, d_far, *table_from)
    d_far, b_far, c_far = together(xor_narrow(d_far, 1), b_far, c_far)
    b_from, c_from = xor_narrow(b_far, 2), xor_narrow(c_far, 2)
    is_mask = (my_inputs == mask_entry).astype(F32)[:, None]
    d_start_rows, d_projected, d_first = qkv_back(
        d_query, d_own, d_far, full_a, d_middle, start, params, is_mask, rows + 16, wide
    )

    d_table = [table_sum(piece) for piece in range(len(cuts))]
    d_start_rows, d_projected, d_first, b_from = together(
        d_start_rows, d_projected, d_first, b_from
    )
    a_sent, a_own = qkv_grads(d_projected, hidden_one, d_attended, mixed)
    a_near, a_far = scatter_core(a_sent, a_own)
    d_start_rows, d_first, c_from, *d_table = together(d_start_rows, d_first, c_from, *d_table)
    d_params = jnp.concatenate([d_first[:2], d_params[2:8], d_first[2:3], d_params[9:]])
    d_modulation = d_params[:8].reshape(-1)
    d_vector = jnp.concatenate([d_params[8:].reshape(-1), d_modulation])
    small = jnp.concatenate(
        [d_modulation.reshape(wide, -1, share), d_vector.reshape(wide, -1, share)], axis=1
    ).astype(BF)
    small = jnp.pad(small, ((0, 0), (0, padded - rows - 16 - small_rows), (0, 0)))
    d_start_rows = jnp.concatenate([d_start_rows, small], axis=1)
    d_start_recv = swap_wide(d_start_rows)
    a_from = xor_narrow(a_far, 2)
    b_half, c_half = [
        scatter_pair((near + other.astype(F32)).reshape(wide, share, width))
        for near, other in ((b_near, b_from), (c_near, c_from))
    ]
    a_from, d_start_recv, b_half, c_half, *d_table = together(
        a_from, d_start_recv, b_half, c_half, *d_table
    )
    d_table = [swap_wide(piece) for piece in d_table]
    d_start_recv = d_start_recv.reshape(wide * padded, share)
    d_start_across = xor_narrow(d_start_recv, 2)
    d_near = (d_start_recv, xor_narrow(d_start_recv, 1))
    d_embed = collect(sort_keys[:2], hits[:2], d_near, shift, None, entries)
    d_start_across, d_embed = together(d_start_across, d_embed)
    d_start_corner = xor_narrow(d_start_across, 1)
    a_from, b_half, c_half, d_start_corner = together(a_from, b_half, c_half, d_start_corner)
    a_half = scatter_pair((a_near + a_from.astype(F32)).reshape(wide, share, width))
    d_b, d_c, d_a = scatter_line(b_half), scatter_line(c_half), scatter_line(a_half)
    d_far = (d_start_across, d_start_corner)
    d_embed = collect(sort_keys[2:], hits[2:], d_far, shift, d_embed, entries)
    d_embed, *d_table = together(d_embed, *d_table)
    d_table = jnp.concatenate(d_table, axis=2).astype(F32).transpose(1, 0, 2)
    d_table = d_table.reshape(share, chunk * wide)[:, :entries]

    small, small_far = [
        sum(
            part.reshape(wide, padded, share)[:, rows + 16 : rows + 16 + small_rows].astype(F32)
            for part in parts
        ).reshape(wide, -1)
        for parts in (d_near, d_far)
    ]
    d_vectors = jnp.sum(small[:, mod_share:] + small_far[:, mod_share:], axis=0)
    condition_far = lax.dynamic_index_in_dim(condition, 1 - micro, 1, keepdims=False)
    d_mod_weight = lax.dot_general(
        condition_mine, small[:, :mod_share], TN, precision=HIGHEST
    ) + lax.dot_general(condition_far, small_far[:, :mod_share], TN, precision=HIGHEST)

    shards = (
        d_embed,
        d_table,
        jnp.stack([d_a[:, k * heads_width : (k + 1) * heads_width] for k in range(3)]),
        flip(d_a[:, 3 * heads_width :]),
        d_b,
        d_c,
        d_mod_weight,
        d_vectors,
    )

    square = jnp.zeros((), F32)
    for grad in shards[:6]:
        square = square + jnp.sum(grad * grad)
    shared_square = jnp.sum(shards[6] * shards[6]) + jnp.sum(shards[7] * shards[7])
    square = square + shared_square / narrow
    sums = lax.all_to_all(
        jnp.broadcast_to(jnp.stack([loss_part / wide, square])[None, None], (wide * narrow, 1, 2)),
        ("wide",) + NARROW,
        0,
        0,
        tiled=True,
    )
    sums = jnp.sum(sums, axis=(0, 1))
    loss_sum = sums[0]
    grad_norm = jnp.sqrt(sums[1])
    factor = CLIP_NORM / jnp.maximum(grad_norm, CLIP_NORM)
    results = []
    for member in range(8):
        turn = (lambda value: value.T) if member in (0, 5) else (lambda value: value)
        master = turn(masters[member])
        grad = shards[member] * factor
        first = BETA_ONE * turn(firsts[member]) + (1.0 - BETA_ONE) * grad
        second = BETA_TWO * turn(seconds[member]) + (1.0 - BETA_TWO) * grad * grad
        stepped = (
            first / (1.0 - BETA_ONE**STEP) / (jnp.sqrt(second / (1.0 - BETA_TWO**STEP)) + ADAM_EPS)
        )
        decay = WEIGHT_DECAY if member < 7 else 0.0
        fresh = master - LEARN_RATES[member] * (stepped + decay * master)
        results.extend([turn(fresh), turn(first), turn(second)])
    return (loss_sum, grad_norm, *results)


def solution(mesh):
    shape = (mesh.shape["wide"], mesh.shape["narrow"] // 2, 2)
    mesh = jax.sharding.Mesh(mesh.devices.reshape(shape), ("wide",) + NARROW)
    weights = (
        P(NARROW, "wide"),
        P("wide", NARROW),
        P(None, "wide", NARROW),
        P(NARROW, "wide"),
        P("wide", NARROW),
        P(NARROW, "wide"),
        P(None, "wide"),
        P("wide"),
    )
    data = (P("wide", None, None), P("wide", None, None), P("wide", None))
    outs = [P(), P()]
    for spec in weights:
        outs.extend([spec] * 3)
    return jax.shard_map(
        local,
        mesh=mesh,
        in_specs=data + weights * 3,
        out_specs=tuple(outs),
        check_vma=False,
    )
```

```python
import functools
import math

import jax
import jax.numpy as jnp
from jax import lax
from jax.experimental import pallas as pl
from jax.experimental.pallas import tpu as pltpu
from jax.sharding import PartitionSpec as P

HD = 64
STEP = 10

HIGHEST = lax.Precision.HIGHEST
NORM_EPS = 1e-06
CLIP_NORM = 0.005
BETA_ONE = 0.9
BETA_TWO = 0.95
ADAM_EPS = 1e-08
WEIGHT_DECAY = 0.1
LEARN_RATES = (1.0, 0.1, 0.07, 0.5, 0.07, 0.04, 0.2, 0.5)
NARROW = ("line", "core")
BF = jnp.bfloat16
F32 = jnp.float32
VMEM_LIMIT = 56 * 1024 * 1024
FREE = pl.CostEstimate(flops=0, bytes_accessed=0, transcendentals=0)


def together(*values):
    return lax.optimization_barrier(values)


def xor_narrow(value, bits):
    return lax.ppermute(
        value, NARROW, [(i, i ^ bits) for i in range(lax.axis_size(NARROW))]
    )


def xor_wide(value, bits):
    return lax.ppermute(value, "wide", [(i, i ^ bits) for i in range(lax.axis_size("wide"))])


def swap_wide(value):
    return lax.all_to_all(value, "wide", 0, 0, tiled=True)


def spread_wide(value):
    if lax.axis_size("wide") > 8:
        return lax.all_gather(value, "wide")
    return swap_wide(jnp.broadcast_to(value[None], (lax.axis_size("wide"),) + value.shape))


def gather_wide(value, axis):
    return lax.all_gather(value, "wide", axis=axis, tiled=True)


def scatter_pair(value):
    count = lax.axis_size("wide")
    if count != 8:
        return value
    side = lax.axis_index("wide") & 1
    pairs = value.reshape((4, 2) + value.shape[1:])
    kept = lax.dynamic_index_in_dim(pairs, side, 1, keepdims=False)
    sent = lax.dynamic_index_in_dim(pairs, 1 - side, 1, keepdims=False).astype(BF)
    return kept + xor_wide(sent, 1).astype(F32)


def scatter_line(half):
    if lax.axis_size("wide") != 8:
        return lax.psum_scatter(half, "wide", scatter_dimension=0)
    depth = lax.axis_index("wide") >> 1
    total = lax.dynamic_index_in_dim(half, depth, 0, keepdims=False)
    low = half.astype(BF)
    for k in (1, 2, 3):
        piece = lax.dynamic_index_in_dim(low, depth ^ k, 0, keepdims=False)
        total = total + xor_wide(piece, 2 * k).astype(F32)
    return total


def scatter_core(sent, own):
    from_core = xor_narrow(sent, 1).astype(F32)
    near = own[0].astype(F32) + from_core[0]
    far = own[1].astype(F32) + from_core[1]
    return near, far.astype(BF)


def gather_narrow(value):
    across = xor_narrow(value, 2)
    beside = xor_narrow(value, 1)
    corner = xor_narrow(across, 1)
    return value, beside, across, corner


def rounded(value):
    return lax.reduce_precision(value, exponent_bits=8, mantissa_bits=7)


def layer_norm(values):
    centered = values - jnp.mean(values, axis=-1, keepdims=True)
    inverse = lax.rsqrt(jnp.mean(centered * centered, axis=-1, keepdims=True) + NORM_EPS)
    return (centered * inverse, inverse)


def norm_back(grad, normed, inverse):
    return inverse * (
        grad
        - jnp.mean(grad, axis=-1, keepdims=True)
        - normed * jnp.mean(grad * normed, axis=-1, keepdims=True)
    )


def gelu_tanh(values):
    inner = 0.7978845608 * (values + 0.044715 * values * values * values)
    return 0.5 * values * (1.0 + jnp.tanh(inner))


def gelu_slope(values):
    tangent = jnp.tanh(0.7978845608 * (values + 0.044715 * values * values * values))
    return 0.5 * (1.0 + tangent) + 0.5 * values * (1.0 - tangent * tangent) * 0.7978845608 * (
        1.0 + 0.134145 * values * values
    )


def rotary_tables(positions, width):
    freqs = jnp.exp(jnp.arange(width // 2, dtype=F32) * (-2.0 * math.log(10000.0) / width))
    angle = positions.astype(F32)[:, None] * freqs[None, :]
    cosine, sine = jnp.cos(angle), jnp.sin(angle)
    return (
        jnp.concatenate([cosine] * 4, axis=1),
        jnp.concatenate([-sine, sine, -sine, sine], axis=1),
    )


def time_features(moment, width):
    freqs = jnp.exp(jnp.arange(width // 2, dtype=F32) * (-math.log(10000.0) / (width // 2)))
    angle = 1000.0 * moment[..., None] * freqs
    return jnp.concatenate([jnp.cos(angle), jnp.sin(angle)], axis=-1)


def turned(values, cosine, sine):
    blocks = []
    for place in range(0, values.shape[1], 2 * HD):
        block = values[:, place : place + 2 * HD]
        lanes = lax.broadcasted_iota(jnp.int32, block.shape, 1)
        ahead = pltpu.roll(block, 2 * HD - HD // 2, 1)
        behind = pltpu.roll(block, HD // 2, 1)
        other = jnp.where((lanes & (HD - 1)) < HD // 2, ahead, behind)
        blocks.append(block * cosine + other * sine)
    return jnp.concatenate(blocks, axis=1) if len(blocks) > 1 else blocks[0]


def turned_back(values, cosine, sine):
    spare = -values.shape[1] % (2 * HD)
    filled = jnp.concatenate([values, jnp.zeros((values.shape[0], spare), F32)], axis=1)
    return turned(filled, cosine, -sine)[:, : values.shape[1]]


NT = (((1,), (1,)), ((), ()))
NN = (((1,), (0,)), ((), ()))
TN = (((0,), (0,)), ((), ()))


def mm(a, b, dims):
    return lax.dot_general(a, b, dims, preferred_element_type=F32)


SHIFT_ONE, SCALE_ONE, GATE_ONE, SHIFT_TWO, SCALE_TWO, GATE_TWO, SHIFT_LAST, SCALE_LAST = range(8)
GAIN_ONE, GAIN_TWO, GAIN_LAST, BIAS_DOWN = range(8, 12)
LOCAL = dict(
    compiler_params=pltpu.CompilerParams(vmem_limit_bytes=60 * 1024 * 1024), cost_estimate=FREE
)
BUSY = dict(LOCAL, cost_estimate=pl.CostEstimate(10**10, 0, 4 * 10**7))


def column_sum(values):
    return jnp.sum(values, axis=0, keepdims=True)


def qkv_kernel(
    recv_ref, par_ref, a0, a1, a2, a3, cos_ref, sin_ref, q_ref, kv_ref, hidden_ref, start_ref
):
    par = lambda k: par_ref[k : k + 1, :]
    rows = start_ref.shape[0]
    start = jnp.concatenate(
        [recv_ref[piece, :rows, :].astype(F32) for piece in range(recv_ref.shape[0])], axis=1
    )
    start_ref[...] = start
    normed, _ = layer_norm(start)
    hidden = normed * par(GAIN_ONE) * (1.0 + par(SCALE_ONE)) + par(SHIFT_ONE)
    hidden = hidden.astype(BF)
    hidden_ref[...] = hidden
    share = q_ref.shape[2]
    for s, weight in enumerate((a0, a1, a2, a3)):
        value = mm(hidden, weight[...], NN)
        pair = turned(value[:, : 2 * share], cos_ref[...], sin_ref[...])
        q_ref[s] = pair[:, :share].astype(BF)
        kv_ref[s] = jnp.concatenate(
            [pair[:, share:], value[:, 2 * share : 3 * share]], axis=1
        ).astype(BF)


def project_qkv(recv, params, weights, cosine, sine):
    rows, width = cosine.shape[0], params.shape[1]
    share = width // 4
    return pl.pallas_call(
        qkv_kernel,
        out_shape=[
            jax.ShapeDtypeStruct((4, rows, share), BF),
            jax.ShapeDtypeStruct((4, rows, 2 * share), BF),
            jax.ShapeDtypeStruct((rows, width), BF),
            jax.ShapeDtypeStruct((rows, width), F32),
        ],
        name="qkv",
        **LOCAL,
    )(recv, params, *weights, cosine, sine)


def head_mask(values, head):
    lanes = lax.broadcasted_iota(jnp.int32, values.shape, 1)
    inside = (lanes >= head * HD) & (lanes < (head + 1) * HD)
    return jnp.where(inside, values, jnp.zeros_like(values))


def attend_kernel(q_ref, own_ref, far_ref, out_ref, log_ref):
    query = q_ref[0] * BF(HD**-0.5)
    share = query.shape[1]
    both = jnp.concatenate([own_ref[0], far_ref[0]], axis=0)
    keys, values = both[:, :share], both[:, share:].T
    parts = []
    for head in range(query.shape[1] // HD):
        scores = mm(keys, head_mask(query, head), NT)
        top = jnp.max(scores, axis=0, keepdims=True)
        shifted = jnp.exp(scores - top)
        total = jnp.sum(shifted, axis=0, keepdims=True)
        weights = (shifted * (1.0 / total)).astype(BF)
        parts.append(mm(values[head * HD : (head + 1) * HD], weights, NN))
        log_ref[0, head : head + 1, :] = top + jnp.log(total)
    out_ref[0] = jnp.concatenate(parts, axis=0).T.astype(BF)


def attend_specs(rows, share):
    return [
        pl.BlockSpec((1, rows, share), lambda s: (s, 0, 0)),
        pl.BlockSpec((1, rows, 2 * share), lambda s: (s, 0, 0)),
        pl.BlockSpec((1, rows, 2 * share), lambda s: (s ^ 1, 0, 0)),
    ]


def attend(query, own, far):
    slots, rows, share = query.shape
    heads = share // HD
    return pl.pallas_call(
        attend_kernel,
        grid=(slots,),
        in_specs=attend_specs(rows, share),
        out_specs=[
            pl.BlockSpec((1, rows, share), lambda s: (s, 0, 0)),
            pl.BlockSpec((1, heads, rows), lambda s: (s, 0, 0)),
        ],
        out_shape=[
            jax.ShapeDtypeStruct((slots, rows, share), BF),
            jax.ShapeDtypeStruct((slots, heads, rows), F32),
        ],
        name="attend",
        **LOCAL,
    )(query, own, far)


def feed_kernel(
    mixed_ref, start_ref, par_ref, a0, a1, a2, a3, bc0, bc1, bc2, bc3, select_ref,
    attended_ref, middle_ref, output_ref, hidden_ref, inner_ref, picked_ref,
):
    par = lambda k: par_ref[k : k + 1, :]
    share = mixed_ref.shape[2]
    attended = sum(
        mm(mixed_ref[s], weight[:, 3 * share :], NT) for s, weight in enumerate((a0, a1, a2, a3))
    )
    attended_ref[...] = attended
    middle = start_ref[...] + par(GATE_ONE) * attended
    middle_ref[...] = middle
    normed, _ = layer_norm(middle)
    hidden = normed * par(GAIN_TWO) * (1.0 + par(SCALE_TWO)) + par(SHIFT_TWO)
    hidden = hidden.astype(BF)
    hidden_ref[...] = hidden
    output = jnp.zeros(middle.shape, F32)
    for s, weight in enumerate((bc0, bc1, bc2, bc3)):
        inner = mm(hidden, weight[0], NN)
        inner_ref[s] = inner
        output = output + mm(gelu_tanh(inner).astype(BF), weight[1], NT)
    output_ref[...] = output
    final = middle + par(GATE_TWO) * (output + par(BIAS_DOWN))
    normed, _ = layer_norm(final)
    last = normed * (par(GAIN_LAST) * (1.0 + par(SCALE_LAST))) + par(SHIFT_LAST)
    picked_ref[...] = mm(select_ref[...], last.astype(BF), NN).astype(BF)


def feed(mixed, start, params, weights_a, weights_bc, select):
    rows, width = start.shape
    plain = jax.ShapeDtypeStruct((rows, width), F32)
    return pl.pallas_call(
        feed_kernel,
        out_shape=[
            plain,
            plain,
            plain,
            jax.ShapeDtypeStruct((rows, width), BF),
            jax.ShapeDtypeStruct((4, rows, width), F32),
            jax.ShapeDtypeStruct((select.shape[0], width), BF),
        ],
        name="feed",
        **LOCAL,
    )(mixed, start, params, *weights_a, *weights_bc, select)


SLOT_PLACES = ((1, 0, 0), (3, 0, 1), (0, 1, 0), (2, 1, 1))


def feed_back_kernel(
    rows_ref, select_ref, par_ref, middle_ref, output_ref, attended_ref, hidden_ref, inner_ref,
    a0, a1, a2, a3, bc0, bc1, bc2, bc3,
    d_middle_ref, d_attended_ref, d_mixed_ref, b_sent_ref, c_sent_ref, b_own_ref, c_own_ref,
    vec_ref,
):
    par = lambda k: par_ref[k : k + 1, :]
    share = d_mixed_ref.shape[2]
    middle, output = middle_ref[...], output_ref[...]
    d_hidden = mm(select_ref[...], rows_ref[...], TN)
    final = middle + par(GATE_TWO) * (output + par(BIAS_DOWN))
    normed, inverse = layer_norm(final)
    d_normed = column_sum(d_hidden * normed)
    vec_ref[SHIFT_LAST : SHIFT_LAST + 1, :] = column_sum(d_hidden)
    vec_ref[SCALE_LAST : SCALE_LAST + 1, :] = d_normed * par(GAIN_LAST)
    vec_ref[GAIN_LAST : GAIN_LAST + 1, :] = d_normed * (1.0 + par(SCALE_LAST))
    d_final = norm_back(d_hidden * (par(GAIN_LAST) * (1.0 + par(SCALE_LAST))), normed, inverse)
    vec_ref[BIAS_DOWN : BIAS_DOWN + 1, :] = column_sum(d_final) * par(GATE_TWO)
    vec_ref[GATE_TWO : GATE_TWO + 1, :] = column_sum(d_final * (output + par(BIAS_DOWN)))
    d_output = (d_final * par(GATE_TWO)).astype(BF)
    hidden = hidden_ref[...]
    d_hidden = jnp.zeros(middle.shape, F32)
    weights = (bc0, bc1, bc2, bc3)
    for s, kept, place in SLOT_PLACES:
        b_ref, c_ref = (b_own_ref, c_own_ref) if kept else (b_sent_ref, c_sent_ref)
        inner = inner_ref[s]
        tangent = jnp.tanh(0.7978845608 * (inner + 0.044715 * inner * inner * inner))
        active = (0.5 * inner * (1.0 + tangent)).astype(BF)
        slope = 0.5 * (1.0 + tangent) + 0.5 * inner * (
            1.0 - tangent * tangent
        ) * 0.7978845608 * (1.0 + 0.134145 * inner * inner)
        d_inner = (mm(d_output, weights[s][1], NN) * slope).astype(BF)
        b_ref[place] = mm(hidden, d_inner, TN).astype(BF)
        c_ref[place] = mm(d_output, active, TN).astype(BF)
        d_hidden = d_hidden + mm(d_inner, weights[s][0], NT)
    normed, inverse = layer_norm(middle)
    d_normed = column_sum(d_hidden * normed)
    vec_ref[SHIFT_TWO : SHIFT_TWO + 1, :] = column_sum(d_hidden)
    vec_ref[SCALE_TWO : SCALE_TWO + 1, :] = d_normed * par(GAIN_TWO)
    vec_ref[GAIN_TWO : GAIN_TWO + 1, :] = d_normed * (1.0 + par(SCALE_TWO))
    d_middle = d_final + norm_back(
        d_hidden * par(GAIN_TWO) * (1.0 + par(SCALE_TWO)), normed, inverse
    )
    d_middle_ref[...] = d_middle
    vec_ref[GATE_ONE : GATE_ONE + 1, :] = column_sum(d_middle * attended_ref[...])
    d_attended = (d_middle * par(GATE_ONE)).astype(BF)
    d_attended_ref[...] = d_attended
    for s, weight in enumerate((a0, a1, a2, a3)):
        d_mixed_ref[s] = mm(d_attended, weight[:, 3 * share :], NN).astype(BF)
    for unused in (SHIFT_ONE, SCALE_ONE, GAIN_ONE):
        vec_ref[unused : unused + 1, :] = jnp.zeros_like(par(0))


def feed_back(
    d_rows, select, params, middle, output, attended, hidden, inner, weights_a, weights_bc
):
    rows, width = middle.shape
    half = jax.ShapeDtypeStruct((2, width, width), BF)
    return pl.pallas_call(
        feed_back_kernel,
        out_shape=[
            jax.ShapeDtypeStruct((rows, width), F32),
            jax.ShapeDtypeStruct((rows, width), BF),
            jax.ShapeDtypeStruct((4, rows, width // 4), BF),
            half,
            half,
            half,
            half,
            jax.ShapeDtypeStruct(params.shape, F32),
        ],
        name="feed_back",
        **BUSY,
    )(
        d_rows, select, params, middle, output, attended, hidden, inner, *weights_a, *weights_bc
    )


def attend_back_kernel(
    q_ref, own_ref, far_ref, grad_ref, log_ref, cos_ref, sin_ref, kcos_ref, ksin_ref,
    dq_ref, d_own_ref, d_far_ref,
):
    query, grad = q_ref[0], grad_ref[0]
    share = query.shape[1]
    both = jnp.concatenate([own_ref[0], far_ref[0]], axis=0)
    keys, values = both[:, :share], both[:, share:]
    turned_keys = keys.T
    scale = HD**-0.5
    rows = query.shape[0]
    dq = []
    dk = jnp.zeros(keys.shape, F32)
    dv = jnp.zeros(keys.shape, F32)
    for head in range(query.shape[1] // HD):
        query_one = head_mask(query * BF(scale), head)
        grad_one = head_mask(grad, head)
        scores = mm(keys, query_one, NT)
        weights = jnp.exp(scores - log_ref[0, head : head + 1, :])
        d_weights = mm(values, grad_one, NT)
        delta = jnp.sum(weights * d_weights, axis=0, keepdims=True)
        d_scores = (weights * (d_weights - delta)).astype(BF)
        dq.append(mm(turned_keys[head * HD : (head + 1) * HD], d_scores, NN))
        dk = dk + mm(d_scores, query_one, NN)
        dv = dv + mm(weights.astype(BF), grad_one, NN)
    dq = jnp.concatenate(dq, axis=0).T * scale
    dq_ref[0] = turned_back(dq, cos_ref[...], sin_ref[...]).astype(BF)
    dk = turned_back(dk, kcos_ref[...], ksin_ref[...])
    both = jnp.concatenate([dk, dv], axis=1)
    d_own_ref[0] = both[:rows]
    d_far_ref[0] = both[rows:].astype(BF)


def attend_back(query, own, far, grad, logs, cosine, sine, key_cosine, key_sine):
    slots, rows, share = query.shape
    heads = share // HD
    whole = lambda table: pl.BlockSpec(table.shape, lambda s: (0, 0))
    one, two, other = attend_specs(rows, share)
    return pl.pallas_call(
        attend_back_kernel,
        grid=(slots,),
        in_specs=[
            one, two, other, one, pl.BlockSpec((1, heads, rows), lambda s: (s, 0, 0)),
            whole(cosine), whole(sine), whole(key_cosine), whole(key_sine),
        ],
        out_specs=[one, two, two],
        out_shape=[
            jax.ShapeDtypeStruct((slots, rows, share), BF),
            jax.ShapeDtypeStruct((slots, rows, 2 * share), F32),
            jax.ShapeDtypeStruct((slots, rows, 2 * share), BF),
        ],
        name="attend_back",
        **LOCAL,
    )(query, own, far, grad, logs, cosine, sine, key_cosine, key_sine)


def slot_grads(dq_ref, d_own_ref, d_far_ref, s):
    return jnp.concatenate(
        [
            dq_ref[s],
            (d_own_ref[s] + d_far_ref[s ^ 1].astype(F32)).astype(BF),
        ],
        axis=1,
    )


def qkv_back_kernel(
    dq_ref, d_own_ref, d_far_ref, a0, a1, a2, a3, d_middle_ref, start_ref, par_ref, mask_ref,
    out_ref, grads_ref, vec_ref,
):
    par = lambda k: par_ref[k : k + 1, :]
    share = dq_ref.shape[2]
    rows = start_ref.shape[0]
    d_hidden = jnp.zeros(start_ref.shape, F32)
    for s, weight in enumerate((a0, a1, a2, a3)):
        grads = slot_grads(dq_ref, d_own_ref, d_far_ref, s)
        grads_ref[s] = grads
        d_hidden = d_hidden + mm(grads, weight[:, : 3 * share], NT)
    normed, inverse = layer_norm(start_ref[...])
    d_normed = column_sum(d_hidden * normed)
    vec_ref[0:1, :] = column_sum(d_hidden)
    vec_ref[1:2, :] = d_normed * par(GAIN_ONE)
    vec_ref[2:3, :] = d_normed * (1.0 + par(SCALE_ONE))
    d_start = d_middle_ref[...] + norm_back(
        d_hidden * par(GAIN_ONE) * (1.0 + par(SCALE_ONE)), normed, inverse
    )
    masked = column_sum(d_start * mask_ref[...])
    extra = out_ref.shape[1] - rows
    first = lax.broadcasted_iota(jnp.int32, (extra, 1), 0) == 0
    whole = jnp.concatenate([d_start, jnp.where(first, masked, 0.0)], axis=0).astype(BF)
    columns = out_ref.shape[2]
    for piece in range(out_ref.shape[0]):
        out_ref[piece] = whole[:, piece * columns : (piece + 1) * columns]


def qkv_back(dq, d_own, d_far, weights, d_middle, start, params, is_mask, padded, wide):
    rows, width = start.shape
    return pl.pallas_call(
        qkv_back_kernel,
        out_shape=[
            jax.ShapeDtypeStruct((wide, padded, width // wide), BF),
            jax.ShapeDtypeStruct((4, rows, 3 * width // 4), BF),
            jax.ShapeDtypeStruct((3, width), F32),
        ],
        name="qkv_back",
        **LOCAL,
    )(dq, d_own, d_far, *weights, d_middle, start, params, is_mask)


def flip(value):
    def kernel(value_ref, out_ref):
        out_ref[...] = value_ref[...].T

    return pl.pallas_call(
        kernel, out_shape=jax.ShapeDtypeStruct(value.shape[::-1], value.dtype), name="flip", **LOCAL
    )(value)


def qkv_grads_kernel(grads_ref, hidden_ref, d_attended_ref, mixed_ref, sent_ref, own_ref):
    for s, kept, place in SLOT_PLACES:
        out_ref = own_ref if kept else sent_ref
        out_ref[place] = jnp.concatenate(
            [
                mm(hidden_ref[...], grads_ref[s], TN),
                mm(d_attended_ref[...], mixed_ref[s], TN),
            ],
            axis=1,
        ).astype(BF)


def qkv_grads(grads, hidden, d_attended, mixed):
    width = hidden.shape[1]
    half = jax.ShapeDtypeStruct((2, width, width), BF)
    return pl.pallas_call(
        qkv_grads_kernel, out_shape=[half, half], name="qkv_grads", **BUSY
    )(grads, hidden, d_attended, mixed)


def rows_kernel(own_ref, other_ref, out_ref):
    step = pl.program_id(0)
    half = pl.num_programs(0) // 2

    @pl.when(step < half)
    def _():
        out_ref[...] = own_ref[...].astype(BF).T.astype(F32)

    @pl.when((step >= half) & (step < 2 * half))
    def _():
        out_ref[...] = other_ref[...].T.astype(F32)

    @pl.when(step == 2 * half)
    def _():
        out_ref[...] = jnp.zeros_like(out_ref)


def table_rows_of(own, other):
    width, entries = own.shape
    block = next(b for b in (1408, 1152, 384, 128) if entries % b == 0)
    half = entries // block
    return pl.pallas_call(
        rows_kernel,
        grid=(2 * half + 1,),
        in_specs=[
            pl.BlockSpec((width, block), lambda i: (0, jnp.minimum(i, half - 1))),
            pl.BlockSpec((width, block), lambda i: (0, jnp.clip(i - half, 0, half - 1))),
        ],
        out_specs=pl.BlockSpec((block, width), lambda i: (i, 0)),
        out_shape=jax.ShapeDtypeStruct((2 * entries + block, width), F32),
        name="table_rows",
        **BUSY,
    )(own, other)


def lookup_kernel(id_ref, table_ref, out_ref, scratch):
    block = scratch.shape[0]
    unroll = 16

    def body(step, _):
        for k in range(unroll):
            place = step * unroll + k
            scratch[pl.ds(place, 1), :] = table_ref[pl.ds(id_ref[0, 0, place], 1), :]
        return 0

    lax.fori_loop(0, block // unroll, body, 0)
    out_ref[...] = scratch[...].astype(BF)


def lookup(table, ids):
    count = ids.shape[0]
    block = min(2048, count)
    width = table.shape[1]
    return pl.pallas_call(
        lookup_kernel,
        grid=(count // block,),
        in_specs=[
            pl.BlockSpec((1, 1, block), lambda i: (i, 0, 0), memory_space=pltpu.SMEM),
            pl.BlockSpec(table.shape, lambda i: (0, 0), pipeline_mode=pl.Buffered(1)),
        ],
        out_specs=pl.BlockSpec((block, width), lambda i: (i, 0)),
        out_shape=jax.ShapeDtypeStruct((count, width), BF),
        scratch_shapes=[pltpu.VMEM((block, width), F32)],
        name="lookup",
        **LOCAL,
    )(ids.reshape(count // block, 1, block), table)


def collect_kernel(shift, first, key_ref, count_ref, one_ref, two_ref, *refs):
    if first:
        out_ref, rows_ref = refs
        sum_ref = out_ref
        sum_ref[...] = jnp.zeros_like(sum_ref)
    else:
        old_ref, out_ref, rows_ref, sum_ref = refs
        sum_ref[...] = old_ref[...]
    mask = (1 << shift) - 1
    unroll = 8
    for part, grad_ref in enumerate((one_ref, two_ref)):
        rows_ref[...] = grad_ref[...].astype(F32)
        count = count_ref[part]

        def group(item, _, part=part):
            keys = [key_ref[part, item * unroll + k] for k in range(unroll)]
            targets = [lax.shift_right_logical(key, shift) for key in keys]
            olds = [sum_ref[pl.ds(target, 1), :] for target in targets]
            news = [rows_ref[pl.ds(key & mask, 1), :] for key in keys]
            sums = []
            for k in range(unroll):
                old = olds[k]
                if k:
                    old = jnp.where(targets[k] == targets[k - 1], sums[k - 1], old)
                sums.append(old + news[k])
            for k in range(unroll):
                sum_ref[pl.ds(targets[k], 1), :] = sums[k]
            return 0

        def single(item, _, part=part):
            key = key_ref[part, item]
            target = pl.ds(lax.shift_right_logical(key, shift), 1)
            sum_ref[target, :] = sum_ref[target, :] + rows_ref[pl.ds(key & mask, 1), :]
            return 0

        groups = lax.shift_right_logical(count, 3)
        lax.fori_loop(0, groups, group, 0)
        lax.fori_loop(groups * unroll, count, single, 0)

    if not first:

        def turn(block, _):
            place = pl.ds(pl.multiple_of(block * 128, 128), 128)
            out_ref[:, place] = sum_ref[place, :].T
            return 0

        lax.fori_loop(0, sum_ref.shape[0] // 128, turn, 0)


def collect(keys, counts, grads, shift, before, entries):
    tokens, width = grads[0].shape
    first = before is None
    out_dims = (entries, width) if first else (width, entries)
    scratch = [pltpu.VMEM((tokens, width), F32)]
    if not first:
        scratch.append(pltpu.VMEM((entries, width), F32))
    smem = pl.BlockSpec(memory_space=pltpu.SMEM)
    vmem = pl.BlockSpec(memory_space=pltpu.VMEM)
    return pl.pallas_call(
        functools.partial(collect_kernel, shift, first),
        in_specs=[smem, smem] + [vmem] * (2 if first else 3),
        out_specs=vmem,
        out_shape=jax.ShapeDtypeStruct(out_dims, F32),
        scratch_shapes=scratch,
        name="collect",
        **LOCAL,
    )(keys, counts, *grads, *([] if first else [before]))


def local(
    token_ids, mask_slots, mask_counts,
    embedding, out_table, qkv_weight, proj_weight, up_weight, down_weight, mod_weight, vectors,
    embedding_first, out_table_first, qkv_first, proj_first, up_first, down_first, mod_first,
    vectors_first,
    embedding_second, out_table_second, qkv_second, proj_second, up_second, down_second,
    mod_second, vectors_second,
):
    masters = (
        embedding, out_table, qkv_weight, proj_weight, up_weight, down_weight, mod_weight, vectors,
    )
    firsts = (
        embedding_first, out_table_first, qkv_first, proj_first, up_first, down_first, mod_first,
        vectors_first,
    )
    seconds = (
        embedding_second, out_table_second, qkv_second, proj_second, up_second, down_second,
        mod_second, vectors_second,
    )
    wide = lax.axis_size("wide")
    narrow = lax.axis_size(NARROW)
    me = lax.axis_index("wide")
    group = lax.axis_index(NARROW)
    part = group & 1
    micro = group >> 1
    entries, share = embedding.shape
    width = share * wide
    vocab = entries * narrow
    micro_count, length = token_ids.shape[1:]
    capacity = mask_slots.shape[2]
    rows = length // 2
    pair_total = 5 * length // 16
    quarter = pair_total // 4
    loss_scale = 1.0 / (length * micro_count * wide)
    positions = jnp.arange(length, dtype=jnp.int32)

    tokens, slots, counts = token_ids[0], mask_slots[0], mask_counts[0]
    at_slot = slots[:, :, None] == positions[None, None, :]
    valid = jnp.arange(capacity)[None, :] < counts[:, None]
    masked = jnp.any(at_slot & valid[:, :, None], axis=1)
    targets = jnp.sum(jnp.where(at_slot, tokens[:, None, :], 0), axis=2)
    inputs = jnp.where(masked, vocab - 1, tokens)
    packed = jnp.concatenate(
        [inputs, targets, jnp.broadcast_to(counts[:, None], (micro_count, 128))], axis=1
    )
    packed_all = spread_wide(packed)
    inputs_all = packed_all[:, :, :length]
    targets_all = packed_all[:, :, length : length + capacity]
    counts_all = packed_all[:, :, length + capacity]

    shard_a = jnp.concatenate(
        [qkv_weight[0], qkv_weight[1], qkv_weight[2], proj_weight.T], axis=1
    ).astype(BF)
    wide_all = gather_wide(
        jnp.stack([shard_a, up_weight.astype(BF), down_weight.T.astype(BF)]), 1
    )
    wide_a, wide_bc = wide_all[0], wide_all[1:]
    heads_width = width // narrow

    chunk = -(-entries // (128 * wide)) * 128
    spare = chunk * wide - entries
    table_own = jnp.pad(out_table.astype(BF), ((0, 0), (0, spare)))
    table_own = table_own.reshape(share, wide, chunk).transpose(1, 0, 2)
    cuts = [(0, chunk)]
    table_own = [table_own[:, :, low:high] for low, high in cuts]

    moments = counts_all.astype(F32) / pair_total
    condition = jax.nn.silu(time_features(moments, mod_weight.shape[0]))
    condition_mine = lax.dynamic_index_in_dim(condition, micro, 1, keepdims=False)
    mod_part = jnp.dot(condition_mine, rounded(mod_weight), precision=HIGHEST)
    mod_share = mod_part.shape[1]
    exact = []
    rest = mod_part
    for _ in range(3):
        exact.append(rounded(rest))
        rest = rest - exact[-1]
    extra = jnp.concatenate(
        exact + [jnp.broadcast_to(rounded(vectors), (wide, vectors.shape[0]))], axis=1
    ).astype(BF)
    extra_rows = extra.shape[1] // share
    extra = extra.reshape(wide, extra_rows, share)
    extra = jnp.pad(extra, ((0, 0), (0, -extra_rows % 16), (0, 0)))

    table_rows = table_rows_of(embedding.T, xor_narrow(embedding.T.astype(BF), 1))
    half_ids = lax.dynamic_slice_in_dim(inputs_all, part * rows, rows, axis=2)
    half_ids = jnp.stack(
        [
            lax.dynamic_index_in_dim(half_ids, micro, 1, keepdims=False),
            lax.dynamic_index_in_dim(half_ids, 1 - micro, 1, keepdims=False),
        ]
    )
    inside, beside = half_ids - group * entries, half_ids - (group ^ 1) * entries
    inside_here = (inside >= 0) & (inside < entries)
    beside_here = (beside >= 0) & (beside < entries)
    places = jnp.where(
        inside_here, inside, jnp.where(beside_here, beside + entries, 2 * entries)
    )
    looked = lookup(table_rows, places.reshape(-1))
    looked = looked.reshape(2, wide, rows, share)
    start_part = looked[0] + xor_narrow(looked[1], 2)
    start_recv_in = jnp.concatenate([start_part, extra], axis=1)
    start_recv_in, wide_a = together(start_recv_in, wide_a)
    full_a = gather_narrow(wide_a)
    start_recv = swap_wide(start_recv_in)

    my_inputs = lax.dynamic_slice_in_dim(
        lax.dynamic_index_in_dim(inputs, micro, 0, keepdims=False), part * rows, rows, axis=0
    )
    small_rows = (9 * width + 3 * width + 8 * width) // wide // share
    padded = rows + 16 + -(-small_rows // 16) * 16
    padded = rows + 16 + 32
    mask_entry = vocab - 1
    ids = jnp.stack(
        [
            lax.dynamic_slice_in_dim(
                lax.dynamic_index_in_dim(inputs_all, (group ^ s) >> 1, 1, keepdims=False),
                ((group ^ s) & 1) * rows,
                rows,
                axis=1,
            )
            for s in range(narrow)
        ]
    )
    ids = jnp.concatenate(
        [
            jnp.where(ids == mask_entry, -1, ids),
            jnp.full((narrow, wide, 1), mask_entry, jnp.int32),
            jnp.full((narrow, wide, padded - rows - 1), -1, jnp.int32),
        ],
        axis=2,
    ).reshape(narrow, wide * padded)
    local_ids = ids - group * entries
    taken = (local_ids >= 0) & (local_ids < entries)
    shift = (wide * padded - 1).bit_length()
    sort_keys = jnp.where(
        taken,
        local_ids * (1 << shift) + jnp.arange(wide * padded, dtype=jnp.int32)[None, :],
        jnp.iinfo(jnp.int32).max,
    )
    hits = jnp.sum(taken.astype(jnp.int32), axis=1)
    wide_bc, *full_a = together(wide_bc, *full_a)
    start_recv, *table_own = together(start_recv, *table_own)
    table_mine = [
        swap_wide(piece).reshape(width, high - low) for piece, (low, high) in zip(table_own, cuts)
    ]
    across_bc = xor_narrow(wide_bc, 2)
    extra = start_recv[:, rows : rows + extra_rows].astype(F32).reshape(wide, -1)
    vector_full = extra[:, 3 * mod_share :].reshape(-1)
    modulation = extra[:, :mod_share] + extra[:, mod_share : 2 * mod_share]
    modulation = (modulation + extra[:, 2 * mod_share : 3 * mod_share]).reshape(-1)
    modulation = modulation + vector_full[4 * width :]
    params = jnp.concatenate(
        [modulation.reshape(8, width), vector_full[: 4 * width].reshape(4, width)]
    )

    my_positions = part * rows + jnp.arange(rows, dtype=jnp.int32)
    far_positions = (1 - part) * rows + jnp.arange(rows, dtype=jnp.int32)
    key_cosine, key_sine = rotary_tables(jnp.concatenate([my_positions, far_positions]), HD)
    cosine, sine = key_cosine[:rows], key_sine[:rows]
    query, own_kv, hidden_one, start = project_qkv(start_recv, params, full_a, cosine, sine)
    query, sort_keys = together(query, sort_keys)
    sort_keys = lax.sort(sort_keys, dimension=1)
    far_kv = xor_narrow(own_kv, 1)
    mixed, logs = attend(query, own_kv, far_kv)
    mixed, sort_keys, hits, across_bc, *table_mine = together(
        mixed, sort_keys, hits, across_bc, *table_mine
    )
    full_bc = (wide_bc, xor_narrow(wide_bc, 1), across_bc, xor_narrow(across_bc, 1))
    tables = [gather_narrow(piece) for piece in table_mine]

    side = me // (wide // 2)
    low = me % (wide // 2)
    count_low = lax.dynamic_index_in_dim(
        lax.dynamic_index_in_dim(counts_all, low, 0, keepdims=False), micro, 0, keepdims=False
    )
    slot_row = lax.dynamic_index_in_dim(slots, micro, 0, keepdims=False)
    offset = jnp.arange(quarter, dtype=jnp.int32)
    order = jnp.concatenate(
        [
            s * (2 * quarter) + p * quarter + offset
            for p in (part, 1 - part)
            for s in (side, 1 - side)
        ]
    )
    from_low = order < count_low
    index = jnp.where(from_low, order, order - count_low)
    mine = from_low == (side == 0)
    wanted = jnp.sum(
        jnp.where(index[:, None] == jnp.arange(capacity)[None, :], slot_row[None, :], 0), axis=1
    )
    select = ((wanted[:, None] == my_positions[None, :]) & mine[:, None]).astype(BF)
    attended, middle, output, hidden_two, inner, picked = feed(
        mixed, start, params, full_a, full_bc, select
    )
    picked = picked[: 2 * quarter] + xor_narrow(picked[2 * quarter :], 1)
    row_part = picked[:quarter] + xor_wide(picked[quarter:], wide // 2)
    head_rows = spread_wide(row_part).reshape(wide * quarter, width)

    targets_mine = lax.dynamic_index_in_dim(targets_all, micro, 1, keepdims=False)
    counts_mine = lax.dynamic_index_in_dim(counts_all, micro, 1, keepdims=False)
    pairs = wide // 2
    both = jnp.concatenate([targets_mine[:pairs], targets_mine[pairs:]], axis=1)
    spot = jnp.stack([s * 2 * quarter + part * quarter + offset for s in (0, 1)])
    low_counts = counts_mine[:pairs, None, None]
    spot = jnp.where(spot[None] < low_counts, spot[None], capacity + spot[None] - low_counts)
    row_targets = jnp.sum(
        jnp.where(
            spot[..., None] == jnp.arange(2 * capacity)[None, None, None, :],
            both[:, None, None, :],
            0,
        ),
        axis=-1,
    )
    row_targets = row_targets.transpose(1, 0, 2).reshape(-1)
    target_owner = sum((row_targets >= k * entries).astype(jnp.int32) for k in range(1, narrow))
    target_rest = row_targets - target_owner * entries - me * chunk
    target_column = jnp.where(
        (target_rest >= 0) & (target_rest < chunk), (target_owner ^ group) * chunk + target_rest, -1
    )

    columns = [
        (slot, piece, slot * chunk + low + jnp.arange(high - low))
        for piece, (low, high) in enumerate(cuts)
        for slot in range(narrow)
    ]
    tables = [tables[piece][slot] for slot, piece, _ in columns]
    logits = [
        jnp.where(
            (me * chunk + at - slot * chunk < entries)[None, :], mm(head_rows, table, NN), -1e30
        )
        for table, (slot, _, at) in zip(tables, columns)
    ]
    hitting = [at[None, :] == target_column[:, None] for _, _, at in columns]
    top = functools.reduce(jnp.maximum, [jnp.max(value, axis=-1) for value in logits])
    total = sum(jnp.sum(jnp.exp(value - top[:, None]), axis=-1) for value in logits)
    target_logit = sum(
        jnp.sum(jnp.where(hit, value, 0.0), axis=-1) for hit, value in zip(hitting, logits)
    )
    stats = spread_wide(jnp.stack([top, total, target_logit]))
    top_all = jnp.max(stats[:, 0], axis=0)
    total_all = jnp.sum(stats[:, 1] * jnp.exp(stats[:, 0] - top_all[None]), axis=0)
    log_total = top_all + jnp.log(total_all)
    loss_part = jnp.sum(log_total - jnp.sum(stats[:, 2], axis=0))
    d_logits = [
        ((jnp.exp(value - log_total[:, None]) - hit.astype(F32)) * loss_scale).astype(BF)
        for hit, value in zip(hitting, logits)
    ]
    d_rows = sum(mm(grad, table, NT) for grad, table in zip(d_logits, tables))
    d_table_parts = [mm(head_rows, grad, TN) for grad in d_logits]
    d_recv = swap_wide(d_rows.astype(BF).reshape(wide, quarter, width))
    d_recv, *d_table_parts = together(d_recv, *d_table_parts)
    d_table_parts = [
        d_table_parts[piece * narrow : (piece + 1) * narrow] for piece in range(len(cuts))
    ]
    table_sent = [[xor_narrow(parts[s].astype(BF), 1) for s in (1, 3)] for parts in d_table_parts]
    d_mine = jnp.sum(d_recv.astype(F32), axis=0).astype(BF)
    d_sides = jnp.concatenate([d_mine, xor_wide(d_mine, wide // 2)])
    d_all = jnp.concatenate([d_sides, xor_narrow(d_sides, 1)])
    table_far = [
        (parts[2] + sent[1].astype(F32)).astype(BF)
        for parts, sent in zip(d_table_parts, table_sent)
    ]
    d_all, *table_far = together(d_all, *table_far)
    table_from = [xor_narrow(far, 2) for far in table_far]

    d_middle, d_attended, d_mixed, b_sent, c_sent, b_own, c_own, d_params = feed_back(
        d_all, select, params, middle, output, attended, hidden_two, inner, full_a, full_bc
    )
    def table_sum(piece):
        value = d_table_parts[piece][0] + table_sent[piece][0].astype(F32)
        value = (value + table_from[piece].astype(F32)).astype(BF)
        return value.reshape(wide, share, value.shape[1])

    d_query, d_own, d_far = attend_back(
        query, own_kv, far_kv, d_mixed, logs, cosine, sine, key_cosine, key_sine
    )
    d_query, d_own, d_far, b_sent, c_sent = together(d_query, d_own, d_far, b_sent, c_sent)
    b_near, b_far = scatter_core(b_sent, b_own)
    c_near, c_far = scatter_core(c_sent, c_own)
    d_query, d_own, d_far, *table_from = together(d_query, d_own, d_far, *table_from)
    d_far, b_far, c_far = together(xor_narrow(d_far, 1), b_far, c_far)
    b_from = xor_narrow(b_far, 2)
    c_pair = [
        scatter_pair(value.astype(F32).reshape(wide, share, width)) for value in (c_near, c_far)
    ]
    is_mask = (my_inputs == mask_entry).astype(F32)[:, None]
    d_start_rows, d_projected, d_first = qkv_back(
        d_query, d_own, d_far, full_a, d_middle, start, params, is_mask, rows + 16, wide
    )

    d_table = [table_sum(piece) for piece in range(len(cuts))]
    d_start_rows, d_projected, d_first, b_from, *c_pair = together(
        d_start_rows, d_projected, d_first, b_from, *c_pair
    )
    c_from = xor_narrow(c_pair[1].astype(BF), 2)
    a_sent, a_own = qkv_grads(d_projected, hidden_one, d_attended, mixed)
    a_near, a_far = scatter_core(a_sent, a_own)
    d_start_rows, d_first, c_from, *d_table = together(d_start_rows, d_first, c_from, *d_table)
    d_params = jnp.concatenate([d_first[:2], d_params[2:8], d_first[2:3], d_params[9:]])
    d_modulation = d_params[:8].reshape(-1)
    d_vector = jnp.concatenate([d_params[8:].reshape(-1), d_modulation])
    small = jnp.concatenate(
        [d_modulation.reshape(wide, -1, share), d_vector.reshape(wide, -1, share)], axis=1
    ).astype(BF)
    small = jnp.pad(small, ((0, 0), (0, padded - rows - 16 - small_rows), (0, 0)))
    d_start_rows = jnp.concatenate([d_start_rows, small], axis=1)
    d_start_recv = swap_wide(d_start_rows)
    a_from = xor_narrow(a_far, 2)
    b_half = scatter_pair((b_near + b_from.astype(F32)).reshape(wide, share, width))
    c_half = c_pair[0] + c_from.astype(F32)
    a_from, d_start_recv, b_half, c_half, *d_table = together(
        a_from, d_start_recv, b_half, c_half, *d_table
    )
    d_table = [swap_wide(piece) for piece in d_table]
    d_start_recv = d_start_recv.reshape(wide * padded, share)
    d_start_across = xor_narrow(d_start_recv, 2)
    d_near = (d_start_recv, xor_narrow(d_start_recv, 1))
    d_embed = collect(sort_keys[:2], hits[:2], d_near, shift, None, entries)
    d_start_across, d_embed = together(d_start_across, d_embed)
    d_start_corner = xor_narrow(d_start_across, 1)
    a_from, b_half, c_half, d_start_corner = together(a_from, b_half, c_half, d_start_corner)
    a_half = scatter_pair((a_near + a_from.astype(F32)).reshape(wide, share, width))
    d_b, d_c, d_a = scatter_line(b_half), scatter_line(c_half), scatter_line(a_half)
    d_far = (d_start_across, d_start_corner)
    d_embed = collect(sort_keys[2:], hits[2:], d_far, shift, d_embed, entries)
    d_embed, *d_table = together(d_embed, *d_table)
    d_table = jnp.concatenate(d_table, axis=2).astype(F32).transpose(1, 0, 2)
    d_table = d_table.reshape(share, chunk * wide)[:, :entries]

    small, small_far = [
        sum(
            part.reshape(wide, padded, share)[:, rows + 16 : rows + 16 + small_rows].astype(F32)
            for part in parts
        ).reshape(wide, -1)
        for parts in (d_near, d_far)
    ]
    d_vectors = jnp.sum(small[:, mod_share:] + small_far[:, mod_share:], axis=0)
    condition_far = lax.dynamic_index_in_dim(condition, 1 - micro, 1, keepdims=False)
    d_mod_weight = lax.dot_general(
        condition_mine, small[:, :mod_share], TN, precision=HIGHEST
    ) + lax.dot_general(condition_far, small_far[:, :mod_share], TN, precision=HIGHEST)

    shards = (
        d_embed,
        d_table,
        jnp.stack([d_a[:, k * heads_width : (k + 1) * heads_width] for k in range(3)]),
        flip(d_a[:, 3 * heads_width :]),
        d_b,
        d_c,
        d_mod_weight,
        d_vectors,
    )

    square = jnp.zeros((), F32)
    for grad in shards[:6]:
        square = square + jnp.sum(grad * grad)
    shared_square = jnp.sum(shards[6] * shards[6]) + jnp.sum(shards[7] * shards[7])
    square = square + shared_square / narrow
    sums = lax.all_to_all(
        jnp.broadcast_to(jnp.stack([loss_part / wide, square])[None, None], (wide * narrow, 1, 2)),
        ("wide",) + NARROW,
        0,
        0,
        tiled=True,
    )
    sums = jnp.sum(sums, axis=(0, 1))
    loss_sum = sums[0]
    grad_norm = jnp.sqrt(sums[1])
    factor = CLIP_NORM / jnp.maximum(grad_norm, CLIP_NORM)
    results = []
    for member in range(8):
        turn = (lambda value: value.T) if member in (0, 5) else (lambda value: value)
        master = turn(masters[member])
        grad = shards[member] * factor
        first = BETA_ONE * turn(firsts[member]) + (1.0 - BETA_ONE) * grad
        second = BETA_TWO * turn(seconds[member]) + (1.0 - BETA_TWO) * grad * grad
        stepped = (
            first / (1.0 - BETA_ONE**STEP) / (jnp.sqrt(second / (1.0 - BETA_TWO**STEP)) + ADAM_EPS)
        )
        decay = WEIGHT_DECAY if member < 7 else 0.0
        fresh = master - LEARN_RATES[member] * (stepped + decay * master)
        results.extend([turn(fresh), turn(first), turn(second)])
    return (loss_sum, grad_norm, *results)


def solution(mesh):
    shape = (mesh.shape["wide"], mesh.shape["narrow"] // 2, 2)
    mesh = jax.sharding.Mesh(mesh.devices.reshape(shape), ("wide",) + NARROW)
    weights = (
        P(NARROW, "wide"),
        P("wide", NARROW),
        P(None, "wide", NARROW),
        P(NARROW, "wide"),
        P("wide", NARROW),
        P(NARROW, "wide"),
        P(None, "wide"),
        P("wide"),
    )
    data = (P("wide", None, None), P("wide", None, None), P("wide", None))
    outs = [P(), P()]
    for spec in weights:
        outs.extend([spec] * 3)
    return jax.shard_map(
        local,
        mesh=mesh,
        in_specs=data + weights * 3,
        out_specs=tuple(outs),
        check_vma=False,
    )
```

```python
import functools
import math

import jax
import jax.numpy as jnp
from jax import lax
from jax.experimental import pallas as pl
from jax.experimental.pallas import tpu as pltpu
from jax.sharding import PartitionSpec as P

HD = 64
STEP = 10

HIGHEST = lax.Precision.HIGHEST
NORM_EPS = 1e-06
CLIP_NORM = 0.005
BETA_ONE = 0.9
BETA_TWO = 0.95
ADAM_EPS = 1e-08
WEIGHT_DECAY = 0.1
LEARN_RATES = (1.0, 0.1, 0.07, 0.5, 0.07, 0.04, 0.2, 0.5)
NARROW = ("line", "core")
BF = jnp.bfloat16
F32 = jnp.float32
VMEM_LIMIT = 56 * 1024 * 1024
FREE = pl.CostEstimate(flops=0, bytes_accessed=0, transcendentals=0)


def together(*values):
    return lax.optimization_barrier(values)


def xor_narrow(value, bits):
    return lax.ppermute(
        value, NARROW, [(i, i ^ bits) for i in range(lax.axis_size(NARROW))]
    )


def xor_wide(value, bits):
    return lax.ppermute(value, "wide", [(i, i ^ bits) for i in range(lax.axis_size("wide"))])


def swap_wide(value):
    return lax.all_to_all(value, "wide", 0, 0, tiled=True)


def spread_wide(value):
    if lax.axis_size("wide") > 8:
        return lax.all_gather(value, "wide")
    return swap_wide(jnp.broadcast_to(value[None], (lax.axis_size("wide"),) + value.shape))


def gather_wide(value, axis):
    return lax.all_gather(value, "wide", axis=axis, tiled=True)


def scatter_pair(value):
    count = lax.axis_size("wide")
    if count != 8:
        return value
    side = lax.axis_index("wide") & 1
    pairs = value.reshape((4, 2) + value.shape[1:])
    kept = lax.dynamic_index_in_dim(pairs, side, 1, keepdims=False)
    sent = lax.dynamic_index_in_dim(pairs, 1 - side, 1, keepdims=False).astype(BF)
    return kept + xor_wide(sent, 1).astype(F32)


def line_pieces(half):
    if lax.axis_size("wide") != 8:
        return [lax.psum_scatter(half, "wide", scatter_dimension=0)]
    depth = lax.axis_index("wide") >> 1
    low = half.astype(BF)
    return [lax.dynamic_index_in_dim(half, depth, 0, keepdims=False)] + [
        xor_wide(lax.dynamic_index_in_dim(low, depth ^ k, 0, keepdims=False), 2 * k)
        for k in (1, 2, 3)
    ]


def total_of(pieces):
    return sum(piece.astype(F32) for piece in pieces)


def scatter_line(half):
    return total_of(line_pieces(half))


def scatter_core(sent, own):
    from_core = xor_narrow(sent, 1).astype(F32)
    near = own[0].astype(F32) + from_core[0]
    far = own[1].astype(F32) + from_core[1]
    return near, far.astype(BF)


def gather_narrow(value):
    across = xor_narrow(value, 2)
    beside = xor_narrow(value, 1)
    corner = xor_narrow(across, 1)
    return value, beside, across, corner


def rounded(value):
    return lax.reduce_precision(value, exponent_bits=8, mantissa_bits=7)


def layer_norm(values):
    centered = values - jnp.mean(values, axis=-1, keepdims=True)
    inverse = lax.rsqrt(jnp.mean(centered * centered, axis=-1, keepdims=True) + NORM_EPS)
    return (centered * inverse, inverse)


def norm_back(grad, normed, inverse):
    return inverse * (
        grad
        - jnp.mean(grad, axis=-1, keepdims=True)
        - normed * jnp.mean(grad * normed, axis=-1, keepdims=True)
    )


def gelu_tanh(values):
    inner = 0.7978845608 * (values + 0.044715 * values * values * values)
    return 0.5 * values * (1.0 + jnp.tanh(inner))


def gelu_slope(values):
    tangent = jnp.tanh(0.7978845608 * (values + 0.044715 * values * values * values))
    return 0.5 * (1.0 + tangent) + 0.5 * values * (1.0 - tangent * tangent) * 0.7978845608 * (
        1.0 + 0.134145 * values * values
    )


def rotary_tables(positions, width):
    freqs = jnp.exp(jnp.arange(width // 2, dtype=F32) * (-2.0 * math.log(10000.0) / width))
    angle = positions.astype(F32)[:, None] * freqs[None, :]
    cosine, sine = jnp.cos(angle), jnp.sin(angle)
    return (
        jnp.concatenate([cosine] * 4, axis=1),
        jnp.concatenate([-sine, sine, -sine, sine], axis=1),
    )


def time_features(moment, width):
    freqs = jnp.exp(jnp.arange(width // 2, dtype=F32) * (-math.log(10000.0) / (width // 2)))
    angle = 1000.0 * moment[..., None] * freqs
    return jnp.concatenate([jnp.cos(angle), jnp.sin(angle)], axis=-1)


def turned(values, cosine, sine):
    blocks = []
    for place in range(0, values.shape[1], 2 * HD):
        block = values[:, place : place + 2 * HD]
        lanes = lax.broadcasted_iota(jnp.int32, block.shape, 1)
        ahead = pltpu.roll(block, 2 * HD - HD // 2, 1)
        behind = pltpu.roll(block, HD // 2, 1)
        other = jnp.where((lanes & (HD - 1)) < HD // 2, ahead, behind)
        blocks.append(block * cosine + other * sine)
    return jnp.concatenate(blocks, axis=1) if len(blocks) > 1 else blocks[0]


def turned_back(values, cosine, sine):
    spare = -values.shape[1] % (2 * HD)
    filled = jnp.concatenate([values, jnp.zeros((values.shape[0], spare), F32)], axis=1)
    return turned(filled, cosine, -sine)[:, : values.shape[1]]


NT = (((1,), (1,)), ((), ()))
NN = (((1,), (0,)), ((), ()))
TN = (((0,), (0,)), ((), ()))


def mm(a, b, dims):
    return lax.dot_general(a, b, dims, preferred_element_type=F32)


SHIFT_ONE, SCALE_ONE, GATE_ONE, SHIFT_TWO, SCALE_TWO, GATE_TWO, SHIFT_LAST, SCALE_LAST = range(8)
GAIN_ONE, GAIN_TWO, GAIN_LAST, BIAS_DOWN = range(8, 12)
LOCAL = dict(
    compiler_params=pltpu.CompilerParams(vmem_limit_bytes=60 * 1024 * 1024), cost_estimate=FREE
)
BUSY = dict(LOCAL, cost_estimate=pl.CostEstimate(10**10, 0, 4 * 10**7))


def column_sum(values):
    return jnp.sum(values, axis=0, keepdims=True)


def qkv_kernel(
    recv_ref, par_ref, a0, a1, a2, a3, cos_ref, sin_ref, q_ref, kv_ref, hidden_ref, start_ref
):
    par = lambda k: par_ref[k : k + 1, :]
    rows = start_ref.shape[0]
    start = jnp.concatenate(
        [recv_ref[piece, :rows, :].astype(F32) for piece in range(recv_ref.shape[0])], axis=1
    )
    start_ref[...] = start
    normed, _ = layer_norm(start)
    hidden = normed * par(GAIN_ONE) * (1.0 + par(SCALE_ONE)) + par(SHIFT_ONE)
    hidden = hidden.astype(BF)
    hidden_ref[...] = hidden
    share = q_ref.shape[2]
    for s, weight in enumerate((a0, a1, a2, a3)):
        value = mm(hidden, weight[...], NN)
        pair = turned(value[:, : 2 * share], cos_ref[...], sin_ref[...])
        q_ref[s] = pair[:, :share].astype(BF)
        kv_ref[s] = jnp.concatenate(
            [pair[:, share:], value[:, 2 * share : 3 * share]], axis=1
        ).astype(BF)


def project_qkv(recv, params, weights, cosine, sine):
    rows, width = cosine.shape[0], params.shape[1]
    share = width // 4
    return pl.pallas_call(
        qkv_kernel,
        out_shape=[
            jax.ShapeDtypeStruct((4, rows, share), BF),
            jax.ShapeDtypeStruct((4, rows, 2 * share), BF),
            jax.ShapeDtypeStruct((rows, width), BF),
            jax.ShapeDtypeStruct((rows, width), F32),
        ],
        name="qkv",
        **LOCAL,
    )(recv, params, *weights, cosine, sine)


def head_mask(values, head):
    lanes = lax.broadcasted_iota(jnp.int32, values.shape, 1)
    inside = (lanes >= head * HD) & (lanes < (head + 1) * HD)
    return jnp.where(inside, values, jnp.zeros_like(values))


def attend_kernel(q_ref, own_ref, far_ref, out_ref, log_ref):
    query = q_ref[0] * BF(HD**-0.5)
    share = query.shape[1]
    both = jnp.concatenate([own_ref[0], far_ref[0]], axis=0)
    keys, values = both[:, :share], both[:, share:].T
    parts = []
    for head in range(query.shape[1] // HD):
        scores = mm(keys, head_mask(query, head), NT)
        top = jnp.max(scores, axis=0, keepdims=True)
        shifted = jnp.exp(scores - top)
        total = jnp.sum(shifted, axis=0, keepdims=True)
        weights = (shifted * (1.0 / total)).astype(BF)
        parts.append(mm(values[head * HD : (head + 1) * HD], weights, NN))
        log_ref[0, head : head + 1, :] = top + jnp.log(total)
    out_ref[0] = jnp.concatenate(parts, axis=0).T.astype(BF)


def attend_specs(rows, share):
    return [
        pl.BlockSpec((1, rows, share), lambda s: (s, 0, 0)),
        pl.BlockSpec((1, rows, 2 * share), lambda s: (s, 0, 0)),
        pl.BlockSpec((1, rows, 2 * share), lambda s: (s ^ 1, 0, 0)),
    ]


def attend(query, own, far):
    slots, rows, share = query.shape
    heads = share // HD
    return pl.pallas_call(
        attend_kernel,
        grid=(slots,),
        in_specs=attend_specs(rows, share),
        out_specs=[
            pl.BlockSpec((1, rows, share), lambda s: (s, 0, 0)),
            pl.BlockSpec((1, heads, rows), lambda s: (s, 0, 0)),
        ],
        out_shape=[
            jax.ShapeDtypeStruct((slots, rows, share), BF),
            jax.ShapeDtypeStruct((slots, heads, rows), F32),
        ],
        name="attend",
        **LOCAL,
    )(query, own, far)


def feed_kernel(
    mixed_ref, start_ref, par_ref, a0, a1, a2, a3, bc0, bc1, bc2, bc3, select_ref,
    attended_ref, middle_ref, output_ref, hidden_ref, inner_ref, picked_ref,
):
    par = lambda k: par_ref[k : k + 1, :]
    share = mixed_ref.shape[2]
    attended = sum(
        mm(mixed_ref[s], weight[:, 3 * share :], NT) for s, weight in enumerate((a0, a1, a2, a3))
    )
    attended_ref[...] = attended
    middle = start_ref[...] + par(GATE_ONE) * attended
    middle_ref[...] = middle
    normed, _ = layer_norm(middle)
    hidden = normed * par(GAIN_TWO) * (1.0 + par(SCALE_TWO)) + par(SHIFT_TWO)
    hidden = hidden.astype(BF)
    hidden_ref[...] = hidden
    output = jnp.zeros(middle.shape, F32)
    for s, weight in enumerate((bc0, bc1, bc2, bc3)):
        inner = mm(hidden, weight[0], NN)
        inner_ref[s] = inner
        output = output + mm(gelu_tanh(inner).astype(BF), weight[1], NT)
    output_ref[...] = output
    final = middle + par(GATE_TWO) * (output + par(BIAS_DOWN))
    normed, _ = layer_norm(final)
    last = normed * (par(GAIN_LAST) * (1.0 + par(SCALE_LAST))) + par(SHIFT_LAST)
    picked_ref[...] = mm(select_ref[...], last.astype(BF), NN).astype(BF)


def feed(mixed, start, params, weights_a, weights_bc, select):
    rows, width = start.shape
    plain = jax.ShapeDtypeStruct((rows, width), F32)
    return pl.pallas_call(
        feed_kernel,
        out_shape=[
            plain,
            plain,
            plain,
            jax.ShapeDtypeStruct((rows, width), BF),
            jax.ShapeDtypeStruct((4, rows, width), F32),
            jax.ShapeDtypeStruct((select.shape[0], width), BF),
        ],
        name="feed",
        **LOCAL,
    )(mixed, start, params, *weights_a, *weights_bc, select)


SLOT_PLACES = ((1, 0, 0), (3, 0, 1), (0, 1, 0), (2, 1, 1))


def feed_back_kernel(
    rows_ref, select_ref, par_ref, middle_ref, output_ref, attended_ref, hidden_ref, inner_ref,
    a0, a1, a2, a3, bc0, bc1, bc2, bc3,
    d_middle_ref, d_attended_ref, d_mixed_ref, b_sent_ref, c_sent_ref, b_own_ref, c_own_ref,
    vec_ref,
):
    par = lambda k: par_ref[k : k + 1, :]
    share = d_mixed_ref.shape[2]
    middle, output = middle_ref[...], output_ref[...]
    d_hidden = mm(select_ref[...], rows_ref[...], TN)
    final = middle + par(GATE_TWO) * (output + par(BIAS_DOWN))
    normed, inverse = layer_norm(final)
    d_normed = column_sum(d_hidden * normed)
    vec_ref[SHIFT_LAST : SHIFT_LAST + 1, :] = column_sum(d_hidden)
    vec_ref[SCALE_LAST : SCALE_LAST + 1, :] = d_normed * par(GAIN_LAST)
    vec_ref[GAIN_LAST : GAIN_LAST + 1, :] = d_normed * (1.0 + par(SCALE_LAST))
    d_final = norm_back(d_hidden * (par(GAIN_LAST) * (1.0 + par(SCALE_LAST))), normed, inverse)
    vec_ref[BIAS_DOWN : BIAS_DOWN + 1, :] = column_sum(d_final) * par(GATE_TWO)
    vec_ref[GATE_TWO : GATE_TWO + 1, :] = column_sum(d_final * (output + par(BIAS_DOWN)))
    d_output = (d_final * par(GATE_TWO)).astype(BF)
    hidden = hidden_ref[...]
    d_hidden = jnp.zeros(middle.shape, F32)
    weights = (bc0, bc1, bc2, bc3)
    for s, kept, place in SLOT_PLACES:
        b_ref, c_ref = (b_own_ref, c_own_ref) if kept else (b_sent_ref, c_sent_ref)
        inner = inner_ref[s]
        tangent = jnp.tanh(0.7978845608 * (inner + 0.044715 * inner * inner * inner))
        active = (0.5 * inner * (1.0 + tangent)).astype(BF)
        slope = 0.5 * (1.0 + tangent) + 0.5 * inner * (
            1.0 - tangent * tangent
        ) * 0.7978845608 * (1.0 + 0.134145 * inner * inner)
        d_inner = (mm(d_output, weights[s][1], NN) * slope).astype(BF)
        b_ref[place] = mm(hidden, d_inner, TN).astype(BF)
        c_ref[place] = mm(d_output, active, TN).astype(BF)
        d_hidden = d_hidden + mm(d_inner, weights[s][0], NT)
    normed, inverse = layer_norm(middle)
    d_normed = column_sum(d_hidden * normed)
    vec_ref[SHIFT_TWO : SHIFT_TWO + 1, :] = column_sum(d_hidden)
    vec_ref[SCALE_TWO : SCALE_TWO + 1, :] = d_normed * par(GAIN_TWO)
    vec_ref[GAIN_TWO : GAIN_TWO + 1, :] = d_normed * (1.0 + par(SCALE_TWO))
    d_middle = d_final + norm_back(
        d_hidden * par(GAIN_TWO) * (1.0 + par(SCALE_TWO)), normed, inverse
    )
    d_middle_ref[...] = d_middle
    vec_ref[GATE_ONE : GATE_ONE + 1, :] = column_sum(d_middle * attended_ref[...])
    d_attended = (d_middle * par(GATE_ONE)).astype(BF)
    d_attended_ref[...] = d_attended
    for s, weight in enumerate((a0, a1, a2, a3)):
        d_mixed_ref[s] = mm(d_attended, weight[:, 3 * share :], NN).astype(BF)
    for unused in (SHIFT_ONE, SCALE_ONE, GAIN_ONE):
        vec_ref[unused : unused + 1, :] = jnp.zeros_like(par(0))


def feed_back(
    d_rows, select, params, middle, output, attended, hidden, inner, weights_a, weights_bc
):
    rows, width = middle.shape
    half = jax.ShapeDtypeStruct((2, width, width), BF)
    return pl.pallas_call(
        feed_back_kernel,
        out_shape=[
            jax.ShapeDtypeStruct((rows, width), F32),
            jax.ShapeDtypeStruct((rows, width), BF),
            jax.ShapeDtypeStruct((4, rows, width // 4), BF),
            half,
            half,
            half,
            half,
            jax.ShapeDtypeStruct(params.shape, F32),
        ],
        name="feed_back",
        **BUSY,
    )(
        d_rows, select, params, middle, output, attended, hidden, inner, *weights_a, *weights_bc
    )


def attend_back_kernel(
    q_ref, own_ref, far_ref, grad_ref, log_ref, cos_ref, sin_ref, kcos_ref, ksin_ref,
    dq_ref, d_own_ref, d_far_ref,
):
    query, grad = q_ref[0], grad_ref[0]
    share = query.shape[1]
    both = jnp.concatenate([own_ref[0], far_ref[0]], axis=0)
    keys, values = both[:, :share], both[:, share:]
    turned_keys = keys.T
    scale = HD**-0.5
    rows = query.shape[0]
    dq = []
    dk = jnp.zeros(keys.shape, F32)
    dv = jnp.zeros(keys.shape, F32)
    for head in range(query.shape[1] // HD):
        query_one = head_mask(query * BF(scale), head)
        grad_one = head_mask(grad, head)
        scores = mm(keys, query_one, NT)
        weights = jnp.exp(scores - log_ref[0, head : head + 1, :])
        d_weights = mm(values, grad_one, NT)
        delta = jnp.sum(weights * d_weights, axis=0, keepdims=True)
        d_scores = (weights * (d_weights - delta)).astype(BF)
        dq.append(mm(turned_keys[head * HD : (head + 1) * HD], d_scores, NN))
        dk = dk + mm(d_scores, query_one, NN)
        dv = dv + mm(weights.astype(BF), grad_one, NN)
    dq = jnp.concatenate(dq, axis=0).T * scale
    dq_ref[0] = turned_back(dq, cos_ref[...], sin_ref[...]).astype(BF)
    dk = turned_back(dk, kcos_ref[...], ksin_ref[...])
    both = jnp.concatenate([dk, dv], axis=1)
    d_own_ref[0] = both[:rows]
    d_far_ref[0] = both[rows:].astype(BF)


def attend_back(query, own, far, grad, logs, cosine, sine, key_cosine, key_sine):
    slots, rows, share = query.shape
    heads = share // HD
    whole = lambda table: pl.BlockSpec(table.shape, lambda s: (0, 0))
    one, two, other = attend_specs(rows, share)
    return pl.pallas_call(
        attend_back_kernel,
        grid=(slots,),
        in_specs=[
            one, two, other, one, pl.BlockSpec((1, heads, rows), lambda s: (s, 0, 0)),
            whole(cosine), whole(sine), whole(key_cosine), whole(key_sine),
        ],
        out_specs=[one, two, two],
        out_shape=[
            jax.ShapeDtypeStruct((slots, rows, share), BF),
            jax.ShapeDtypeStruct((slots, rows, 2 * share), F32),
            jax.ShapeDtypeStruct((slots, rows, 2 * share), BF),
        ],
        name="attend_back",
        **LOCAL,
    )(query, own, far, grad, logs, cosine, sine, key_cosine, key_sine)


def slot_grads(dq_ref, d_own_ref, d_far_ref, s):
    return jnp.concatenate(
        [
            dq_ref[s],
            (d_own_ref[s] + d_far_ref[s ^ 1].astype(F32)).astype(BF),
        ],
        axis=1,
    )


def qkv_back_kernel(
    dq_ref, d_own_ref, d_far_ref, a0, a1, a2, a3, d_middle_ref, start_ref, par_ref, mask_ref,
    out_ref, grads_ref, vec_ref,
):
    par = lambda k: par_ref[k : k + 1, :]
    share = dq_ref.shape[2]
    rows = start_ref.shape[0]
    d_hidden = jnp.zeros(start_ref.shape, F32)
    for s, weight in enumerate((a0, a1, a2, a3)):
        grads = slot_grads(dq_ref, d_own_ref, d_far_ref, s)
        grads_ref[s] = grads
        d_hidden = d_hidden + mm(grads, weight[:, : 3 * share], NT)
    normed, inverse = layer_norm(start_ref[...])
    d_normed = column_sum(d_hidden * normed)
    vec_ref[0:1, :] = column_sum(d_hidden)
    vec_ref[1:2, :] = d_normed * par(GAIN_ONE)
    vec_ref[2:3, :] = d_normed * (1.0 + par(SCALE_ONE))
    d_start = d_middle_ref[...] + norm_back(
        d_hidden * par(GAIN_ONE) * (1.0 + par(SCALE_ONE)), normed, inverse
    )
    masked = column_sum(d_start * mask_ref[...])
    extra = out_ref.shape[1] - rows
    first = lax.broadcasted_iota(jnp.int32, (extra, 1), 0) == 0
    whole = jnp.concatenate([d_start, jnp.where(first, masked, 0.0)], axis=0).astype(BF)
    columns = out_ref.shape[2]
    for piece in range(out_ref.shape[0]):
        out_ref[piece] = whole[:, piece * columns : (piece + 1) * columns]


def qkv_back(dq, d_own, d_far, weights, d_middle, start, params, is_mask, padded, wide):
    rows, width = start.shape
    return pl.pallas_call(
        qkv_back_kernel,
        out_shape=[
            jax.ShapeDtypeStruct((wide, padded, width // wide), BF),
            jax.ShapeDtypeStruct((4, rows, 3 * width // 4), BF),
            jax.ShapeDtypeStruct((3, width), F32),
        ],
        name="qkv_back",
        **LOCAL,
    )(dq, d_own, d_far, *weights, d_middle, start, params, is_mask)


def flip(value):
    def kernel(value_ref, out_ref):
        out_ref[...] = value_ref[...].T

    return pl.pallas_call(
        kernel, out_shape=jax.ShapeDtypeStruct(value.shape[::-1], value.dtype), name="flip", **LOCAL
    )(value)


def qkv_grads_kernel(grads_ref, hidden_ref, d_attended_ref, mixed_ref, sent_ref, own_ref):
    for s, kept, place in SLOT_PLACES:
        out_ref = own_ref if kept else sent_ref
        out_ref[place] = jnp.concatenate(
            [
                mm(hidden_ref[...], grads_ref[s], TN),
                mm(d_attended_ref[...], mixed_ref[s], TN),
            ],
            axis=1,
        ).astype(BF)


def qkv_grads(grads, hidden, d_attended, mixed):
    width = hidden.shape[1]
    half = jax.ShapeDtypeStruct((2, width, width), BF)
    return pl.pallas_call(
        qkv_grads_kernel, out_shape=[half, half], name="qkv_grads", **BUSY
    )(grads, hidden, d_attended, mixed)


def rows_kernel(own_ref, other_ref, out_ref):
    step = pl.program_id(0)
    half = pl.num_programs(0) // 2

    @pl.when(step < half)
    def _():
        out_ref[...] = own_ref[...].astype(BF).T.astype(F32)

    @pl.when((step >= half) & (step < 2 * half))
    def _():
        out_ref[...] = other_ref[...].T.astype(F32)

    @pl.when(step == 2 * half)
    def _():
        out_ref[...] = jnp.zeros_like(out_ref)


def table_rows_of(own, other):
    width, entries = own.shape
    block = next(b for b in (1408, 1152, 384, 128) if entries % b == 0)
    half = entries // block
    return pl.pallas_call(
        rows_kernel,
        grid=(2 * half + 1,),
        in_specs=[
            pl.BlockSpec((width, block), lambda i: (0, jnp.minimum(i, half - 1))),
            pl.BlockSpec((width, block), lambda i: (0, jnp.clip(i - half, 0, half - 1))),
        ],
        out_specs=pl.BlockSpec((block, width), lambda i: (i, 0)),
        out_shape=jax.ShapeDtypeStruct((2 * entries + block, width), F32),
        name="table_rows",
        **BUSY,
    )(own, other)


def lookup_kernel(id_ref, table_ref, out_ref, scratch):
    block = scratch.shape[0]
    unroll = 16

    def body(step, _):
        for k in range(unroll):
            place = step * unroll + k
            scratch[pl.ds(place, 1), :] = table_ref[pl.ds(id_ref[0, 0, place], 1), :]
        return 0

    lax.fori_loop(0, block // unroll, body, 0)
    out_ref[...] = scratch[...].astype(BF)


def lookup(table, ids):
    count = ids.shape[0]
    block = min(2048, count)
    width = table.shape[1]
    return pl.pallas_call(
        lookup_kernel,
        grid=(count // block,),
        in_specs=[
            pl.BlockSpec((1, 1, block), lambda i: (i, 0, 0), memory_space=pltpu.SMEM),
            pl.BlockSpec(table.shape, lambda i: (0, 0), pipeline_mode=pl.Buffered(1)),
        ],
        out_specs=pl.BlockSpec((block, width), lambda i: (i, 0)),
        out_shape=jax.ShapeDtypeStruct((count, width), BF),
        scratch_shapes=[pltpu.VMEM((block, width), F32)],
        name="lookup",
        **LOCAL,
    )(ids.reshape(count // block, 1, block), table)


def collect_kernel(shift, first, key_ref, count_ref, one_ref, two_ref, *refs):
    if first:
        out_ref, rows_ref = refs
        sum_ref = out_ref
        sum_ref[...] = jnp.zeros_like(sum_ref)
    else:
        old_ref, out_ref, rows_ref, sum_ref = refs
        sum_ref[...] = old_ref[...]
    mask = (1 << shift) - 1
    unroll = 8
    for part, grad_ref in enumerate((one_ref, two_ref)):
        rows_ref[...] = grad_ref[...].astype(F32)
        count = count_ref[part]

        def group(item, _, part=part):
            keys = [key_ref[part, item * unroll + k] for k in range(unroll)]
            targets = [lax.shift_right_logical(key, shift) for key in keys]
            olds = [sum_ref[pl.ds(target, 1), :] for target in targets]
            news = [rows_ref[pl.ds(key & mask, 1), :] for key in keys]
            sums = []
            for k in range(unroll):
                old = olds[k]
                if k:
                    old = jnp.where(targets[k] == targets[k - 1], sums[k - 1], old)
                sums.append(old + news[k])
            for k in range(unroll):
                sum_ref[pl.ds(targets[k], 1), :] = sums[k]
            return 0

        def single(item, _, part=part):
            key = key_ref[part, item]
            target = pl.ds(lax.shift_right_logical(key, shift), 1)
            sum_ref[target, :] = sum_ref[target, :] + rows_ref[pl.ds(key & mask, 1), :]
            return 0

        groups = lax.shift_right_logical(count, 3)
        lax.fori_loop(0, groups, group, 0)
        lax.fori_loop(groups * unroll, count, single, 0)

    if not first:

        def turn(block, _):
            place = pl.ds(pl.multiple_of(block * 128, 128), 128)
            out_ref[:, place] = sum_ref[place, :].T
            return 0

        lax.fori_loop(0, sum_ref.shape[0] // 128, turn, 0)


def collect(keys, counts, grads, shift, before, entries):
    tokens, width = grads[0].shape
    first = before is None
    out_dims = (entries, width) if first else (width, entries)
    scratch = [pltpu.VMEM((tokens, width), F32)]
    if not first:
        scratch.append(pltpu.VMEM((entries, width), F32))
    smem = pl.BlockSpec(memory_space=pltpu.SMEM)
    vmem = pl.BlockSpec(memory_space=pltpu.VMEM)
    return pl.pallas_call(
        functools.partial(collect_kernel, shift, first),
        in_specs=[smem, smem] + [vmem] * (2 if first else 3),
        out_specs=vmem,
        out_shape=jax.ShapeDtypeStruct(out_dims, F32),
        scratch_shapes=scratch,
        name="collect",
        **LOCAL,
    )(keys, counts, *grads, *([] if first else [before]))


def local(
    token_ids, mask_slots, mask_counts,
    embedding, out_table, qkv_weight, proj_weight, up_weight, down_weight, mod_weight, vectors,
    embedding_first, out_table_first, qkv_first, proj_first, up_first, down_first, mod_first,
    vectors_first,
    embedding_second, out_table_second, qkv_second, proj_second, up_second, down_second,
    mod_second, vectors_second,
):
    masters = (
        embedding, out_table, qkv_weight, proj_weight, up_weight, down_weight, mod_weight, vectors,
    )
    firsts = (
        embedding_first, out_table_first, qkv_first, proj_first, up_first, down_first, mod_first,
        vectors_first,
    )
    seconds = (
        embedding_second, out_table_second, qkv_second, proj_second, up_second, down_second,
        mod_second, vectors_second,
    )
    wide = lax.axis_size("wide")
    narrow = lax.axis_size(NARROW)
    me = lax.axis_index("wide")
    group = lax.axis_index(NARROW)
    part = group & 1
    micro = group >> 1
    entries, share = embedding.shape
    width = share * wide
    vocab = entries * narrow
    micro_count, length = token_ids.shape[1:]
    capacity = mask_slots.shape[2]
    rows = length // 2
    pair_total = 5 * length // 16
    quarter = pair_total // 4
    loss_scale = 1.0 / (length * micro_count * wide)
    positions = jnp.arange(length, dtype=jnp.int32)

    tokens, slots, counts = token_ids[0], mask_slots[0], mask_counts[0]
    at_slot = slots[:, :, None] == positions[None, None, :]
    valid = jnp.arange(capacity)[None, :] < counts[:, None]
    masked = jnp.any(at_slot & valid[:, :, None], axis=1)
    targets = jnp.sum(jnp.where(at_slot, tokens[:, None, :], 0), axis=2)
    inputs = jnp.where(masked, vocab - 1, tokens)
    packed = jnp.concatenate(
        [inputs, targets, jnp.broadcast_to(counts[:, None], (micro_count, 128))], axis=1
    )
    packed_all = spread_wide(packed)
    inputs_all = packed_all[:, :, :length]
    targets_all = packed_all[:, :, length : length + capacity]
    counts_all = packed_all[:, :, length + capacity]

    shard_a = jnp.concatenate(
        [qkv_weight[0], qkv_weight[1], qkv_weight[2], proj_weight.T], axis=1
    ).astype(BF)
    wide_all = gather_wide(
        jnp.stack([shard_a, up_weight.astype(BF), down_weight.T.astype(BF)]), 1
    )
    wide_a, wide_bc = wide_all[0], wide_all[1:]
    heads_width = width // narrow

    chunk = -(-entries // (128 * wide)) * 128
    spare = chunk * wide - entries
    table_own = jnp.pad(out_table.astype(BF), ((0, 0), (0, spare)))
    table_own = table_own.reshape(share, wide, chunk).transpose(1, 0, 2)
    cuts = [(0, chunk)]
    table_own = [table_own[:, :, low:high] for low, high in cuts]

    moments = counts_all.astype(F32) / pair_total
    condition = jax.nn.silu(time_features(moments, mod_weight.shape[0]))
    condition_mine = lax.dynamic_index_in_dim(condition, micro, 1, keepdims=False)
    mod_part = jnp.dot(condition_mine, rounded(mod_weight), precision=HIGHEST)
    mod_share = mod_part.shape[1]
    exact = []
    rest = mod_part
    for _ in range(3):
        exact.append(rounded(rest))
        rest = rest - exact[-1]
    extra = jnp.concatenate(
        exact + [jnp.broadcast_to(rounded(vectors), (wide, vectors.shape[0]))], axis=1
    ).astype(BF)
    extra_rows = extra.shape[1] // share
    extra = extra.reshape(wide, extra_rows, share)
    extra = jnp.pad(extra, ((0, 0), (0, -extra_rows % 16), (0, 0)))

    table_rows = table_rows_of(embedding.T, xor_narrow(embedding.T.astype(BF), 1))
    half_ids = lax.dynamic_slice_in_dim(inputs_all, part * rows, rows, axis=2)
    half_ids = jnp.stack(
        [
            lax.dynamic_index_in_dim(half_ids, micro, 1, keepdims=False),
            lax.dynamic_index_in_dim(half_ids, 1 - micro, 1, keepdims=False),
        ]
    )
    inside, beside = half_ids - group * entries, half_ids - (group ^ 1) * entries
    inside_here = (inside >= 0) & (inside < entries)
    beside_here = (beside >= 0) & (beside < entries)
    places = jnp.where(
        inside_here, inside, jnp.where(beside_here, beside + entries, 2 * entries)
    )
    looked = lookup(table_rows, places.reshape(-1))
    looked = looked.reshape(2, wide, rows, share)
    start_part = looked[0] + xor_narrow(looked[1], 2)
    start_recv_in = jnp.concatenate([start_part, extra], axis=1)
    start_recv_in, wide_a = together(start_recv_in, wide_a)
    full_a = gather_narrow(wide_a)
    start_recv = swap_wide(start_recv_in)

    my_inputs = lax.dynamic_slice_in_dim(
        lax.dynamic_index_in_dim(inputs, micro, 0, keepdims=False), part * rows, rows, axis=0
    )
    small_rows = (9 * width + 3 * width + 8 * width) // wide // share
    padded = rows + 16 + -(-small_rows // 16) * 16
    padded = rows + 16 + 32
    mask_entry = vocab - 1
    ids = jnp.stack(
        [
            lax.dynamic_slice_in_dim(
                lax.dynamic_index_in_dim(inputs_all, (group ^ s) >> 1, 1, keepdims=False),
                ((group ^ s) & 1) * rows,
                rows,
                axis=1,
            )
            for s in range(narrow)
        ]
    )
    ids = jnp.concatenate(
        [
            jnp.where(ids == mask_entry, -1, ids),
            jnp.full((narrow, wide, 1), mask_entry, jnp.int32),
            jnp.full((narrow, wide, padded - rows - 1), -1, jnp.int32),
        ],
        axis=2,
    ).reshape(narrow, wide * padded)
    local_ids = ids - group * entries
    taken = (local_ids >= 0) & (local_ids < entries)
    shift = (wide * padded - 1).bit_length()
    sort_keys = jnp.where(
        taken,
        local_ids * (1 << shift) + jnp.arange(wide * padded, dtype=jnp.int32)[None, :],
        jnp.iinfo(jnp.int32).max,
    )
    hits = jnp.sum(taken.astype(jnp.int32), axis=1)
    wide_bc, *full_a = together(wide_bc, *full_a)
    start_recv, *table_own = together(start_recv, *table_own)
    table_mine = [
        swap_wide(piece).reshape(width, high - low) for piece, (low, high) in zip(table_own, cuts)
    ]
    across_bc = xor_narrow(wide_bc, 2)
    extra = start_recv[:, rows : rows + extra_rows].astype(F32).reshape(wide, -1)
    vector_full = extra[:, 3 * mod_share :].reshape(-1)
    modulation = extra[:, :mod_share] + extra[:, mod_share : 2 * mod_share]
    modulation = (modulation + extra[:, 2 * mod_share : 3 * mod_share]).reshape(-1)
    modulation = modulation + vector_full[4 * width :]
    params = jnp.concatenate(
        [modulation.reshape(8, width), vector_full[: 4 * width].reshape(4, width)]
    )

    my_positions = part * rows + jnp.arange(rows, dtype=jnp.int32)
    far_positions = (1 - part) * rows + jnp.arange(rows, dtype=jnp.int32)
    key_cosine, key_sine = rotary_tables(jnp.concatenate([my_positions, far_positions]), HD)
    cosine, sine = key_cosine[:rows], key_sine[:rows]
    query, own_kv, hidden_one, start = project_qkv(start_recv, params, full_a, cosine, sine)
    query, sort_keys = together(query, sort_keys)
    sort_keys = lax.sort(sort_keys, dimension=1)
    far_kv = xor_narrow(own_kv, 1)
    mixed, logs = attend(query, own_kv, far_kv)
    mixed, sort_keys, hits, across_bc, *table_mine = together(
        mixed, sort_keys, hits, across_bc, *table_mine
    )
    full_bc = (wide_bc, xor_narrow(wide_bc, 1), across_bc, xor_narrow(across_bc, 1))
    tables = [gather_narrow(piece) for piece in table_mine]

    side = me // (wide // 2)
    low = me % (wide // 2)
    count_low = lax.dynamic_index_in_dim(
        lax.dynamic_index_in_dim(counts_all, low, 0, keepdims=False), micro, 0, keepdims=False
    )
    slot_row = lax.dynamic_index_in_dim(slots, micro, 0, keepdims=False)
    offset = jnp.arange(quarter, dtype=jnp.int32)
    order = jnp.concatenate(
        [
            s * (2 * quarter) + p * quarter + offset
            for p in (part, 1 - part)
            for s in (side, 1 - side)
        ]
    )
    from_low = order < count_low
    index = jnp.where(from_low, order, order - count_low)
    mine = from_low == (side == 0)
    wanted = jnp.sum(
        jnp.where(index[:, None] == jnp.arange(capacity)[None, :], slot_row[None, :], 0), axis=1
    )
    select = ((wanted[:, None] == my_positions[None, :]) & mine[:, None]).astype(BF)
    attended, middle, output, hidden_two, inner, picked = feed(
        mixed, start, params, full_a, full_bc, select
    )
    picked = picked[: 2 * quarter] + xor_narrow(picked[2 * quarter :], 1)
    row_part = picked[:quarter] + xor_wide(picked[quarter:], wide // 2)
    head_rows = spread_wide(row_part).reshape(wide * quarter, width)

    targets_mine = lax.dynamic_index_in_dim(targets_all, micro, 1, keepdims=False)
    counts_mine = lax.dynamic_index_in_dim(counts_all, micro, 1, keepdims=False)
    pairs = wide // 2
    both = jnp.concatenate([targets_mine[:pairs], targets_mine[pairs:]], axis=1)
    spot = jnp.stack([s * 2 * quarter + part * quarter + offset for s in (0, 1)])
    low_counts = counts_mine[:pairs, None, None]
    spot = jnp.where(spot[None] < low_counts, spot[None], capacity + spot[None] - low_counts)
    row_targets = jnp.sum(
        jnp.where(
            spot[..., None] == jnp.arange(2 * capacity)[None, None, None, :],
            both[:, None, None, :],
            0,
        ),
        axis=-1,
    )
    row_targets = row_targets.transpose(1, 0, 2).reshape(-1)
    target_owner = sum((row_targets >= k * entries).astype(jnp.int32) for k in range(1, narrow))
    target_rest = row_targets - target_owner * entries - me * chunk
    target_column = jnp.where(
        (target_rest >= 0) & (target_rest < chunk), (target_owner ^ group) * chunk + target_rest, -1
    )

    columns = [
        (slot, piece, slot * chunk + low + jnp.arange(high - low))
        for piece, (low, high) in enumerate(cuts)
        for slot in range(narrow)
    ]
    tables = [tables[piece][slot] for slot, piece, _ in columns]
    logits = [
        jnp.where(
            (me * chunk + at - slot * chunk < entries)[None, :], mm(head_rows, table, NN), -1e30
        )
        for table, (slot, _, at) in zip(tables, columns)
    ]
    hitting = [at[None, :] == target_column[:, None] for _, _, at in columns]
    top = functools.reduce(jnp.maximum, [jnp.max(value, axis=-1) for value in logits])
    total = sum(jnp.sum(jnp.exp(value - top[:, None]), axis=-1) for value in logits)
    target_logit = sum(
        jnp.sum(jnp.where(hit, value, 0.0), axis=-1) for hit, value in zip(hitting, logits)
    )
    stats = spread_wide(jnp.stack([top, total, target_logit]))
    top_all = jnp.max(stats[:, 0], axis=0)
    total_all = jnp.sum(stats[:, 1] * jnp.exp(stats[:, 0] - top_all[None]), axis=0)
    log_total = top_all + jnp.log(total_all)
    loss_part = jnp.sum(log_total - jnp.sum(stats[:, 2], axis=0))
    d_logits = [
        ((jnp.exp(value - log_total[:, None]) - hit.astype(F32)) * loss_scale).astype(BF)
        for hit, value in zip(hitting, logits)
    ]
    d_rows = sum(mm(grad, table, NT) for grad, table in zip(d_logits, tables))
    d_table_parts = [mm(head_rows, grad, TN) for grad in d_logits]
    d_recv = swap_wide(d_rows.astype(BF).reshape(wide, quarter, width))
    d_recv, *d_table_parts = together(d_recv, *d_table_parts)
    d_table_parts = [
        d_table_parts[piece * narrow : (piece + 1) * narrow] for piece in range(len(cuts))
    ]
    table_sent = [[xor_narrow(parts[s].astype(BF), 1) for s in (1, 3)] for parts in d_table_parts]
    d_mine = jnp.sum(d_recv.astype(F32), axis=0).astype(BF)
    d_sides = jnp.concatenate([d_mine, xor_wide(d_mine, wide // 2)])
    d_all = jnp.concatenate([d_sides, xor_narrow(d_sides, 1)])
    table_far = [
        (parts[2] + sent[1].astype(F32)).astype(BF)
        for parts, sent in zip(d_table_parts, table_sent)
    ]
    d_all, *table_far = together(d_all, *table_far)
    table_from = [xor_narrow(far, 2) for far in table_far]

    d_middle, d_attended, d_mixed, b_sent, c_sent, b_own, c_own, d_params = feed_back(
        d_all, select, params, middle, output, attended, hidden_two, inner, full_a, full_bc
    )
    def table_sum(piece):
        value = d_table_parts[piece][0] + table_sent[piece][0].astype(F32)
        value = (value + table_from[piece].astype(F32)).astype(BF)
        return value.reshape(wide, share, value.shape[1])

    d_query, d_own, d_far = attend_back(
        query, own_kv, far_kv, d_mixed, logs, cosine, sine, key_cosine, key_sine
    )
    d_query, d_own, d_far, b_sent, c_sent = together(d_query, d_own, d_far, b_sent, c_sent)
    b_near, b_far = scatter_core(b_sent, b_own)
    c_near, c_far = scatter_core(c_sent, c_own)
    d_query, d_own, d_far, *table_from = together(d_query, d_own, d_far, *table_from)
    d_far, b_far, c_far = together(xor_narrow(d_far, 1), b_far, c_far)
    b_from = xor_narrow(b_far, 2)
    c_pair = [
        scatter_pair(value.astype(F32).reshape(wide, share, width)) for value in (c_near, c_far)
    ]
    is_mask = (my_inputs == mask_entry).astype(F32)[:, None]
    d_start_rows, d_projected, d_first = qkv_back(
        d_query, d_own, d_far, full_a, d_middle, start, params, is_mask, rows + 16, wide
    )

    d_table = [table_sum(piece) for piece in range(len(cuts))]
    d_start_rows, d_projected, d_first, b_from, *c_pair = together(
        d_start_rows, d_projected, d_first, b_from, *c_pair
    )
    c_from = xor_narrow(c_pair[1].astype(BF), 2)
    a_sent, a_own = qkv_grads(d_projected, hidden_one, d_attended, mixed)
    a_near, a_far = scatter_core(a_sent, a_own)
    d_start_rows, d_first, c_from, *d_table = together(d_start_rows, d_first, c_from, *d_table)
    d_params = jnp.concatenate([d_first[:2], d_params[2:8], d_first[2:3], d_params[9:]])
    d_modulation = d_params[:8].reshape(-1)
    d_vector = jnp.concatenate([d_params[8:].reshape(-1), d_modulation])
    small = jnp.concatenate(
        [d_modulation.reshape(wide, -1, share), d_vector.reshape(wide, -1, share)], axis=1
    ).astype(BF)
    small = jnp.pad(small, ((0, 0), (0, padded - rows - 16 - small_rows), (0, 0)))
    d_start_rows = jnp.concatenate([d_start_rows, small], axis=1)
    d_start_recv = swap_wide(d_start_rows)
    a_from = xor_narrow(a_far, 2)
    b_half = scatter_pair((b_near + b_from.astype(F32)).reshape(wide, share, width))
    c_half = c_pair[0] + c_from.astype(F32)
    a_from, d_start_recv, b_half, c_half, *d_table = together(
        a_from, d_start_recv, b_half, c_half, *d_table
    )
    d_table = [swap_wide(piece) for piece in d_table]
    d_start_recv = d_start_recv.reshape(wide * padded, share)
    d_start_across = xor_narrow(d_start_recv, 2)
    d_near = (d_start_recv, xor_narrow(d_start_recv, 1))
    d_embed = collect(sort_keys[:2], hits[:2], d_near, shift, None, entries)
    d_start_across, d_embed = together(d_start_across, d_embed)
    d_start_corner = xor_narrow(d_start_across, 1)
    a_from, b_half, c_half, d_start_corner = together(a_from, b_half, c_half, d_start_corner)
    a_half = scatter_pair((a_near + a_from.astype(F32)).reshape(wide, share, width))
    d_b, d_c = scatter_line(b_half), scatter_line(c_half)
    a_pieces = line_pieces(a_half)
    d_far = (d_start_across, d_start_corner)
    d_embed = collect(sort_keys[2:], hits[2:], d_far, shift, d_embed, entries)
    d_embed, *d_table = together(d_embed, *d_table)
    d_table = jnp.concatenate(d_table, axis=2).astype(F32).transpose(1, 0, 2)
    d_table = d_table.reshape(share, chunk * wide)[:, :entries]
    square = jnp.sum(d_embed * d_embed) + jnp.sum(d_table * d_table)
    square, *a_pieces = together(square, *a_pieces)
    d_a = total_of(a_pieces)

    small, small_far = [
        sum(
            part.reshape(wide, padded, share)[:, rows + 16 : rows + 16 + small_rows].astype(F32)
            for part in parts
        ).reshape(wide, -1)
        for parts in (d_near, d_far)
    ]
    d_vectors = jnp.sum(small[:, mod_share:] + small_far[:, mod_share:], axis=0)
    condition_far = lax.dynamic_index_in_dim(condition, 1 - micro, 1, keepdims=False)
    d_mod_weight = lax.dot_general(
        condition_mine, small[:, :mod_share], TN, precision=HIGHEST
    ) + lax.dot_general(condition_far, small_far[:, :mod_share], TN, precision=HIGHEST)

    shards = (
        d_embed,
        d_table,
        jnp.stack([d_a[:, k * heads_width : (k + 1) * heads_width] for k in range(3)]),
        flip(d_a[:, 3 * heads_width :]),
        d_b,
        d_c,
        d_mod_weight,
        d_vectors,
    )

    for grad in shards[2:6]:
        square = square + jnp.sum(grad * grad)
    shared_square = jnp.sum(shards[6] * shards[6]) + jnp.sum(shards[7] * shards[7])
    square = square + shared_square / narrow
    sums = lax.all_to_all(
        jnp.broadcast_to(jnp.stack([loss_part / wide, square])[None, None], (wide * narrow, 1, 2)),
        ("wide",) + NARROW,
        0,
        0,
        tiled=True,
    )
    sums = jnp.sum(sums, axis=(0, 1))
    loss_sum = sums[0]
    grad_norm = jnp.sqrt(sums[1])
    factor = CLIP_NORM / jnp.maximum(grad_norm, CLIP_NORM)
    results = []
    for member in range(8):
        turn = (lambda value: value.T) if member in (0, 5) else (lambda value: value)
        master = turn(masters[member])
        grad = shards[member] * factor
        first = BETA_ONE * turn(firsts[member]) + (1.0 - BETA_ONE) * grad
        second = BETA_TWO * turn(seconds[member]) + (1.0 - BETA_TWO) * grad * grad
        stepped = (
            first / (1.0 - BETA_ONE**STEP) / (jnp.sqrt(second / (1.0 - BETA_TWO**STEP)) + ADAM_EPS)
        )
        decay = WEIGHT_DECAY if member < 7 else 0.0
        fresh = master - LEARN_RATES[member] * (stepped + decay * master)
        results.extend([turn(fresh), turn(first), turn(second)])
    return (loss_sum, grad_norm, *results)


def solution(mesh):
    shape = (mesh.shape["wide"], mesh.shape["narrow"] // 2, 2)
    mesh = jax.sharding.Mesh(mesh.devices.reshape(shape), ("wide",) + NARROW)
    weights = (
        P(NARROW, "wide"),
        P("wide", NARROW),
        P(None, "wide", NARROW),
        P(NARROW, "wide"),
        P("wide", NARROW),
        P(NARROW, "wide"),
        P(None, "wide"),
        P("wide"),
    )
    data = (P("wide", None, None), P("wide", None, None), P("wide", None))
    outs = [P(), P()]
    for spec in weights:
        outs.extend([spec] * 3)
    return jax.shard_map(
        local,
        mesh=mesh,
        in_specs=data + weights * 3,
        out_specs=tuple(outs),
        check_vma=False,
    )
```
